32 devices in a mesh: group: 8 (over z, y), psg: 4 (over x, core).
Axes of the slice: x: 2, y: 2, z: 4, core: 2. Of those that a mesh axis runs over, the one named last changes fastest.
Arguments:
- hidden_in: bfloat16 [40960, 768], P(('group', 'psg')), may hold values from -6 to 6
- passage_lengths: int32 [32, 4], P(('group', 'psg')), may hold values from 20 to 300, as said below
- positive: int32 [512], P(('group', 'psg')), may hold values from 0 to 15
- inward_weight: float32 [768, 2304], P(('group', 'psg')), may hold values from -0.21875 to 0.21875
- outward_weight: float32 [768, 768], P(('group', 'psg')), may hold values from -0.625 to 0.625
- upward_weight: float32 [768, 3072], P(('group', 'psg')), may hold values from -0.21875 to 0.21875
- downward_weight: float32 [3072, 768], P(('group', 'psg')), may hold values from -0.109375 to 0.109375
- embed_weight: float32 [768, 128], P(('group', 'psg')), may hold values from -0.21875 to 0.21875
- layer_vectors: float32 [768, 12], P(('group', 'psg')), may hold values from -0.3 to 2.5, as said below
- first_inward: float32 [768, 2304], P(('group', 'psg')), may hold values from -1.1444092e-05 to 1.1444092e-05
- first_outward: float32 [768, 768], P(('group', 'psg')), may hold values from -1.1444092e-05 to 1.1444092e-05
- first_upward: float32 [768, 3072], P(('group', 'psg')), may hold values from -1.1444092e-05 to 1.1444092e-05
- first_downward: float32 [3072, 768], P(('group', 'psg')), may hold values from -1.1444092e-05 to 1.1444092e-05
- first_embed: float32 [768, 128], P(('group', 'psg')), may hold values from -1.1444092e-05 to 1.1444092e-05
- first_vectors: float32 [768, 12], P(('group', 'psg')), may hold values from -4.5776367e-05 to 4.5776367e-05
- second_inward: float32 [768, 2304], P(('group', 'psg')), may hold values from 5.5668377e-14 to 2.2267351e-13
- second_outward: float32 [768, 768], P(('group', 'psg')), may hold values from 5.5668377e-14 to 2.2267351e-13
- second_upward: float32 [768, 3072], P(('group', 'psg')), may hold values from 5.5668377e-14 to 2.2267351e-13
- second_downward: float32 [3072, 768], P(('group', 'psg')), may hold values from 5.5668377e-14 to 2.2267351e-13
- second_embed: float32 [768, 128], P(('group', 'psg')), may hold values from 5.5668377e-14 to 2.2267351e-13
- second_vectors: float32 [768, 12], P(('group', 'psg')), may hold values from 8.9069404e-13 to 3.5627762e-12
Outputs:
- loss: float32 [], replicated
- input_grad: float32 [40960, 768], P(('group', 'psg'))
- grad_norm: float32 [], replicated
- mean_inward: float32 [768, 2304], P(('group', 'psg'))
- mean_outward: float32 [768, 768], P(('group', 'psg'))
- mean_upward: float32 [768, 3072], P(('group', 'psg'))
- mean_downward: float32 [3072, 768], P(('group', 'psg'))
- mean_embed: float32 [768, 128], P(('group', 'psg'))
- mean_vectors: float32 [768, 12], P(('group', 'psg'))
- square_inward: float32 [768, 2304], P(('group', 'psg'))
- square_outward: float32 [768, 768], P(('group', 'psg'))
- square_upward: float32 [768, 3072], P(('group', 'psg'))
- square_downward: float32 [3072, 768], P(('group', 'psg'))
- square_embed: float32 [768, 128], P(('group', 'psg'))
- square_vectors: float32 [768, 12], P(('group', 'psg'))
- fresh_inward: float32 [768, 2304], P(('group', 'psg'))
- fresh_outward: float32 [768, 768], P(('group', 'psg'))
- fresh_upward: float32 [768, 3072], P(('group', 'psg'))
- fresh_downward: float32 [3072, 768], P(('group', 'psg'))
- fresh_embed: float32 [768, 128], P(('group', 'psg'))
- fresh_vectors: float32 [768, 12], P(('group', 'psg'))
The draws below stay inside these ranges and needn't reach their ends.
Inputs may be any that keep to these rules, and one draw needn't show every extreme that they name: `passage_lengths`: each device's 4 lengths add up to 768; in every draw some device holds a passage of 300 tokens. `layer_vectors`: columns 0 and 2 are positive gains, the others biases.
All inputs are finite; a program needn't handle non-finite values.
Results may differ from the reference program's by a relative error of at most 0.012.
The reference program's roundings to bfloat16 on the way count: a program that leaves them out, or rounds other values in their place, can miss the bound.
Values may be sent and summed in bfloat16 or wider, within the bound.
No kernel may reach another device: no remote copies, remote signals or barrier semaphores. Data moves between devices by JAX's collectives and lax.ppermute only.
A program may use at most 256 MiB of HBM per device.

```python
import math
import jax
import jax.numpy as jnp
from jax import lax

D = 768
HEADS = 12
HEAD = 64
FF = 3072
EMB = 128
QLEN = 32
Q_DEV = 16
P_DEV = 4
PACK = 768
MAXLEN = 300
MINLEN = 20
STEP = 10
ROWS = 1280
TOTAL = 40960
P_GROUP = 16
NQ = 512
VROWS = 12
PARAMS = 7185408
N_GROUP = 8
N_PSG = 4


def draw_layer_vectors(key, part):
    key = jax.random.fold_in(key, 11)
    keys = jax.random.split(key, 2)
    places = jnp.arange(D, dtype=jnp.float32) / D
    spread = jax.random.uniform(keys[0], (D, 2), jnp.float32, 0.75, 1.25)
    ramp = 0.5 + places
    biases = 0.1 * jax.random.truncated_normal(keys[1], -3.0, 3.0, (D, VROWS - 2), jnp.float32)
    gains = ramp[:, None] * spread
    return jnp.concatenate([gains[:, :1], biases[:, :1], gains[:, 1:], biases[:, 1:]], 1)


def draw_passage_lengths(key, part):
    key = jax.random.fold_in(key, 23)
    keys = jax.random.split(key, P_DEV + 1)
    devices_all = N_GROUP * N_PSG
    ceiling = MAXLEN - MINLEN
    forced = jax.random.randint(keys[P_DEV], (), 0, devices_all, dtype=jnp.int32)
    marked = jnp.arange(devices_all, dtype=jnp.int32) == forced
    remain = jnp.full((devices_all,), PACK - P_DEV * MINLEN, jnp.int32)
    columns = []
    for slot in range(P_DEV - 1):
        slots_left = P_DEV - 1 - slot
        floor_now = jnp.maximum(0, remain - slots_left * ceiling).astype(jnp.int32)
        top_now = jnp.minimum(ceiling, remain).astype(jnp.int32)
        if slot == 0:
            floor_now = jnp.where(marked, ceiling, floor_now).astype(jnp.int32)
            top_now = jnp.where(marked, ceiling, top_now).astype(jnp.int32)
        chosen = jax.random.randint(keys[slot], (devices_all,), floor_now, top_now + 1, dtype=jnp.int32)
        columns.append(chosen)
        remain = remain - chosen
    columns.append(remain)
    return (MINLEN + jnp.stack(columns, 1)).astype(jnp.int32)


def touch_ends(drawn, own_key, smallest, largest):
    spot = [jax.random.randint(jax.random.fold_in(own_key, axis), (), 0, length) for axis, length in enumerate(drawn.shape)]
    longest = drawn.shape.index(max(drawn.shape))
    next_to = spot[:longest] + [(spot[longest] + 1) % drawn.shape[longest]] + spot[longest + 1:]
    return drawn.at[tuple(spot)].set(smallest).at[tuple(next_to)].set(largest)


def block_levels(key, shape, cuts, smallest, top_value):
    gain = 1.0
    for dim, shards_of in cuts:
        steps = jax.random.uniform(jax.random.fold_in(jax.random.fold_in(key, 6), dim), (shards_of,), jnp.float32, smallest / len(cuts), top_value / len(cuts))
        gain = gain * jnp.repeat(jnp.exp(steps), shape[dim] // shards_of).reshape((-1,) + (1,) * (len(shape) - 1 - dim))
    return gain


def bell_draw(key, extent, width, reach, shards=(), held_as=jnp.bfloat16):
    array = jax.random.normal(key, extent, jnp.float32) * width
    if len(shards) > 0:
        array = block_levels(key, extent, shards, -0.22, 0.18) * array
    return jnp.clip(array, min=-reach, max=reach).astype(held_as)


def setup_inputs(seed: int = 0) -> dict:
    seeds = jax.random.split(jax.random.key(seed), 22)
    hidden_in = bell_draw(seeds[0], (TOTAL, D), 1.0, 6.0, ((0, 32),))
    passage_lengths = draw_passage_lengths(jax.random.fold_in(seeds[21], 71), 0)
    positive = touch_ends(jax.random.randint(seeds[2], (NQ,), 0, P_GROUP), jax.random.fold_in(seeds[2], 1), 0, P_GROUP - 1).astype(jnp.int32)
    inward_weight = bell_draw(seeds[3], (D, 3 * D), D ** -0.5, 0.21875, ((0, 32),), jnp.float32)
    outward_weight = bell_draw(seeds[4], (D, D), (D // 8) ** -0.5, 0.625, ((0, 32),), jnp.float32)
    upward_weight = bell_draw(seeds[5], (D, FF), D ** -0.5, 0.21875, ((0, 32),), jnp.float32)
    downward_weight = bell_draw(seeds[6], (FF, D), FF ** -0.5, 0.109375, ((0, 32),), jnp.float32)
    embed_weight = bell_draw(seeds[7], (D, EMB), D ** -0.5, 0.21875, ((0, 32),), jnp.float32)
    layer_vectors = draw_layer_vectors(jax.random.fold_in(seeds[21], 71), 0)
    first_inward = bell_draw(seeds[9], (D, 3 * D), (0.0022 * PARAMS ** -0.5), 1.1444091796875e-05, ((0, 32),), jnp.float32)
    first_outward = bell_draw(seeds[10], (D, D), (0.0022 * PARAMS ** -0.5), 1.1444091796875e-05, ((0, 32),), jnp.float32)
    first_upward = bell_draw(seeds[11], (D, FF), (0.0022 * PARAMS ** -0.5), 1.1444091796875e-05, ((0, 32),), jnp.float32)
    first_downward = bell_draw(seeds[12], (FF, D), (0.0022 * PARAMS ** -0.5), 1.1444091796875e-05, ((0, 32),), jnp.float32)
    first_embed = bell_draw(seeds[13], (D, EMB), (0.0022 * PARAMS ** -0.5), 1.1444091796875e-05, ((0, 32),), jnp.float32)
    first_vectors = bell_draw(seeds[14], (D, VROWS), (0.0088 * PARAMS ** -0.5), 4.57763671875e-05, ((0, 32),), jnp.float32)
    second_inward = jnp.clip(jnp.exp(math.log(2.2267350994770868e-13) - 1.3862944 * jax.random.uniform(seeds[15], (D, 3 * D), jnp.float32) ** block_levels(seeds[15], (D, 3 * D), ((0, 32),), -0.2, 0.2)), 5.566837748692717e-14, 2.2267350994770868e-13)
    second_outward = jnp.clip(jnp.exp(math.log(2.2267350994770868e-13) - 1.3862944 * jax.random.uniform(seeds[16], (D, D), jnp.float32) ** block_levels(seeds[16], (D, D), ((0, 32),), -0.2, 0.2)), 5.566837748692717e-14, 2.2267350994770868e-13)
    second_upward = jnp.clip(jnp.exp(math.log(2.2267350994770868e-13) - 1.3862944 * jax.random.uniform(seeds[17], (D, FF), jnp.float32) ** block_levels(seeds[17], (D, FF), ((0, 32),), -0.2, 0.2)), 5.566837748692717e-14, 2.2267350994770868e-13)
    second_downward = jnp.clip(jnp.exp(math.log(2.2267350994770868e-13) - 1.3862944 * jax.random.uniform(seeds[18], (FF, D), jnp.float32) ** block_levels(seeds[18], (FF, D), ((0, 32),), -0.2, 0.2)), 5.566837748692717e-14, 2.2267350994770868e-13)
    second_embed = jnp.clip(jnp.exp(math.log(2.2267350994770868e-13) - 1.3862944 * jax.random.uniform(seeds[19], (D, EMB), jnp.float32) ** block_levels(seeds[19], (D, EMB), ((0, 32),), -0.2, 0.2)), 5.566837748692717e-14, 2.2267350994770868e-13)
    second_vectors = jnp.clip(jnp.exp(math.log(3.562776159163339e-12) - 1.3862944 * jax.random.uniform(seeds[20], (D, VROWS), jnp.float32) ** block_levels(seeds[20], (D, VROWS), ((0, 32),), -0.2, 0.2)), 8.906940397908347e-13, 3.562776159163339e-12)
    return {"hidden_in": hidden_in, "passage_lengths": passage_lengths, "positive": positive, "inward_weight": inward_weight, "outward_weight": outward_weight, "upward_weight": upward_weight, "downward_weight": downward_weight, "embed_weight": embed_weight, "layer_vectors": layer_vectors, "first_inward": first_inward, "first_outward": first_outward, "first_upward": first_upward, "first_downward": first_downward, "first_embed": first_embed, "first_vectors": first_vectors, "second_inward": second_inward, "second_outward": second_outward, "second_upward": second_upward, "second_downward": second_downward, "second_embed": second_embed, "second_vectors": second_vectors}


HIGH = lax.Precision.HIGHEST
TAU_INV = 10.0
SCORE_SCALE = 10.0
CLIP_NORM = 0.02
BETA_ONE = 0.9
BETA_TWO = 0.999
ADAM_EPS = 1e-08
RATE_MATRIX = 0.05
RATE_VECTOR = 0.5
DECAY = 0.01
NORM_EPS = 1e-12
UNIT_EPS = 1e-06

@jax.custom_vjp
def low(v):
    return lax.optimization_barrier(v.astype(jnp.bfloat16)).astype(jnp.float32)

@jax.custom_vjp
def low_back(v):
    return v

def low_keep(v):
    return (low(v), None)

def low_pass(kept, grad):
    return (grad,)

def back_keep(v):
    return (v, None)

def back_low(kept, grad):
    return (low(grad),)
low.defvjp(low_keep, low_pass)
low_back.defvjp(back_keep, back_low)

def layer_norm(residual, gain_vec, offset):
    center = lax.optimization_barrier(jnp.mean(residual, -1, keepdims=True))
    shifted = residual - center
    spread = lax.optimization_barrier(jnp.mean(shifted * shifted, -1, keepdims=True))
    return shifted * lax.rsqrt(spread + NORM_EPS) * gain_vec + offset

def unit_rows(projected):
    return projected * lax.rsqrt(lax.optimization_barrier(jnp.sum(projected * projected, -1, keepdims=True)) + UNIT_EPS)

def segment_ids(lengths, length):
    ends = jnp.cumsum(lengths)
    places = jnp.arange(length, dtype=jnp.int32)
    return lax.optimization_barrier(jnp.sum((places[:, None] >= ends[None, :]).astype(jnp.int32), -1))

def attend(query_heads, key_heads, value_heads, allowed):
    raw_scores = jnp.einsum('blhe,bmhe->bhlm', query_heads, key_heads, precision=HIGH)
    scores = low_back(raw_scores * HEAD ** (-0.5))
    scores = jnp.where(allowed[:, None], scores, -1000000000.0)
    weights = low(jax.nn.softmax(scores, -1))
    return low(low_back(jnp.einsum('bhlm,bmhe->blhe', weights, value_heads, precision=HIGH)))

def encode(token_rows, lengths, weights):
    inward, outward, upward, downward, embed_proj, vectors = weights
    query_rows = Q_DEV * QLEN
    merged_proj = jnp.dot(token_rows, inward, precision=HIGH)
    query_heads = low(low_back(merged_proj[:, :D] + vectors[:, 4]))
    key_heads = low(low_back(merged_proj[:, D:2 * D]))
    value_heads = low(low_back(merged_proj[:, 2 * D:] + vectors[:, 5]))
    segment = segment_ids(lengths, PACK)
    same_passage = (segment[:, None] == segment[None, :])[None]
    query_mask = jnp.ones((Q_DEV, QLEN, QLEN), bool)

    def short_part(block):
        return block[:query_rows].reshape(Q_DEV, QLEN, HEADS, HEAD)

    def long_part(block):
        return block[query_rows:].reshape(1, PACK, HEADS, HEAD)
    context_short = attend(short_part(query_heads), short_part(key_heads), short_part(value_heads), query_mask)
    context_long = attend(long_part(query_heads), long_part(key_heads), long_part(value_heads), same_passage)
    context = jnp.concatenate([context_short.reshape(query_rows, D), context_long.reshape(PACK, D)], 0)
    branch = low_back(jnp.dot(context, outward, precision=HIGH) + vectors[:, 6])
    norm_one = layer_norm(token_rows + branch, vectors[:, 0], vectors[:, 1])
    up_bias = vectors[:, 8:].T.reshape(FF)
    up_input = low_back(jnp.dot(low(norm_one), upward, precision=HIGH) + up_bias)
    active = low(jax.nn.gelu(up_input, approximate=False))
    down_out = low_back(jnp.dot(active, downward, precision=HIGH) + vectors[:, 7])
    norm_two = layer_norm(norm_one + down_out, vectors[:, 2], vectors[:, 3])
    projected = low_back(jnp.dot(low(norm_two), embed_proj, precision=HIGH))
    return (low(unit_rows(projected)), segment)

def group_loss(token_rows, lengths, chosen, weights):
    embedded, segment = jax.vmap(lambda block, sizes: encode(block, sizes, weights))(token_rows, lengths)
    query_rows = Q_DEV * QLEN
    queries = embedded[:, :query_rows].reshape(N_PSG * query_rows, EMB)
    passages = embedded[:, query_rows:]
    similar = low_back(jnp.einsum('ie,pte->pit', queries, passages, precision=HIGH))
    row_peak = lax.optimization_barrier(jnp.max(similar, -1, keepdims=True))
    member = (segment[:, :, None] == jnp.arange(P_DEV, dtype=jnp.int32)[None, None, :]).astype(jnp.float32)
    totals = jnp.einsum('pit,ptj->pij', jnp.exp((similar - row_peak) * TAU_INV), member, precision=HIGH)
    log_length = jnp.log(lengths.astype(jnp.float32))
    smooth = jnp.log(totals) / TAU_INV + row_peak - log_length[:, None, :] / TAU_INV
    per_query = lax.optimization_barrier(jnp.sum(smooth.reshape(N_PSG, N_PSG * Q_DEV, QLEN, P_DEV), 2))
    logits = SCORE_SCALE * jnp.transpose(per_query, (1, 0, 2)).reshape(N_PSG * Q_DEV, N_PSG * P_DEV)
    picked = (chosen[:, None] == jnp.arange(N_PSG * P_DEV, dtype=jnp.int32)[None, :]).astype(jnp.float32)
    return jnp.sum(jax.nn.logsumexp(logits, -1) - lax.optimization_barrier(jnp.sum(picked * logits, -1)))

def adam_step(weight, grad, first, second, rate, decay):
    first_new = BETA_ONE * first + (1.0 - BETA_ONE) * grad
    second_new = BETA_TWO * second + (1.0 - BETA_TWO) * grad * grad
    fix_one = 1.0 - BETA_ONE ** STEP
    fix_two = 1.0 - BETA_TWO ** STEP
    update = first_new / fix_one / (jnp.sqrt(second_new / fix_two) + ADAM_EPS)
    return (first_new, second_new, weight - rate * (update + decay * weight))

def reference(hidden_in, passage_lengths, positive, inward_weight, outward_weight, upward_weight, downward_weight, embed_weight, layer_vectors, first_inward, first_outward, first_upward, first_downward, first_embed, first_vectors, second_inward, second_outward, second_upward, second_downward, second_embed, second_vectors):
    token_rows = hidden_in.astype(jnp.float32)
    masters = (inward_weight, outward_weight, upward_weight, downward_weight, embed_weight, layer_vectors)
    grouped = (passage_lengths.reshape(N_GROUP, N_PSG, P_DEV), positive.reshape(N_GROUP, N_PSG * Q_DEV))

    def total_loss(all_rows, inward, outward, upward, downward, embed_proj, vectors):
        weights = (low(inward), low(outward), low(upward), low(downward), low(embed_proj), low(vectors))

        def one_group(group_item):
            block, sizes, chosen = group_item
            return group_loss(block, sizes, chosen, weights)
        losses = lax.map(jax.checkpoint(one_group), (all_rows.reshape(N_GROUP, N_PSG, ROWS, D), grouped[0], grouped[1]))
        return jnp.sum(losses) / NQ
    loss, backward = jax.vjp(total_loss, token_rows, *masters)
    grads = backward(jnp.ones_like(loss))
    input_grad = grads[0]
    weight_grads = grads[1:]
    squares = jnp.zeros((), jnp.float32)
    for grad in weight_grads:
        squares = squares + jnp.sum(grad * grad)
    grad_norm = jnp.sqrt(squares)
    factor = CLIP_NORM / jnp.maximum(grad_norm, CLIP_NORM)
    firsts = (first_inward, first_outward, first_upward, first_downward, first_embed, first_vectors)
    seconds = (second_inward, second_outward, second_upward, second_downward, second_embed, second_vectors)
    means = []
    squared = []
    freshes = []
    for index in range(6):
        rate = RATE_VECTOR if index == 5 else RATE_MATRIX
        decay = 0.0 if index == 5 else DECAY
        first_new, second_new, weight_new = adam_step(masters[index], weight_grads[index] * factor, firsts[index], seconds[index], rate, decay)
        means.append(first_new)
        squared.append(second_new)
        freshes.append(weight_new)
    return (loss, input_grad, grad_norm, means[0], means[1], means[2], means[3], means[4], means[5], squared[0], squared[1], squared[2], squared[3], squared[4], squared[5], freshes[0], freshes[1], freshes[2], freshes[3], freshes[4], freshes[5])
```

```python
import functools

import jax
import jax.numpy as jnp
from jax import lax
from jax.experimental import pallas as pl
from jax.experimental.pallas import tpu as pltpu
from jax.sharding import PartitionSpec as P

HEADS = 12
HEAD = 64
QLEN = 32
STEP = 10

TAU_INV = 10.0
SCORE_SCALE = 10.0
CLIP_NORM = 0.02
BETA_ONE = 0.9
BETA_TWO = 0.999
ADAM_EPS = 1e-08
RATE_MATRIX = 0.05
RATE_VECTOR = 0.5
DECAY = 0.01
NORM_EPS = 1e-12
UNIT_EPS = 1e-06

AXES = ("group", "psg")
LANES = 128
PIECES = 16
TILE = 256
MIB = 2**20
BF = jnp.bfloat16
F32 = jnp.float32


def mm(left, right):
    return lax.dot_general(left, right, (((1,), (0,)), ((), ())), preferred_element_type=F32)


def mm_nt(left, right):
    return lax.dot_general(left, right, (((1,), (1,)), ((), ())), preferred_element_type=F32)


def mm_tn(left, right):
    return lax.dot_general(left, right, (((0,), (0,)), ((), ())), preferred_element_type=F32)


def full(shape):
    return pl.BlockSpec(shape, lambda *_: (0,) * len(shape))


def params(mib=56):
    return pltpu.CompilerParams(
        vmem_limit_bytes=mib * MIB, dimension_semantics=("arbitrary",)
    )


def cost(flops, moved, special=0):
    return pl.CostEstimate(flops=int(flops), bytes_accessed=int(moved), transcendentals=int(special))


def shape_of(shape, dtype):
    return jax.ShapeDtypeStruct(shape, dtype)


def any_space():
    return pl.BlockSpec(memory_space=pl.ANY)


def fetch_pieces(where_ref, own_ref, other_ref, moves, sems):
    chip, core = where_ref[0], where_ref[1]
    rows = own_ref.shape[1]

    def start(halves):
        for piece in range(own_ref.shape[0]):
            source = lax.bitwise_xor(chip, piece)
            for number, (half, first, width, target, column) in enumerate(moves):
                pltpu.make_async_copy(
                    halves[half].at[source, :, pl.ds(first, width)],
                    target.at[pl.ds(rows * piece, rows), pl.ds(column, width)],
                    sems.at[number],
                ).start()

    pl.when(core == 0)(lambda: start((own_ref, other_ref)))
    pl.when(core == 1)(lambda: start((other_ref, own_ref)))
    for number, (_, _, width, target, column) in enumerate(moves):
        landed = target.at[:, pl.ds(column, width)]
        pltpu.make_async_copy(landed, landed, sems.at[number]).wait()


def project_kernel(
    where_ref, rows_ref, own_ref, other_ref, merged_ref, in_ref, out_ref, embed_ref, vec_ref, raw, sems
):
    width = rows_ref.shape[1]
    half_in, half_out = 3 * width // 2, width // 2

    @pl.when(pl.program_id(0) == 0)
    def _():
        moves = []
        for half in (0, 1):
            moves.append((half, 0, half_in, in_ref, half * half_in))
            moves.append((half, half_in, half_out, out_ref, half * half_out))
        moves.append((0, half_in + half_out, LANES, embed_ref, 0))
        moves.append((1, half_in + half_out, LANES, raw, 0))
        fetch_pieces(where_ref, own_ref, other_ref, moves, sems)
        vec_ref[...] = raw[...].astype(F32).T[: vec_ref.shape[0]]

    rows = rows_ref[...]
    for part, bias in ((0, 4), (1, None), (2, 5)):
        block = mm(rows, in_ref[:, part * width : (part + 1) * width])
        if bias is not None:
            block = block + vec_ref[bias : bias + 1, :]
        merged_ref[:, part * width : (part + 1) * width] = block.astype(BF)


def project(where, hidden, own, other):
    rows, width = hidden.shape
    return pl.pallas_call(
        project_kernel,
        grid_spec=pltpu.PrefetchScalarGridSpec(
            num_scalar_prefetch=1,
            grid=(rows // TILE,),
            in_specs=[pl.BlockSpec((TILE, width), lambda i, w: (i, 0)), any_space(), any_space()],
            out_specs=[
                pl.BlockSpec((TILE, 3 * width), lambda i, w: (i, 0)),
                full((width, 3 * width)),
                full((width, width)),
                full((width, LANES)),
                full((16, width)),
            ],
            scratch_shapes=[pltpu.VMEM((width, LANES), BF), pltpu.SemaphoreType.DMA((6,))],
        ),
        out_shape=[
            shape_of((rows, 3 * width), BF),
            shape_of((width, 3 * width), BF),
            shape_of((width, width), BF),
            shape_of((width, LANES), BF),
            shape_of((16, width), F32),
        ],
        compiler_params=params(),
        cost_estimate=cost(6 * rows * width * width, 8 * rows * width + 16 * width * width),
        name="project",
    )(where, hidden, own, other)


def head_masks():
    lane = lax.broadcasted_iota(jnp.int32, (1, LANES), 1)
    return [(lane < HEAD).astype(BF), (lane >= HEAD).astype(BF)]


def softmax_rows(scores):
    peak = jnp.max(scores, -1, keepdims=True)
    expo = jnp.exp(scores - peak)
    return expo * (1.0 / jnp.sum(expo, -1, keepdims=True))


def blocks_of(rows, query_rows):
    listed = [(first, LANES, first, LANES, True) for first in range(0, query_rows, LANES)]
    for first in range(query_rows, rows, TILE):
        listed.append((first, TILE, query_rows, rows - query_rows, False))
    return listed


def allowed_pairs(block, seg_col, seg_row, query_rows):
    first, count, _, keys, is_query = block
    if is_query:
        mine = lax.broadcasted_iota(jnp.int32, (count, keys), 0) // QLEN
        theirs = lax.broadcasted_iota(jnp.int32, (count, keys), 1) // QLEN
        return mine == theirs
    begin = first - query_rows
    return seg_col[begin : begin + count, :] == seg_row[0:1, :]


def attend_kernel(query_rows, seg_col, seg_row, q_ref, k_ref, v_ref, out_ref):
    masks = head_masks()
    for block in blocks_of(q_ref.shape[0], query_rows):
        first, count, begin, keys, _ = block
        allowed = allowed_pairs(block, seg_col, seg_row, query_rows)
        query = q_ref[first : first + count, :]
        key = k_ref[begin : begin + keys, :]
        value = v_ref[begin : begin + keys, :]
        total = None
        for mask in masks:
            scores = jnp.where(allowed, mm_nt(query * (mask * HEAD**-0.5), key), -1e9)
            part = mm(softmax_rows(scores).astype(BF), value * mask)
            total = part if total is None else total + part
        out_ref[first : first + count, :] = total.astype(BF)


def attend(merged, seg_col, seg_row, query_rows):
    rows, wide = merged.shape
    pairs = wide // 3 // LANES
    pack = rows - query_rows

    def column(part):
        return pl.BlockSpec((rows, LANES), lambda h: (0, part * pairs + h))

    return pl.pallas_call(
        functools.partial(attend_kernel, query_rows),
        grid=(pairs,),
        in_specs=[full((pack, 1)), full((1, pack)), column(0), column(1), column(2)],
        out_specs=pl.BlockSpec((rows, LANES), lambda h: (0, h)),
        out_shape=shape_of((rows, wide // 3), BF),
        compiler_params=params(),
        cost_estimate=cost(
            8 * HEADS * pack * pack * LANES, 8 * rows * wide, HEADS * pack * pack
        ),
        name="attend",
    )(seg_col, seg_row, merged, merged, merged)


def put_rows(where_ref, target, values):
    pieces, rows = target.shape[1], target.shape[2]
    chip = lax.bitwise_and(where_ref[0], pieces - 1)
    for piece in range(pieces):
        for half in (0, 1):
            begin = (2 * piece + half) * rows
            target[
                lax.bitwise_xor(where_ref[1], half), lax.bitwise_xor(chip, piece)
            ] = values[begin : begin + rows, :].astype(BF)


def attend_back_kernel(
    query_rows,
    where_ref,
    seg_col,
    seg_row,
    q_ref,
    k_ref,
    v_ref,
    d_ref,
    turned_ref,
    dq_ref,
    dk_ref,
    dv_ref,
    grad_ref,
    sum_ref,
    acc_k,
    acc_v,
):
    masks = head_masks()
    rows = q_ref.shape[0]
    acc_k[...] = jnp.zeros_like(acc_k)
    acc_v[...] = jnp.zeros_like(acc_v)
    for block in blocks_of(rows, query_rows):
        first, count, begin, keys, is_query = block
        allowed = allowed_pairs(block, seg_col, seg_row, query_rows)
        query = q_ref[first : first + count, :]
        given = d_ref[first : first + count, :]
        key = k_ref[begin : begin + keys, :]
        value = v_ref[begin : begin + keys, :]
        dq = dk = dv = 0.0
        for mask in masks:
            scaled = query * (mask * HEAD**-0.5)
            own = given * mask
            weights = softmax_rows(jnp.where(allowed, mm_nt(scaled, key), -1e9))
            d_weights = mm_nt(own, value)
            inner = jnp.sum(d_weights * weights, -1, keepdims=True)
            d_scores = (weights * (d_weights - inner)).astype(BF)
            dq = dq + mm(d_scores, key * (mask * HEAD**-0.5))
            dk = dk + mm_tn(d_scores, scaled)
            dv = dv + mm_tn(weights.astype(BF), own)
        dq_ref[first : first + count, :] = dq.astype(BF)
        if is_query:
            dk_ref[begin : begin + keys, :] = dk.astype(BF)
            dv_ref[begin : begin + keys, :] = dv.astype(BF)
        else:
            acc_k[...] += dk
            acc_v[...] += dv
    dk_ref[query_rows:, :] = acc_k[...].astype(BF)
    dv_ref[query_rows:, :] = acc_v[...].astype(BF)
    turned = turned_ref[...]
    grad = jnp.concatenate(
        [mm(turned, dq_ref[...]), mm(turned, dk_ref[...]), mm(turned, dv_ref[...])], 1
    )
    put_rows(where_ref, grad_ref, grad)
    sum_ref[...] = jnp.concatenate(
        [
            jnp.sum(dq_ref[...].astype(F32), 0, keepdims=True),
            jnp.sum(dv_ref[...].astype(F32), 0, keepdims=True),
            jnp.zeros((6, LANES), F32),
        ],
        0,
    )


def attend_back(where, merged, d_context, turned, seg_col, seg_row, query_rows, first_pair, count):
    rows, wide = merged.shape
    width = wide // 3
    pairs = width // LANES
    pack = rows - query_rows
    owned = width // PIECES // 2

    def column(part):
        return pl.BlockSpec((rows, LANES), lambda h, w: (0, part * pairs + first_pair + h))

    own_column = pl.BlockSpec((rows, LANES), lambda h, w: (0, h))
    return pl.pallas_call(
        functools.partial(attend_back_kernel, query_rows),
        grid_spec=pltpu.PrefetchScalarGridSpec(
            num_scalar_prefetch=1,
            grid=(count,),
            in_specs=[
                full((pack, 1)),
                full((1, pack)),
                column(0),
                column(1),
                column(2),
                pl.BlockSpec((rows, LANES), lambda h, w: (0, first_pair + h)),
                full((width, rows)),
            ],
            out_specs=[
                own_column,
                own_column,
                own_column,
                pl.BlockSpec((2, PIECES, owned, 3 * LANES), lambda h, w: (0, 0, 0, h)),
                pl.BlockSpec((8, LANES), lambda h, w: (0, h)),
            ],
            scratch_shapes=[pltpu.VMEM((pack, LANES), F32), pltpu.VMEM((pack, LANES), F32)],
        ),
        out_shape=[
            shape_of((rows, count * LANES), BF),
            shape_of((rows, count * LANES), BF),
            shape_of((rows, count * LANES), BF),
            shape_of((2, PIECES, owned, 3 * count * LANES), BF),
            shape_of((8, count * LANES), F32),
        ],
        compiler_params=params(),
        cost_estimate=cost(
            count * (20 * pack * pack * LANES + 6 * rows * width * LANES),
            count * rows * LANES * 14,
            2 * count * pack * pack,
        ),
        name="attend_back",
    )(where, seg_col, seg_row, merged, merged, merged, d_context, turned)


def normalize(residual):
    center = jnp.mean(residual, -1, keepdims=True)
    shifted = residual - center
    spread = jnp.mean(shifted * shifted, -1, keepdims=True)
    scale = lax.rsqrt(spread + NORM_EPS)
    return shifted * scale, scale


def normalize_back(d_out, gain, unit, scale):
    d_unit = d_out * gain
    return scale * (
        d_unit
        - jnp.mean(d_unit, -1, keepdims=True)
        - unit * jnp.mean(d_unit * unit, -1, keepdims=True)
    )


ERFC = (0.254829592, -0.284496736, 1.421413741, -1.453152027, 1.061405429)


def gelu_parts(given):
    size = jnp.abs(given)
    near = 1.0 / (1.0 + (0.3275911 * 0.5**0.5) * size)
    bell = jnp.exp(-0.5 * given * given)
    series = ERFC[4]
    for factor in (ERFC[3], ERFC[2], ERFC[1], ERFC[0]):
        series = series * near + factor
    tail = 0.5 * series * near * bell
    below = jnp.where(given >= 0, 1.0 - tail, tail)
    return given * below, below + given * bell * 0.3989422804014327


def widen_kernel(
    where_ref,
    context_ref,
    hidden_ref,
    out_ref,
    vec_ref,
    own_ref,
    other_ref,
    unit_ref,
    scale_ref,
    low_ref,
    active_ref,
    slope_ref,
    up_ref,
    sems,
):
    width = hidden_ref.shape[1]
    half = up_ref.shape[1] // 2

    @pl.when(pl.program_id(0) == 0)
    def _():
        moves = [(0, 0, half, up_ref, 0), (1, 0, half, up_ref, half)]
        fetch_pieces(where_ref, own_ref, other_ref, moves, sems)

    branch = mm(context_ref[...], out_ref[...]) + vec_ref[6:7, :]
    unit, scale = normalize(hidden_ref[...].astype(F32) + branch)
    unit_ref[...] = unit
    scale_ref[...] = scale
    low = (unit * vec_ref[0:1, :] + vec_ref[1:2, :]).astype(BF)
    low_ref[...] = low
    for part in range(up_ref.shape[1] // width):
        columns = slice(part * width, (part + 1) * width)
        raised = mm(low, up_ref[:, columns]) + vec_ref[8 + part : 9 + part, :]
        value, slope = gelu_parts(raised)
        active_ref[:, columns] = value.astype(BF)
        slope_ref[:, columns] = slope.astype(BF)


def widen(where, context, hidden, w_out, vectors, own, other):
    rows, width = hidden.shape
    wide = 2 * own.shape[2]

    def tile(columns):
        return pl.BlockSpec((TILE, columns), lambda i, w: (i, 0))

    return pl.pallas_call(
        widen_kernel,
        grid_spec=pltpu.PrefetchScalarGridSpec(
            num_scalar_prefetch=1,
            grid=(rows // TILE,),
            in_specs=[
                tile(width),
                tile(width),
                full((width, width)),
                full((16, width)),
                any_space(),
                any_space(),
            ],
            out_specs=[tile(width), tile(1), tile(width), tile(wide), tile(wide), full((width, wide))],
            scratch_shapes=[pltpu.SemaphoreType.DMA((2,))],
        ),
        out_shape=[
            shape_of((rows, width), F32),
            shape_of((rows, 1), F32),
            shape_of((rows, width), BF),
            shape_of((rows, wide), BF),
            shape_of((rows, wide), BF),
            shape_of((width, wide), BF),
        ],
        compiler_params=params(),
        cost_estimate=cost(
            2 * rows * width * (width + wide), rows * (10 * width + 4 * wide), rows * wide
        ),
        name="widen",
    )(where, context, hidden, w_out, vectors, own, other)


def narrow_kernel(
    active_ref, down_ref, unit_in_ref, vec_ref, embed_ref, unit_ref, scale_ref, low_ref, proj_ref, row_ref
):
    first = unit_in_ref[...] * vec_ref[0:1, :] + vec_ref[1:2, :]
    out = mm(active_ref[...], down_ref[...]) + vec_ref[7:8, :]
    unit, scale = normalize(first + out)
    unit_ref[...] = unit
    scale_ref[...] = scale
    low = (unit * vec_ref[2:3, :] + vec_ref[3:4, :]).astype(BF)
    low_ref[...] = low
    projected = mm(low, embed_ref[...])
    proj_ref[...] = projected
    size = jnp.sum(projected * projected, -1, keepdims=True)
    row_ref[...] = (projected * lax.rsqrt(size + UNIT_EPS)).astype(BF)


def narrow(active, w_down, unit_one, vectors, w_embed):
    rows, wide = active.shape
    width = w_down.shape[1]

    def tile(columns):
        return pl.BlockSpec((TILE, columns), lambda i: (i, 0))

    return pl.pallas_call(
        narrow_kernel,
        grid=(rows // TILE,),
        in_specs=[
            tile(wide),
            full((wide, width)),
            tile(width),
            full((16, width)),
            full((width, LANES)),
        ],
        out_specs=[tile(width), tile(1), tile(width), tile(LANES), tile(LANES)],
        out_shape=[
            shape_of((rows, width), F32),
            shape_of((rows, 1), F32),
            shape_of((rows, width), BF),
            shape_of((rows, LANES), F32),
            shape_of((rows, LANES), BF),
        ],
        compiler_params=params(),
        cost_estimate=cost(2 * rows * width * (wide + LANES), rows * (2 * wide + 10 * width)),
        name="narrow",
    )(active, w_down, unit_one, vectors, w_embed)


def split_two(values):
    high = values.astype(BF)
    return high, (values - high.astype(F32)).astype(BF)


def score_kernel(
    query_rows,
    query_total,
    slots,
    rows_ref,
    begin_ref,
    end_ref,
    log_ref,
    positive_ref,
    loss_ref,
    d_ref,
    expo,
    totals,
    member,
    scaled,
):
    peers, rows, _ = rows_ref.shape
    pack = rows - query_rows
    queries = query_rows // QLEN
    place = lax.broadcasted_iota(jnp.int32, (pack, LANES), 0)
    lane = lax.broadcasted_iota(jnp.int32, (1, LANES), 1)
    for peer in range(peers):
        inside = (place >= begin_ref[peer : peer + 1, :]) & (place < end_ref[peer : peer + 1, :])
        member[peer] = inside.astype(F32).astype(BF)

    def forward(asker, carry):
        query = rows_ref[asker, :query_rows, :]
        total = jnp.zeros((query_rows, LANES), F32)
        peaks = jnp.zeros((query_rows, LANES), F32)
        for peer in range(peers):
            similar = mm_nt(query, rows_ref[peer, query_rows:, :])
            peak = jnp.max(similar, -1, keepdims=True)
            value = jnp.exp((similar - peak) * TAU_INV)
            expo[asker, peer] = value
            high, low = split_two(value)
            total = total + (mm(high, member[peer]) + mm(low, member[peer]))
            peaks = jnp.where(lane // slots == peer, peak, peaks)
        used = lane < peers * slots
        total = jnp.where(used, total, 1.0)
        smooth = jnp.log(total) / TAU_INV + peaks - log_ref[...] / TAU_INV
        logits = SCORE_SCALE * jnp.sum(smooth.reshape(queries, QLEN, LANES), 1)
        logits = jnp.where(used, logits, -1e30)
        picked = (positive_ref[asker] == lane).astype(F32)
        high = jnp.max(logits, -1, keepdims=True)
        powers = jnp.where(used, jnp.exp(logits - high), 0.0)
        norm = jnp.sum(powers, -1, keepdims=True)
        each = high + jnp.log(norm) - jnp.sum(picked * logits, -1, keepdims=True)
        d_logits = (powers / norm - picked) / query_total
        spread = jnp.broadcast_to(
            (SCORE_SCALE * d_logits)[:, None, :], (queries, QLEN, LANES)
        ).reshape(query_rows, LANES)
        scaled[asker] = jnp.where(used, spread / total, 0.0)

        @pl.when(asker == 0)
        def _():
            loss_ref[...] = jnp.broadcast_to(jnp.sum(each), loss_ref.shape)

        return carry

    lax.fori_loop(0, peers, forward, 0)

    def d_similar(asker, peer):
        high, low = split_two(scaled[asker])
        factor = mm_nt(high, member[peer]) + mm_nt(low, member[peer])
        return (expo[asker, peer] * factor).astype(BF)

    shared = d_similar(0, 0)
    d_query = mm(shared, rows_ref[0, query_rows:, :])
    d_passage = mm_tn(shared, rows_ref[0, :query_rows, :])
    for peer in range(1, peers):
        d_query = d_query + mm(d_similar(0, peer), rows_ref[peer, query_rows:, :])
        d_passage = d_passage + mm_tn(d_similar(peer, 0), rows_ref[peer, :query_rows, :])
    d_ref[:query_rows, :] = d_query
    d_ref[query_rows:, :] = d_passage


def score(gathered, begins, ends, logs, positive, query_rows, query_total, slots):
    peers, rows, _ = gathered.shape
    pack = rows - query_rows
    pairs = peers * peers * query_rows * pack
    vmem = pl.BlockSpec(memory_space=pltpu.VMEM)
    return pl.pallas_call(
        functools.partial(score_kernel, query_rows, float(query_total), slots),
        in_specs=[vmem] * 5,
        out_specs=[vmem, vmem],
        out_shape=[shape_of((8, LANES), F32), shape_of((rows, LANES), F32)],
        scratch_shapes=[
            pltpu.VMEM((peers, peers, query_rows, pack), F32),
            pltpu.VMEM((8, LANES), F32),
            pltpu.VMEM((peers, pack, LANES), BF),
            pltpu.VMEM((peers, query_rows, LANES), F32),
        ],
        compiler_params=pltpu.CompilerParams(vmem_limit_bytes=56 * MIB),
        cost_estimate=cost(8 * pairs * LANES, 4 * peers * rows * LANES, pairs),
        name="score",
    )(gathered, begins, ends, logs, positive)


def back_top_kernel(
    where_ref,
    d_ref,
    proj_ref,
    unit_ref,
    scale_ref,
    low_ref,
    embed_ref,
    vec_ref,
    mid_ref,
    down_ref,
    grad_ref,
    sum_ref,
    acc,
):
    step = pl.program_id(0)

    @pl.when(step == 0)
    def _():
        acc[...] = jnp.zeros_like(acc)
        sum_ref[...] = jnp.zeros_like(sum_ref)

    projected = proj_ref[...]
    given = d_ref[...]
    size = lax.rsqrt(jnp.sum(projected * projected, -1, keepdims=True) + UNIT_EPS)
    along = jnp.sum(given * projected, -1, keepdims=True)
    d_proj = (size * given - projected * (size * size * size * along)).astype(BF)
    acc[...] += mm_tn(low_ref[...], d_proj)
    d_out = mm_nt(d_proj, embed_ref[...])
    unit = unit_ref[...]
    d_mid = normalize_back(d_out, vec_ref[2:3, :], unit, scale_ref[...])
    mid_ref[...] = d_mid
    low = d_mid.astype(BF)
    down_ref[...] = low
    sum_ref[0:1, :] += jnp.sum(d_out * unit, 0, keepdims=True)
    sum_ref[1:2, :] += jnp.sum(d_out, 0, keepdims=True)
    sum_ref[2:3, :] += jnp.sum(low.astype(F32), 0, keepdims=True)

    @pl.when(step == pl.num_programs(0) - 1)
    def _():
        put_rows(where_ref, grad_ref, acc[...])


def back_top(where, d_unit, projected, unit_two, scale_two, low_two, w_embed, vectors):
    rows, width = unit_two.shape
    owned = width // PIECES // 2

    def tile(columns):
        return pl.BlockSpec((TILE, columns), lambda i, w: (i, 0))

    return pl.pallas_call(
        back_top_kernel,
        grid_spec=pltpu.PrefetchScalarGridSpec(
            num_scalar_prefetch=1,
            grid=(rows // TILE,),
            in_specs=[
                tile(LANES),
                tile(LANES),
                tile(width),
                tile(1),
                tile(width),
                full((width, LANES)),
                full((16, width)),
            ],
            out_specs=[
                tile(width),
                tile(width),
                full((2, PIECES, owned, LANES)),
                full((8, width)),
            ],
            scratch_shapes=[pltpu.VMEM((width, LANES), F32)],
        ),
        out_shape=[
            shape_of((rows, width), F32),
            shape_of((rows, width), BF),
            shape_of((2, PIECES, owned, LANES), BF),
            shape_of((8, width), F32),
        ],
        compiler_params=params(),
        cost_estimate=cost(4 * rows * width * LANES, rows * width * 12),
        name="back_top",
    )(where, d_unit, projected, unit_two, scale_two, low_two, w_embed, vectors)


def back_down_kernel(where_ref, d_ref, down_ref, slope_ref, active_ref, up_ref, grad_ref, sum_ref):
    given = d_ref[...]
    low = (mm_nt(given, down_ref[...]) * slope_ref[...].astype(F32)).astype(BF)
    up_ref[...] = low
    sum_ref[0:1, :] = jnp.sum(low.astype(F32), 0, keepdims=True)
    put_rows(where_ref, grad_ref, mm_tn(active_ref[...], given))


def back_down(where, d_down, w_down, slope, active):
    rows, width = d_down.shape
    wide = w_down.shape[0]
    steps = wide // width
    parts = PIECES // steps
    owned = wide // PIECES // 2
    column = pl.BlockSpec((rows, width), lambda t, w: (0, t))
    return pl.pallas_call(
        back_down_kernel,
        grid_spec=pltpu.PrefetchScalarGridSpec(
            num_scalar_prefetch=1,
            grid=(steps,),
            in_specs=[
                full((rows, width)),
                pl.BlockSpec((width, width), lambda t, w: (t, 0)),
                column,
                column,
            ],
            out_specs=[
                column,
                pl.BlockSpec(
                    (2, parts, owned, width),
                    lambda t, w: (0, lax.bitwise_xor(t, w[0] // parts), 0, 0),
                ),
                pl.BlockSpec((8, width), lambda t, w: (0, t)),
            ],
        ),
        out_shape=[
            shape_of((rows, wide), BF),
            shape_of((2, PIECES, owned, width), BF),
            shape_of((8, wide), F32),
        ],
        compiler_params=params(),
        cost_estimate=cost(4 * rows * width * wide, 6 * rows * wide + 4 * wide * width),
        name="back_down",
    )(where, d_down, w_down, slope, active)


def back_up_kernel(where_ref, mid_ref, low_ref, d_ref, up_ref, out_ref, grad_ref, turned):
    @pl.when(pl.program_id(0) == 0)
    def _():
        out_ref[...] = mid_ref[...]
        turned[...] = low_ref[...].T

    given = d_ref[...]
    out_ref[...] += mm_nt(given, up_ref[...])
    put_rows(where_ref, grad_ref, mm(turned[...], given))


def back_up(where, d_mid, low_one, d_up, w_up):
    rows, width = d_mid.shape
    wide = w_up.shape[1]
    owned = width // PIECES // 2
    return pl.pallas_call(
        back_up_kernel,
        grid_spec=pltpu.PrefetchScalarGridSpec(
            num_scalar_prefetch=1,
            grid=(wide // width,),
            in_specs=[
                full((rows, width)),
                full((rows, width)),
                pl.BlockSpec((rows, width), lambda t, w: (0, t)),
                pl.BlockSpec((width, width), lambda t, w: (0, t)),
            ],
            out_specs=[
                full((rows, width)),
                pl.BlockSpec((2, PIECES, owned, width), lambda t, w: (0, 0, 0, t)),
            ],
            scratch_shapes=[pltpu.VMEM((width, rows), BF)],
        ),
        out_shape=[
            shape_of((rows, width), F32),
            shape_of((2, PIECES, owned, wide), BF),
        ],
        compiler_params=params(),
        cost_estimate=cost(4 * rows * width * wide, 2 * rows * wide + 4 * wide * width),
        name="back_up",
    )(where, d_mid, low_one, d_up, w_up)


def back_out_kernel(
    where_ref,
    d_ref,
    unit_ref,
    scale_ref,
    context_ref,
    out_ref,
    vec_ref,
    resid_ref,
    d_context_ref,
    grad_ref,
    sum_ref,
    acc,
):
    step = pl.program_id(0)

    @pl.when(step == 0)
    def _():
        acc[...] = jnp.zeros_like(acc)
        sum_ref[...] = jnp.zeros_like(sum_ref)

    d_out = d_ref[...]
    unit = unit_ref[...]
    d_resid = normalize_back(d_out, vec_ref[0:1, :], unit, scale_ref[...])
    resid_ref[...] = d_resid
    low = d_resid.astype(BF)
    d_context_ref[...] = mm_nt(low, out_ref[...]).astype(BF)
    acc[...] += mm_tn(context_ref[...], low)
    sum_ref[0:1, :] += jnp.sum(d_out * unit, 0, keepdims=True)
    sum_ref[1:2, :] += jnp.sum(d_out, 0, keepdims=True)
    sum_ref[2:3, :] += jnp.sum(low.astype(F32), 0, keepdims=True)

    @pl.when(step == pl.num_programs(0) - 1)
    def _():
        put_rows(where_ref, grad_ref, acc[...])


def back_out(where, d_one, unit_one, scale_one, context, w_out, vectors):
    rows, width = d_one.shape
    owned = width // PIECES // 2

    def tile(columns):
        return pl.BlockSpec((TILE, columns), lambda i, w: (i, 0))

    return pl.pallas_call(
        back_out_kernel,
        grid_spec=pltpu.PrefetchScalarGridSpec(
            num_scalar_prefetch=1,
            grid=(rows // TILE,),
            in_specs=[
                tile(width),
                tile(width),
                tile(1),
                tile(width),
                full((width, width)),
                full((16, width)),
            ],
            out_specs=[
                tile(width),
                tile(width),
                full((2, PIECES, owned, width)),
                full((8, width)),
            ],
            scratch_shapes=[pltpu.VMEM((width, width), F32)],
        ),
        out_shape=[
            shape_of((rows, width), F32),
            shape_of((rows, width), BF),
            shape_of((2, PIECES, owned, width), BF),
            shape_of((8, width), F32),
        ],
        compiler_params=params(),
        cost_estimate=cost(4 * rows * width * width, rows * width * 16),
        name="back_out",
    )(where, d_one, unit_one, scale_one, context, w_out, vectors)


def back_in_kernel(resid_ref, *refs):
    *parts, in_ref, out_ref = refs
    total = resid_ref[...]
    column = 0
    for part in parts:
        count = part.shape[1]
        total = total + mm_nt(part[...], in_ref[:, column : column + count])
        column += count
    out_ref[...] = total


def back_in(d_resid, parts, w_in):
    rows, width = d_resid.shape

    def tile(columns):
        return pl.BlockSpec((TILE, columns), lambda i: (i, 0))

    return pl.pallas_call(
        back_in_kernel,
        grid=(rows // TILE,),
        in_specs=[tile(width)] + [tile(p.shape[1]) for p in parts] + [full(w_in.shape)],
        out_specs=tile(width),
        out_shape=shape_of((rows, width), F32),
        compiler_params=params(),
        cost_estimate=cost(6 * rows * width * width, rows * width * 14),
        name="back_in",
    )(d_resid, *parts, w_in)


def turn_kernel(where_ref, rows_ref, out_ref):
    rows = rows_ref[...]
    padded = jnp.concatenate([rows, jnp.zeros((LANES - rows.shape[0], rows.shape[1]), F32)], 0)
    put_rows(where_ref, out_ref, padded.T)


def turn(where, rows):
    width = rows.shape[1]
    owned = width // PIECES // 2
    return pl.pallas_call(
        turn_kernel,
        grid_spec=pltpu.PrefetchScalarGridSpec(
            num_scalar_prefetch=1,
            grid=(1,),
            in_specs=[full(rows.shape)],
            out_specs=full((2, PIECES, owned, LANES)),
        ),
        out_shape=shape_of((2, PIECES, owned, LANES), BF),
        compiler_params=params(),
        cost_estimate=cost(0, 8 * width * LANES),
        name="turn",
    )(where, rows)


def swap(block, bits):
    count = lax.axis_size(AXES)
    return lax.ppermute(block, AXES, [(d, d ^ bits) for d in range(count)])


def gather_columns(first, second, core):
    keep = jnp.where(core == 0, first, second)
    give = jnp.where(core == 0, second, first)
    theirs = swap(give, 1)
    mine = jnp.concatenate(
        [jnp.where(core == 0, keep, theirs), jnp.where(core == 0, theirs, keep)], 0
    )
    far = jnp.stack([mine] + [swap(mine, 8 * step) for step in (1, 2, 3)])
    width = mine.shape[1]
    cut = (width // LANES + 1) // 2 * LANES
    left, right = far[:, :, :cut], far[:, :, cut:]
    left = jnp.stack([left, swap(left, 2)], 1)
    right = jnp.stack([right, swap(right, 4)], 1)
    left = jnp.stack([left, swap(left, 4)], 1)
    right = jnp.stack([right, swap(right, 2)], 2)
    own = jnp.concatenate([left, right], -1).reshape(PIECES, mine.shape[0], width)
    return own, swap(own, 1)


def gather_plain(first, second):
    whole = [lax.all_gather(half, AXES, axis=0, tiled=True) for half in (first, second)]
    return [half.reshape(PIECES, -1, half.shape[1]) for half in whole]


def added(mine, theirs):
    return (mine.astype(F32) + theirs.astype(F32)).astype(BF)


def scatter_rows(blocks):
    _, _, rows, width = blocks.shape
    near = added(blocks[0], swap(blocks[1], 1)).reshape(4, 2, 2, rows, width)
    cut = (width // LANES + 1) // 2 * LANES
    left, right = near[..., :cut], near[..., cut:]
    left = added(left[:, :, 0], swap(left[:, :, 1], 2))
    right = added(right[:, 0], swap(right[:, 1], 4))
    left = added(left[:, 0], swap(left[:, 1], 4))
    right = added(right[:, 0], swap(right[:, 1], 2))
    far = jnp.concatenate([left, right], -1)
    total = far[0].astype(F32)
    for step in (1, 2, 3):
        total = total + swap(far[step], 8 * step).astype(F32)
    return total


def scatter_plain(blocks):
    _, pieces, rows, width = blocks.shape
    whole = blocks.transpose(1, 0, 2, 3).reshape(2 * pieces * rows, width)
    return lax.psum_scatter(whole, AXES, scatter_dimension=0, tiled=True).astype(F32)


def sum_everywhere(values):
    count = lax.axis_size(AXES)
    bit = 1
    while bit < count:
        values = values + swap(values, bit)
        bit *= 2
    return values


def gather_peers(block):
    peers = block[None]
    bit = lax.axis_size("psg") // 2
    while bit > 0:
        peers = jnp.stack([peers, swap(peers, bit)], 1).reshape(-1, *block.shape)
        bit //= 2
    return peers


def adam_step(weight, grad, first, second, rate, decay):
    first_new = BETA_ONE * first + (1.0 - BETA_ONE) * grad
    second_new = BETA_TWO * second + (1.0 - BETA_TWO) * grad * grad
    fix_one = 1.0 - BETA_ONE**STEP
    fix_two = 1.0 - BETA_TWO**STEP
    update = first_new / fix_one / (jnp.sqrt(second_new / fix_two) + ADAM_EPS)
    return (first_new, second_new, weight - rate * (update + decay * weight))


def local(hidden, lengths_in, positive, *shards):
    masters, firsts, seconds = shards[:6], shards[6:12], shards[12:]
    low = [master.astype(BF) for master in masters]
    psg_count = lax.axis_size("psg")
    count = lax.axis_size(AXES)
    split = count == 2 * PIECES
    mine = lax.axis_index("psg")
    rows, width = hidden.shape
    queries = positive.shape[0]
    query_rows = queries * QLEN
    query_total = queries * count
    slots = lengths_in.shape[1]
    pack = rows - query_rows
    index = lax.axis_index(AXES)
    if split:
        where = jnp.stack([index // 2, index % 2]).astype(jnp.int32)
    else:
        where = jnp.zeros((2,), jnp.int32)

    half_in, half_out = 3 * width // 2, width // 2
    padded = jnp.pad(low[5], ((0, 0), (0, LANES - low[5].shape[1])))
    halves = [
        jnp.concatenate([low[0][:, :half_in], low[1][:, :half_out], low[4]], 1),
        jnp.concatenate([low[0][:, half_in:], low[1][:, half_out:], padded], 1),
    ]
    wide = low[2].shape[1]
    up_halves = [low[2][:, : wide // 2], low[2][:, wide // 2 :]]
    if split:
        front = gather_columns(*halves, where[1])
        up = gather_columns(*up_halves, where[1])
    else:
        front = gather_plain(*halves)
        up = gather_plain(*up_halves)
    w_down = lax.all_gather(low[3], AXES, axis=0, tiled=True)

    facts = gather_peers(jnp.concatenate([lengths_in[0], positive])[None])
    facts = facts.reshape(psg_count, -1)
    lengths, chosen = facts[:, :slots], facts[:, slots:]
    ends = jnp.cumsum(lengths, 1)
    lane_slot = jnp.eye(psg_count, dtype=jnp.int32)[:, :, None]
    unused = LANES - psg_count * slots

    def by_lane(values):
        spread = (lane_slot * values[:, None, :]).reshape(psg_count, psg_count * slots)
        return jnp.pad(spread, ((0, 0), (0, unused)))

    end_lanes = by_lane(ends)
    begin_lanes = by_lane(ends - lengths)
    log_lanes = jnp.pad(jnp.log(lengths.astype(F32)).reshape(1, -1), ((0, 0), (0, unused)))
    chosen = jnp.bitwise_xor(chosen, mine * slots)[:, :, None]
    places = jnp.arange(pack, dtype=jnp.int32)
    segment = jnp.sum((places[:, None] >= ends[0][None, :]).astype(jnp.int32), -1)
    seg_col, seg_row = segment[:, None], segment[None, :]
    turned = hidden.T

    merged, w_in, w_out, w_embed, vectors = project(where, hidden, *front)
    context = attend(merged, seg_col, seg_row, query_rows)
    unit_one, scale_one, low_one, active, slope, w_up = widen(
        where, context, hidden, w_out, vectors, *up
    )
    unit_two, scale_two, low_two, projected, embedded = narrow(
        active, w_down, unit_one, vectors, w_embed
    )
    peers = gather_peers(embedded)
    loss_block, d_unit = score(
        peers, begin_lanes, end_lanes, log_lanes, chosen, query_rows, query_total, slots
    )
    d_mid, d_down, grad_embed, sums_top = back_top(
        where, d_unit, projected, unit_two, scale_two, low_two, w_embed, vectors
    )
    d_up, grad_down, sums_up = back_down(where, d_down, w_down, slope, active)
    scatter = scatter_rows if split else scatter_plain
    total_down = scatter(grad_down)
    d_one, grad_up = back_up(where, d_mid, low_one, d_up, w_up)
    d_resid, d_context, grad_out, sums_out = back_out(
        where, d_one, unit_one, scale_one, context, w_out, vectors
    )
    total_mid = scatter(jnp.concatenate([grad_up, grad_out, grad_embed], -1))
    pairs = width // LANES
    parts, sums_in, totals_in = [], [], []
    for begin in (0, pairs // 2):
        *d_part, grad_in, sums_part = attend_back(
            where, merged, d_context, turned, seg_col, seg_row, query_rows, begin, pairs // 2
        )
        parts.append(d_part)
        sums_in.append(sums_part)
        if begin > 0:
            both = jnp.concatenate(sums_in, 1)
            stacked = [sums_out[0:2], sums_top[0:2], both[0:2], sums_out[2:3], sums_top[2:3]]
            stacked.append(sums_up[0].reshape(-1, width))
            vector_rows = jnp.concatenate(stacked, 0)
            vector_count = vector_rows.shape[0]
            vector_rows = jnp.pad(vector_rows, ((0, 16 - vector_count), (0, 0)))
            grad_in = jnp.concatenate([grad_in, turn(where, vector_rows)], -1)
        totals_in.append(scatter(grad_in))
    ordered = [parts[half][part] for part in (0, 1, 2) for half in (0, 1)]
    input_grad = back_in(d_resid, ordered, w_in)

    owned = totals_in[0].shape[0]
    half = totals_in[0].shape[1]
    inward = [total[:, :half].reshape(owned, pairs // 2, 3, LANES) for total in totals_in]
    inward = jnp.concatenate(inward, 1).transpose(0, 2, 1, 3).reshape(owned, 3 * width)
    summed = (
        inward,
        total_mid[:, wide : wide + width],
        total_mid[:, :wide],
        total_down,
        total_mid[:, wide + width :],
        totals_in[1][:, half : half + vector_count],
    )
    squares = sum(jnp.sum(grad * grad) for grad in summed)
    pair = jnp.stack([loss_block[0, 0], squares])
    pair = sum_everywhere(jnp.broadcast_to(pair[:, None], (2, LANES)))
    loss = pair[0, 0] / query_total
    grad_norm = jnp.sqrt(pair[1, 0])
    factor = CLIP_NORM / jnp.maximum(grad_norm, CLIP_NORM)
    stepped = []
    for item in range(6):
        rate = RATE_VECTOR if item == 5 else RATE_MATRIX
        decay = 0.0 if item == 5 else DECAY
        stepped.append(
            adam_step(masters[item], summed[item] * factor, firsts[item], seconds[item], rate, decay)
        )
    return (loss, input_grad, grad_norm) + tuple(
        stepped[item][which] for which in (0, 1, 2) for item in range(6)
    )


def solution(mesh):
    by_rows = P(AXES, None)
    placed = (by_rows, by_rows, P(AXES)) + (by_rows,) * 18
    return jax.shard_map(
        local,
        mesh=mesh,
        in_specs=placed,
        out_specs=(P(), by_rows, P()) + (by_rows,) * 18,
        check_vma=False,
    )
```

```python
import functools

import jax
import jax.numpy as jnp
from jax import lax
from jax.experimental import pallas as pl
from jax.experimental.pallas import tpu as pltpu
from jax.sharding import PartitionSpec as P

HEADS = 12
HEAD = 64
QLEN = 32
STEP = 10

TAU_INV = 10.0
SCORE_SCALE = 10.0
CLIP_NORM = 0.02
BETA_ONE = 0.9
BETA_TWO = 0.999
ADAM_EPS = 1e-08
RATE_MATRIX = 0.05
RATE_VECTOR = 0.5
DECAY = 0.01
NORM_EPS = 1e-12
UNIT_EPS = 1e-06

AXES = ("group", "psg")
LANES = 128
PIECES = 16
TILE = 256
MIB = 2**20
BF = jnp.bfloat16
F32 = jnp.float32


def mm(left, right):
    return lax.dot_general(left, right, (((1,), (0,)), ((), ())), preferred_element_type=F32)


def mm_nt(left, right):
    return lax.dot_general(left, right, (((1,), (1,)), ((), ())), preferred_element_type=F32)


def mm_tn(left, right):
    return lax.dot_general(left, right, (((0,), (0,)), ((), ())), preferred_element_type=F32)


def full(shape):
    return pl.BlockSpec(shape, lambda *_: (0,) * len(shape))


def params(mib=56):
    return pltpu.CompilerParams(
        vmem_limit_bytes=mib * MIB, dimension_semantics=("arbitrary",)
    )


def cost(flops, moved, special=0):
    return pl.CostEstimate(flops=int(flops), bytes_accessed=int(moved), transcendentals=int(special))


def shape_of(shape, dtype):
    return jax.ShapeDtypeStruct(shape, dtype)


def far_shape(shape, dtype):
    return pltpu.HBM(shape, dtype)


def far(*blocks):
    held = [pltpu.with_memory_space_constraint(block, pltpu.HBM) for block in blocks]
    return held if len(held) > 1 else held[0]


def near_shape(shape, dtype):
    return pltpu.VMEM(shape, dtype)


def near(*blocks):
    held = [pltpu.with_memory_space_constraint(block, pltpu.VMEM) for block in blocks]
    return held if len(held) > 1 else held[0]


def any_space():
    return pl.BlockSpec(memory_space=pl.ANY)


def fetch_pieces(where_ref, own_ref, other_ref, moves, sems):
    chip, core = where_ref[0], where_ref[1]
    rows = own_ref.shape[1]

    def start(halves):
        for piece in range(own_ref.shape[0]):
            source = lax.bitwise_xor(chip, piece)
            for number, (half, first, width, target, column) in enumerate(moves):
                pltpu.make_async_copy(
                    halves[half].at[source, :, pl.ds(first, width)],
                    target.at[pl.ds(rows * piece, rows), pl.ds(column, width)],
                    sems.at[number],
                ).start()

    pl.when(core == 0)(lambda: start((own_ref, other_ref)))
    pl.when(core == 1)(lambda: start((other_ref, own_ref)))
    for number, (_, _, width, target, column) in enumerate(moves):
        landed = target.at[:, pl.ds(column, width)]
        pltpu.make_async_copy(landed, landed, sems.at[number]).wait()


def pack_kernel(where_ref, in_ref, out_ref, up_ref, embed_ref, vec_ref, down_ref, *targets):
    front_keep, front_give, rest_keep, rest_give, down_low = targets
    half_in, half_out, half_up = (ref.shape[1] // 2 for ref in (in_ref, out_ref, up_ref))
    owned = in_ref.shape[0]
    down_low[...] = down_ref[...].astype(BF)

    def fill(front, rest, half):
        front[:, :half_in] = in_ref[:, half * half_in : (half + 1) * half_in].astype(BF)
        if half == 0:
            front[:, half_in:] = embed_ref[...].astype(BF)
        else:
            empty = jnp.zeros((owned, LANES - vec_ref.shape[1]), F32)
            front[:, half_in:] = jnp.concatenate([vec_ref[...], empty], 1).astype(BF)
        rest[:, :half_up] = up_ref[:, half * half_up : (half + 1) * half_up].astype(BF)
        rest[:, half_up:] = out_ref[:, half * half_out : (half + 1) * half_out].astype(BF)

    @pl.when(where_ref[1] == 0)
    def _():
        fill(front_keep, rest_keep, 0)
        fill(front_give, rest_give, 1)

    @pl.when(where_ref[1] == 1)
    def _():
        fill(front_keep, rest_keep, 1)
        fill(front_give, rest_give, 0)


def pack(where, inward, outward, upward, embed, vectors, downward):
    owned, width = outward.shape
    front = 3 * width // 2 + LANES
    rest = upward.shape[1] // 2 + width // 2
    vmem = pl.BlockSpec(memory_space=pltpu.VMEM)
    return pl.pallas_call(
        pack_kernel,
        in_specs=[pl.BlockSpec(memory_space=pltpu.SMEM)] + [vmem] * 6,
        out_specs=[vmem] * 5,
        out_shape=[
            shape_of((owned, front), BF),
            shape_of((owned, front), BF),
            shape_of((owned, rest), BF),
            shape_of((owned, rest), BF),
            shape_of(downward.shape, BF),
        ],
        compiler_params=pltpu.CompilerParams(vmem_limit_bytes=16 * MIB),
        name="pack",
    )(where, inward, outward, upward, embed, vectors, downward)


def project_kernel(
    where_ref, rows_ref, own_ref, other_ref, merged_ref, turned_ref, in_ref, embed_ref, vec_ref, raw, sems
):
    width = rows_ref.shape[1]
    half_in = 3 * width // 2

    @pl.when(pl.program_id(0) == 0)
    def _():
        moves = [(half, 0, half_in, in_ref, half * half_in) for half in (0, 1)]
        moves.append((0, half_in, LANES, embed_ref, 0))
        moves.append((1, half_in, LANES, raw, 0))
        fetch_pieces(where_ref, own_ref, other_ref, moves, sems)
        vec_ref[...] = raw[...].astype(F32).T[: vec_ref.shape[0]]

    rows = rows_ref[...]
    turned_ref[...] = rows.T
    for part, bias in ((0, 4), (1, None), (2, 5)):
        block = mm(rows, in_ref[:, part * width : (part + 1) * width])
        if bias is not None:
            block = block + vec_ref[bias : bias + 1, :]
        merged_ref[:, part * width : (part + 1) * width] = block.astype(BF)


def project(where, hidden, own, other):
    rows, width = hidden.shape
    return pl.pallas_call(
        project_kernel,
        grid_spec=pltpu.PrefetchScalarGridSpec(
            num_scalar_prefetch=1,
            grid=(rows // TILE,),
            in_specs=[pl.BlockSpec((TILE, width), lambda i, w: (i, 0)), any_space(), any_space()],
            out_specs=[
                pl.BlockSpec((TILE, 3 * width), lambda i, w: (i, 0)),
                pl.BlockSpec((width, TILE), lambda i, w: (0, i)),
                full((width, 3 * width)),
                full((width, LANES)),
                full((16, width)),
            ],
            scratch_shapes=[pltpu.VMEM((width, LANES), BF), pltpu.SemaphoreType.DMA((4,))],
        ),
        out_shape=[
            far_shape((rows, 3 * width), BF),
            far_shape((width, rows), BF),
            far_shape((width, 3 * width), BF),
            shape_of((width, LANES), BF),
            shape_of((16, width), F32),
        ],
        compiler_params=params(20),
        cost_estimate=cost(6 * rows * width * width, 8 * rows * width + 16 * width * width),
        name="project",
    )(where, *far(hidden, own, other))


def head_masks():
    lane = lax.broadcasted_iota(jnp.int32, (1, LANES), 1)
    return [(lane < HEAD).astype(BF), (lane >= HEAD).astype(BF)]


def softmax_rows(scores):
    peak = jnp.max(scores, -1, keepdims=True)
    expo = jnp.exp(scores - peak)
    return expo * (1.0 / jnp.sum(expo, -1, keepdims=True))


QUERY_TILE = 256
PACK_TILE = 384


def blocks_of(rows, query_rows):
    size = QUERY_TILE
    listed = [(first, size, first, size, True) for first in range(0, query_rows, size)]
    for first in range(query_rows, rows, PACK_TILE):
        listed.append((first, PACK_TILE, query_rows, rows - query_rows, False))
    return listed


def allowed_pairs(block, seg_col, seg_row, query_rows):
    first, count, _, keys, is_query = block
    if is_query:
        mine = lax.broadcasted_iota(jnp.int32, (count, keys), 0) // QLEN
        theirs = lax.broadcasted_iota(jnp.int32, (count, keys), 1) // QLEN
        return mine == theirs
    begin = first - query_rows
    return seg_col[begin : begin + count, :] == seg_row[0:1, :]


def attend_kernel(query_rows, seg_col, seg_row, q_ref, k_ref, v_ref, out_ref):
    masks = head_masks()
    blocks = blocks_of(q_ref.shape[0], query_rows)

    def products(block):
        first, count, begin, keys, _ = block
        query = q_ref[first : first + count, :]
        key = k_ref[begin : begin + keys, :]
        return [mm_nt(query * (mask * HEAD**-0.5), key) for mask in masks]

    ahead = products(blocks[0])
    for place, block in enumerate(blocks):
        first, count, begin, keys, _ = block
        scores = ahead
        if place + 1 < len(blocks):
            ahead = products(blocks[place + 1])
        allowed = allowed_pairs(block, seg_col, seg_row, query_rows)
        value = v_ref[begin : begin + keys, :]
        total = None
        for mask, score in zip(masks, scores):
            weights = softmax_rows(jnp.where(allowed, score, -1e9)).astype(BF)
            part = mm(weights, value * mask)
            total = part if total is None else total + part
        out_ref[first : first + count, :] = total.astype(BF)


def attend(merged, seg_col, seg_row, query_rows, first_pair, count):
    rows, wide = merged.shape
    pairs = wide // 3 // LANES
    pack = rows - query_rows

    def column(part):
        return pl.BlockSpec((rows, LANES), lambda h: (0, part * pairs + first_pair + h))

    return pl.pallas_call(
        functools.partial(attend_kernel, query_rows),
        grid=(count,),
        in_specs=[full((pack, 1)), full((1, pack)), column(0), column(1), column(2)],
        out_specs=pl.BlockSpec((rows, LANES), lambda h: (0, h)),
        out_shape=shape_of((rows, count * LANES), BF),
        compiler_params=params(16),
        cost_estimate=cost(
            16 * count * pack * pack * LANES, 8 * rows * count * LANES, 2 * count * pack * pack
        ),
        name="attend",
    )(seg_col, seg_row, *far(merged, merged, merged))


def put_rows(where_ref, own_ref, other_ref, values):
    pieces, rows = own_ref.shape[0], own_ref.shape[1]
    chip = lax.bitwise_and(where_ref[0], pieces - 1)

    def store(targets):
        for piece in range(pieces):
            for half in (0, 1):
                begin = (2 * piece + half) * rows
                targets[half][lax.bitwise_xor(chip, piece)] = values[begin : begin + rows, :].astype(BF)

    pl.when(where_ref[1] == 0)(lambda: store((own_ref, other_ref)))
    pl.when(where_ref[1] == 1)(lambda: store((other_ref, own_ref)))


def attend_back_pair(query_rows, seg_col, seg_row, q_ref, k_ref, v_ref, d_ref, dq_ref, dk_ref, dv_ref, acc_k, acc_v):
    masks = head_masks()
    rows = q_ref.shape[0]
    blocks = blocks_of(rows, query_rows)

    def products(block):
        first, count, begin, keys, _ = block
        query = q_ref[first : first + count, :]
        given = d_ref[first : first + count, :]
        key = k_ref[begin : begin + keys, :]
        value = v_ref[begin : begin + keys, :]
        made = []
        for mask in masks:
            scaled = query * (mask * HEAD**-0.5)
            own = given * mask
            made.append((scaled, own, mm_nt(scaled, key), mm_nt(own, value)))
        return made

    ahead = products(blocks[0])
    started = False
    for place, block in enumerate(blocks):
        first, count, begin, keys, is_query = block
        held = ahead
        if place + 1 < len(blocks):
            ahead = products(blocks[place + 1])
        allowed = allowed_pairs(block, seg_col, seg_row, query_rows)
        key = k_ref[begin : begin + keys, :]
        dq = dk = dv = 0.0
        for mask, (scaled, own, scores, d_weights) in zip(masks, held):
            weights = softmax_rows(jnp.where(allowed, scores, -1e9))
            inner = jnp.sum(d_weights * weights, -1, keepdims=True)
            d_scores = (weights * (d_weights - inner)).astype(BF)
            dq = dq + mm(d_scores, key * (mask * HEAD**-0.5))
            dk = dk + mm_tn(d_scores, scaled)
            dv = dv + mm_tn(weights.astype(BF), own)
        dq_ref[first : first + count, :] = dq.astype(BF)
        if is_query:
            dk_ref[begin : begin + keys, :] = dk.astype(BF)
            dv_ref[begin : begin + keys, :] = dv.astype(BF)
        elif started:
            acc_k[...] += dk
            acc_v[...] += dv
        else:
            acc_k[...] = dk
            acc_v[...] = dv
            started = True
    dk_ref[query_rows:, :] = acc_k[...].astype(BF)
    dv_ref[query_rows:, :] = acc_v[...].astype(BF)


def column_sums(block):
    return jnp.sum(block.astype(F32), 0, keepdims=True)


def attend_back_kernel(query_rows, count, extra, where_ref, *refs):
    seg_col, seg_row, q_ref, k_ref, v_ref, d_ref, turned_ref, *refs = refs
    passed, refs = refs[: len(refs) - 8], refs[len(refs) - 8 :]
    dq_ref, dk_ref, dv_ref, own_ref, other_ref, sum_ref, acc_k, acc_v = refs
    step = pl.program_id(0)

    @pl.when(step < count)
    def _():
        attend_back_pair(
            query_rows, seg_col, seg_row, q_ref, k_ref, v_ref, d_ref, dq_ref, dk_ref, dv_ref, acc_k, acc_v
        )
        turned = turned_ref[...]
        grads = [mm(turned, ref[...]) for ref in (dq_ref, dk_ref, dv_ref)]
        put_rows(where_ref, own_ref, other_ref, jnp.concatenate(grads, 1))
        empty = jnp.zeros((6, LANES), F32)
        sums = [column_sums(dq_ref[...]), column_sums(dv_ref[...]), empty]
        sum_ref[step] = jnp.concatenate(sums, 0)

    @pl.when(step >= count)
    def _():
        if extra == "copied":
            own_ref[...] = passed[0][...]
            other_ref[...] = passed[1][...]
        elif extra == "vectors":
            own_embed, other_embed, out_sums, top_sums, up_sums, *in_sums = passed
            width = out_sums.shape[1]
            blocks = [ref[place] for ref in in_sums for place in range(ref.shape[0])]
            both = jnp.concatenate(blocks + [sum_ref[place] for place in range(count)], 1)
            stacked = [out_sums[0:2, :], top_sums[0:2, :], both[0:2]]
            stacked += [out_sums[2:3, :], top_sums[2:3, :]]
            for part in range(up_sums.shape[1] // width):
                stacked.append(up_sums[0:1, part * width : (part + 1) * width])
            used = sum(block.shape[0] for block in stacked)
            stacked.append(jnp.zeros((LANES - used, width), F32))
            turned_sums = jnp.concatenate(stacked, 0).T
            empty = jnp.zeros((width, 2 * LANES), F32)
            put_rows(where_ref, own_ref, other_ref, jnp.concatenate([turned_sums, empty], 1))
            own_ref[:, :, LANES : 2 * LANES] = own_embed[...]
            other_ref[:, :, LANES : 2 * LANES] = other_embed[...]


def attend_back(
    where, merged, d_context, turned, seg_col, seg_row, query_rows, first_pair, count, extra=None, passed=()
):
    rows, wide = merged.shape
    width = wide // 3
    pairs = width // LANES
    pack = rows - query_rows
    owned = width // PIECES // 2
    block = 3 * LANES
    steps = count
    passed_specs = []
    if extra == "copied":
        steps = count + passed[0].shape[2] // block
        own = pl.BlockSpec((PIECES, owned, block), lambda h, w: (0, 0, jnp.maximum(h - count, 0)))
        passed_specs = [own, own]
    elif extra == "vectors":
        steps = count + 1
        passed_specs = [full(block_in.shape) for block_in in passed]

    def pair_of(step):
        return jnp.minimum(step, count - 1)

    def column(part):
        return pl.BlockSpec((rows, LANES), lambda h, w: (0, part * pairs + first_pair + pair_of(h)))

    own_column = pl.BlockSpec((rows, LANES), lambda h, w: (0, pair_of(h)))
    grad_block = pl.BlockSpec((PIECES, owned, block), lambda h, w: (0, 0, h))
    return pl.pallas_call(
        functools.partial(attend_back_kernel, query_rows, count, extra),
        grid_spec=pltpu.PrefetchScalarGridSpec(
            num_scalar_prefetch=1,
            grid=(steps,),
            in_specs=[
                full((pack, 1)),
                full((1, pack)),
                column(0),
                column(1),
                column(2),
                pl.BlockSpec((rows, LANES), lambda h, w: (0, first_pair + pair_of(h))),
                full((width, rows)),
                *passed_specs,
            ],
            out_specs=[
                own_column,
                own_column,
                own_column,
                grad_block,
                grad_block,
                full((count, 8, LANES)),
            ],
            scratch_shapes=[pltpu.VMEM((pack, LANES), F32), pltpu.VMEM((pack, LANES), F32)],
        ),
        out_shape=[
            shape_of((rows, count * LANES), BF),
            shape_of((rows, count * LANES), BF),
            shape_of((rows, count * LANES), BF),
            shape_of((PIECES, owned, steps * block), BF),
            shape_of((PIECES, owned, steps * block), BF),
            shape_of((count, 8, LANES), F32),
        ],
        compiler_params=params(24),
        cost_estimate=cost(
            count * (20 * pack * pack * LANES + 6 * rows * width * LANES),
            count * rows * LANES * 14,
            2 * count * pack * pack,
        ),
        name="attend_back",
    )(where, seg_col, seg_row, *far(merged, merged, merged), d_context, far(turned), *passed)


def normalize(residual):
    center = jnp.mean(residual, -1, keepdims=True)
    shifted = residual - center
    spread = jnp.mean(shifted * shifted, -1, keepdims=True)
    scale = lax.rsqrt(spread + NORM_EPS)
    return shifted * scale, scale


def normalize_back(d_out, gain, unit, scale):
    d_unit = d_out * gain
    return scale * (
        d_unit
        - jnp.mean(d_unit, -1, keepdims=True)
        - unit * jnp.mean(d_unit * unit, -1, keepdims=True)
    )


def gelu_parts(given):
    below = 0.5 + 0.5 * lax.erf(given * 0.5**0.5)
    bell = jnp.exp(-0.5 * given * given)
    return given * below, below + given * bell * 0.3989422804014327


def encode_kernel(
    where_ref,
    first_ref,
    second_ref,
    hidden_ref,
    vec_ref,
    embed_ref,
    down_ref,
    own_ref,
    other_ref,
    unit_ref,
    scale_ref,
    low_ref,
    active_ref,
    slope_ref,
    unit_two_ref,
    scale_two_ref,
    low_two_ref,
    proj_ref,
    row_ref,
    up_far,
    out_far,
    up_ref,
    out_ref,
    sems,
    sent,
):
    width = hidden_ref.shape[1]
    half, half_out = up_ref.shape[1] // 2, width // 2
    copies = [
        pltpu.make_async_copy(up_ref, up_far, sent.at[0]),
        pltpu.make_async_copy(out_ref, out_far, sent.at[1]),
    ]

    @pl.when(pl.program_id(0) == 0)
    def _():
        moves = []
        for side in (0, 1):
            moves.append((side, half, half_out, out_ref, side * half_out))
            moves.append((side, 0, half, up_ref, side * half))
        fetch_pieces(where_ref, own_ref, other_ref, moves, sems)
        for copy in copies:
            copy.start()

    cut = first_ref.shape[1]
    branch = mm(first_ref[...], out_ref[:cut, :]) + mm(second_ref[...], out_ref[cut:, :])
    unit, scale = normalize(hidden_ref[...].astype(F32) + (branch + vec_ref[6:7, :]))
    unit_ref[...] = unit
    scale_ref[...] = scale
    first = unit * vec_ref[0:1, :] + vec_ref[1:2, :]
    low = first.astype(BF)
    low_ref[...] = low
    parts = up_ref.shape[1] // width

    def raised_part(part):
        raised = mm(low, up_ref[:, part * width : (part + 1) * width])
        return raised + vec_ref[8 + part : 9 + part, :]

    ahead = raised_part(0)
    total = first + vec_ref[7:8, :]
    for part in range(parts):
        raised = ahead
        if part + 1 < parts:
            ahead = raised_part(part + 1)
        columns = slice(part * width, (part + 1) * width)
        value, slope = gelu_parts(raised)
        value = value.astype(BF)
        active_ref[:, columns] = value
        slope_ref[:, columns] = slope.astype(BF)
        total = total + mm(value, down_ref[columns, :])
    unit, scale = normalize(total)
    unit_two_ref[...] = unit
    scale_two_ref[...] = scale
    low = (unit * vec_ref[2:3, :] + vec_ref[3:4, :]).astype(BF)
    low_two_ref[...] = low
    projected = mm(low, embed_ref[...])
    proj_ref[...] = projected
    size = jnp.sum(projected * projected, -1, keepdims=True)
    row_ref[...] = (projected * lax.rsqrt(size + UNIT_EPS)).astype(BF)

    @pl.when(pl.program_id(0) == pl.num_programs(0) - 1)
    def _():
        for copy in copies:
            copy.wait()


def encode(where, contexts, hidden, vectors, w_embed, w_down, own, other):
    rows, width = hidden.shape
    wide = w_down.shape[0]

    def tile(columns):
        return pl.BlockSpec((TILE, columns), lambda i, w: (i, 0))

    return pl.pallas_call(
        encode_kernel,
        grid_spec=pltpu.PrefetchScalarGridSpec(
            num_scalar_prefetch=1,
            grid=(rows // TILE,),
            in_specs=[
                *[tile(part.shape[1]) for part in contexts],
                tile(width),
                full((16, width)),
                full((width, LANES)),
                full((wide, width)),
                any_space(),
                any_space(),
            ],
            out_specs=[
                tile(width),
                tile(1),
                tile(width),
                tile(wide),
                tile(wide),
                tile(width),
                tile(1),
                tile(width),
                tile(LANES),
                tile(LANES),
                any_space(),
                any_space(),
            ],
            scratch_shapes=[
                pltpu.VMEM((width, wide), BF),
                pltpu.VMEM((width, width), BF),
                pltpu.SemaphoreType.DMA((4,)),
                pltpu.SemaphoreType.DMA((2,)),
            ],
        ),
        out_shape=[
            far_shape((rows, width), F32),
            far_shape((rows, 1), F32),
            far_shape((rows, width), BF),
            far_shape((rows, wide), BF),
            far_shape((rows, wide), BF),
            far_shape((rows, width), F32),
            far_shape((rows, 1), F32),
            far_shape((rows, width), BF),
            far_shape((rows, LANES), F32),
            shape_of((rows, LANES), BF),
            far_shape((width, wide), BF),
            far_shape((width, width), BF),
        ],
        compiler_params=params(44),
        cost_estimate=cost(
            2 * rows * width * (width + 2 * wide), rows * (20 * width + 4 * wide), rows * wide
        ),
        name="encode",
    )(where, *contexts, far(hidden), vectors, w_embed, *far(w_down, own, other))


def split_two(values):
    high = values.astype(BF)
    return high, (values - high.astype(F32)).astype(BF)


def score_kernel(
    query_rows,
    query_total,
    slots,
    begin_ref,
    end_ref,
    log_ref,
    positive_ref,
    *refs,
):
    *block_refs, loss_ref, d_ref, rows_ref, expo, member, scaled = refs
    peers, rows, _ = rows_ref.shape
    place = 0
    for ref in block_refs:
        rows_ref[place : place + ref.shape[0]] = ref[...]
        place += ref.shape[0]
    pack = rows - query_rows
    queries = query_rows // QLEN
    place = lax.broadcasted_iota(jnp.int32, (pack, LANES), 0)
    lane = lax.broadcasted_iota(jnp.int32, (1, LANES), 1)
    for peer in range(peers):
        inside = (place >= begin_ref[peer : peer + 1, :]) & (place < end_ref[peer : peer + 1, :])
        member[peer] = inside.astype(F32).astype(BF)

    def forward(asker, carry):
        query = rows_ref[asker, :query_rows, :]
        total = jnp.zeros((query_rows, LANES), F32)
        peaks = jnp.zeros((query_rows, LANES), F32)
        for peer in range(peers):
            similar = mm_nt(query, rows_ref[peer, query_rows:, :])
            peak = jnp.max(similar, -1, keepdims=True)
            value = jnp.exp((similar - peak) * TAU_INV)
            if peer == 0:
                expo[asker] = value
            else:

                @pl.when(asker == 0)
                def _():
                    expo[peers + peer] = value

            high, low = split_two(value)
            total = total + (mm(high, member[peer]) + mm(low, member[peer]))
            peaks = jnp.where(lane // slots == peer, peak, peaks)
        used = lane < peers * slots
        total = jnp.where(used, total, 1.0)
        smooth = jnp.log(total) / TAU_INV + peaks - log_ref[...] / TAU_INV
        logits = SCORE_SCALE * jnp.sum(smooth.reshape(queries, QLEN, LANES), 1)
        logits = jnp.where(used, logits, -1e30)
        picked = (positive_ref[asker] == lane).astype(F32)
        high = jnp.max(logits, -1, keepdims=True)
        powers = jnp.where(used, jnp.exp(logits - high), 0.0)
        norm = jnp.sum(powers, -1, keepdims=True)
        each = high + jnp.log(norm) - jnp.sum(picked * logits, -1, keepdims=True)
        d_logits = (powers / norm - picked) / query_total
        spread = jnp.broadcast_to(
            (SCORE_SCALE * d_logits)[:, None, :], (queries, QLEN, LANES)
        ).reshape(query_rows, LANES)
        scaled[asker] = jnp.where(used, spread / total, 0.0)

        @pl.when(asker == 0)
        def _():
            loss_ref[...] = jnp.broadcast_to(jnp.sum(each), loss_ref.shape)

        return carry

    lax.fori_loop(0, peers, forward, 0)

    def d_similar(asker, peer):
        high, low = split_two(scaled[asker])
        factor = mm_nt(high, member[peer]) + mm_nt(low, member[peer])
        return (expo[asker if peer == 0 else peers + peer] * factor).astype(BF)

    shared = d_similar(0, 0)
    d_query = mm(shared, rows_ref[0, query_rows:, :])
    d_passage = mm_tn(shared, rows_ref[0, :query_rows, :])
    for peer in range(1, peers):
        d_query = d_query + mm(d_similar(0, peer), rows_ref[peer, query_rows:, :])
        d_passage = d_passage + mm_tn(d_similar(peer, 0), rows_ref[peer, :query_rows, :])
    d_ref[:query_rows, :] = d_query
    d_ref[query_rows:, :] = d_passage


def score(blocks, begins, ends, logs, positive, query_rows, query_total, slots):
    peers, rows = sum(block.shape[0] for block in blocks), blocks[0].shape[1]
    pack = rows - query_rows
    pairs = peers * peers * query_rows * pack
    vmem = pl.BlockSpec(memory_space=pltpu.VMEM)
    return pl.pallas_call(
        functools.partial(score_kernel, query_rows, float(query_total), slots),
        in_specs=[vmem] * (4 + len(blocks)),
        out_specs=[vmem, vmem],
        out_shape=[shape_of((8, LANES), F32), shape_of((rows, LANES), F32)],
        scratch_shapes=[
            pltpu.VMEM((peers, rows, LANES), BF),
            pltpu.VMEM((2 * peers, query_rows, pack), F32),
            pltpu.VMEM((peers, pack, LANES), BF),
            pltpu.VMEM((peers, query_rows, LANES), F32),
        ],
        compiler_params=pltpu.CompilerParams(vmem_limit_bytes=26 * MIB),
        cost_estimate=cost(8 * pairs * LANES, 4 * peers * rows * LANES, pairs),
        name="score",
    )(begins, ends, logs, positive, *blocks)


def back_top_kernel(
    where_ref,
    d_ref,
    proj_ref,
    unit_ref,
    scale_ref,
    low_ref,
    embed_ref,
    vec_ref,
    mid_ref,
    down_ref,
    own_ref,
    other_ref,
    sum_ref,
    acc,
):
    step = pl.program_id(0)

    @pl.when(step == 0)
    def _():
        acc[...] = jnp.zeros_like(acc)
        sum_ref[...] = jnp.zeros_like(sum_ref)

    projected = proj_ref[...]
    given = d_ref[...]
    size = lax.rsqrt(jnp.sum(projected * projected, -1, keepdims=True) + UNIT_EPS)
    along = jnp.sum(given * projected, -1, keepdims=True)
    d_proj = (size * given - projected * (size * size * size * along)).astype(BF)
    acc[...] += mm_tn(low_ref[...], d_proj)
    d_out = mm_nt(d_proj, embed_ref[...])
    unit = unit_ref[...]
    d_mid = normalize_back(d_out, vec_ref[2:3, :], unit, scale_ref[...])
    mid_ref[...] = d_mid
    low = d_mid.astype(BF)
    down_ref[...] = low
    sum_ref[0:1, :] += jnp.sum(d_out * unit, 0, keepdims=True)
    sum_ref[1:2, :] += jnp.sum(d_out, 0, keepdims=True)
    sum_ref[2:3, :] += jnp.sum(low.astype(F32), 0, keepdims=True)

    @pl.when(step == pl.num_programs(0) - 1)
    def _():
        put_rows(where_ref, own_ref, other_ref, acc[...])


def back_top(where, d_unit, projected, unit_two, scale_two, low_two, w_embed, vectors):
    rows, width = unit_two.shape
    owned = width // PIECES // 2

    def tile(columns):
        return pl.BlockSpec((TILE, columns), lambda i, w: (i, 0))

    return pl.pallas_call(
        back_top_kernel,
        grid_spec=pltpu.PrefetchScalarGridSpec(
            num_scalar_prefetch=1,
            grid=(rows // TILE,),
            in_specs=[
                tile(LANES),
                tile(LANES),
                tile(width),
                tile(1),
                tile(width),
                full((width, LANES)),
                full((16, width)),
            ],
            out_specs=[
                tile(width),
                tile(width),
                full((PIECES, owned, LANES)),
                full((PIECES, owned, LANES)),
                full((8, width)),
            ],
            scratch_shapes=[pltpu.VMEM((width, LANES), F32)],
        ),
        out_shape=[
            shape_of((rows, width), F32),
            shape_of((rows, width), BF),
            shape_of((PIECES, owned, LANES), BF),
            shape_of((PIECES, owned, LANES), BF),
            shape_of((8, width), F32),
        ],
        compiler_params=params(16),
        cost_estimate=cost(4 * rows * width * LANES, rows * width * 12),
        name="back_top",
    )(where, d_unit, projected, unit_two, scale_two, low_two, w_embed, vectors)


def back_down_kernel(
    where_ref, d_ref, down_ref, slope_ref, active_ref, up_ref, own_ref, other_ref, sum_ref
):
    given = d_ref[...]
    low = (mm_nt(given, down_ref[...]) * slope_ref[...].astype(F32)).astype(BF)
    up_ref[...] = low
    sum_ref[0:1, :] = jnp.sum(low.astype(F32), 0, keepdims=True)
    put_rows(where_ref, own_ref, other_ref, mm_tn(active_ref[...], given))


def back_down(where, d_down, w_down, slope, active):
    rows, width = d_down.shape
    wide = w_down.shape[0]
    steps = wide // width
    parts = PIECES // steps
    owned = wide // PIECES // 2
    column = pl.BlockSpec((rows, width), lambda t, w: (0, t))
    grad_block = pl.BlockSpec(
        (parts, owned, width), lambda t, w: (lax.bitwise_xor(t, w[0] // parts), 0, 0)
    )
    return pl.pallas_call(
        back_down_kernel,
        grid_spec=pltpu.PrefetchScalarGridSpec(
            num_scalar_prefetch=1,
            grid=(steps,),
            in_specs=[
                full((rows, width)),
                pl.BlockSpec((width, width), lambda t, w: (t, 0)),
                column,
                column,
            ],
            out_specs=[
                column,
                grad_block,
                grad_block,
                pl.BlockSpec((8, width), lambda t, w: (0, t)),
            ],
        ),
        out_shape=[
            near_shape((rows, wide), BF),
            shape_of((PIECES, owned, width), BF),
            shape_of((PIECES, owned, width), BF),
            shape_of((8, wide), F32),
        ],
        compiler_params=params(24),
        cost_estimate=cost(4 * rows * width * wide, 6 * rows * wide + 4 * wide * width),
        name="back_down",
    )(where, d_down, far(w_down), far(slope), far(active))


def back_up_kernel(where_ref, mid_ref, low_ref, d_ref, up_ref, out_ref, own_ref, other_ref, turned):
    @pl.when(pl.program_id(0) == 0)
    def _():
        out_ref[...] = mid_ref[...]
        turned[...] = low_ref[...].T

    given = d_ref[...]
    out_ref[...] += mm_nt(given, up_ref[...])
    put_rows(where_ref, own_ref, other_ref, mm(turned[...], given))


def back_up(where, d_mid, low_one, d_up, w_up):
    rows, width = d_mid.shape
    wide = w_up.shape[1]
    owned = width // PIECES // 2
    return pl.pallas_call(
        back_up_kernel,
        grid_spec=pltpu.PrefetchScalarGridSpec(
            num_scalar_prefetch=1,
            grid=(wide // width,),
            in_specs=[
                full((rows, width)),
                full((rows, width)),
                pl.BlockSpec((rows, width), lambda t, w: (0, t)),
                pl.BlockSpec((width, width), lambda t, w: (0, t)),
            ],
            out_specs=[
                full((rows, width)),
                pl.BlockSpec((PIECES, owned, width), lambda t, w: (0, 0, t)),
                pl.BlockSpec((PIECES, owned, width), lambda t, w: (0, 0, t)),
            ],
            scratch_shapes=[pltpu.VMEM((width, rows), BF)],
        ),
        out_shape=[
            shape_of((rows, width), F32),
            shape_of((PIECES, owned, wide), BF),
            shape_of((PIECES, owned, wide), BF),
        ],
        compiler_params=params(28),
        cost_estimate=cost(4 * rows * width * wide, 2 * rows * wide + 4 * wide * width),
        name="back_up",
    )(where, d_mid, far(low_one), near(d_up), far(w_up))


def back_out_kernel(
    where_ref,
    d_ref,
    unit_ref,
    scale_ref,
    first_ref,
    second_ref,
    out_ref,
    vec_ref,
    resid_ref,
    d_context_ref,
    own_ref,
    other_ref,
    sum_ref,
    acc,
):
    step = pl.program_id(0)

    @pl.when(step == 0)
    def _():
        acc[...] = jnp.zeros_like(acc)
        sum_ref[...] = jnp.zeros_like(sum_ref)

    d_out = d_ref[...]
    unit = unit_ref[...]
    d_resid = normalize_back(d_out, vec_ref[0:1, :], unit, scale_ref[...])
    resid_ref[...] = d_resid
    low = d_resid.astype(BF)
    d_context_ref[...] = mm_nt(low, out_ref[...]).astype(BF)
    cut = first_ref.shape[1]
    acc[:cut, :] += mm_tn(first_ref[...], low)
    acc[cut:, :] += mm_tn(second_ref[...], low)
    sum_ref[0:1, :] += jnp.sum(d_out * unit, 0, keepdims=True)
    sum_ref[1:2, :] += jnp.sum(d_out, 0, keepdims=True)
    sum_ref[2:3, :] += jnp.sum(low.astype(F32), 0, keepdims=True)

    @pl.when(step == pl.num_programs(0) - 1)
    def _():
        put_rows(where_ref, own_ref, other_ref, acc[...])


def back_out(where, d_one, unit_one, scale_one, contexts, w_out, vectors):
    rows, width = d_one.shape
    owned = width // PIECES // 2

    def tile(columns):
        return pl.BlockSpec((TILE, columns), lambda i, w: (i, 0))

    return pl.pallas_call(
        back_out_kernel,
        grid_spec=pltpu.PrefetchScalarGridSpec(
            num_scalar_prefetch=1,
            grid=(rows // TILE,),
            in_specs=[
                tile(width),
                tile(width),
                tile(1),
                *[tile(part.shape[1]) for part in contexts],
                full((width, width)),
                full((16, width)),
            ],
            out_specs=[
                tile(width),
                tile(width),
                full((PIECES, owned, width)),
                full((PIECES, owned, width)),
                full((8, width)),
            ],
            scratch_shapes=[pltpu.VMEM((width, width), F32)],
        ),
        out_shape=[
            shape_of((rows, width), F32),
            shape_of((rows, width), BF),
            shape_of((PIECES, owned, width), BF),
            shape_of((PIECES, owned, width), BF),
            shape_of((8, width), F32),
        ],
        compiler_params=params(20),
        cost_estimate=cost(4 * rows * width * width, rows * width * 16),
        name="back_out",
    )(where, d_one, unit_one, scale_one, *contexts, far(w_out), vectors)


def back_in_kernel(resid_ref, *refs):
    *parts, in_ref, out_ref = refs
    total = resid_ref[...]
    column = 0
    for part in parts:
        count = part.shape[1]
        total = total + mm_nt(part[...], in_ref[:, column : column + count])
        column += count
    out_ref[...] = total


def back_in(d_resid, parts, w_in):
    rows, width = d_resid.shape

    def tile(columns):
        return pl.BlockSpec((TILE, columns), lambda i: (i, 0))

    return pl.pallas_call(
        back_in_kernel,
        grid=(rows // TILE,),
        in_specs=[tile(width)] + [tile(p.shape[1]) for p in parts] + [full(w_in.shape)],
        out_specs=tile(width),
        out_shape=shape_of((rows, width), F32),
        compiler_params=params(24),
        cost_estimate=cost(6 * rows * width * width, rows * width * 14),
        name="back_in",
    )(d_resid, *parts, far(w_in))


def finish_kernel(steps, *refs):
    places = len(steps)
    pair_ref, *refs = refs
    totals, refs = refs[: len(refs) - 6 * places], refs[len(refs) - 6 * places :]
    weights, firsts, seconds = refs[:places], refs[places : 2 * places], refs[2 * places : 3 * places]
    outs = refs[3 * places :]
    norm = jnp.sqrt(pair_ref[1:2, 0:1])
    factor = CLIP_NORM / jnp.maximum(norm, CLIP_NORM)
    fix_one = 1.0 / (1.0 - BETA_ONE**STEP)
    fix_two = 1.0 / (1.0 - BETA_TWO**STEP)
    for item, (rate, decay, pieces) in enumerate(steps):
        for source, begin, width, target in pieces:
            grad = totals[source][:, begin : begin + width] * factor
            columns = slice(target, target + width)
            weight = weights[item][:, columns]
            first = BETA_ONE * firsts[item][:, columns] + (1.0 - BETA_ONE) * grad
            second = BETA_TWO * seconds[item][:, columns] + (1.0 - BETA_TWO) * grad * grad
            update = first * fix_one / (jnp.sqrt(second * fix_two) + ADAM_EPS)
            outs[item][:, columns] = first
            outs[places + item][:, columns] = second
            outs[2 * places + item][:, columns] = weight - rate * (update + decay * weight)


def finish(steps, pair, totals, masters, firsts, seconds):
    vmem = pl.BlockSpec(memory_space=pltpu.VMEM)
    held = [*masters, *firsts, *seconds]
    return pl.pallas_call(
        functools.partial(finish_kernel, steps),
        in_specs=[vmem] * (1 + len(totals) + len(held)),
        out_specs=[vmem] * len(held),
        out_shape=[shape_of(block.shape, F32) for block in held],
        compiler_params=pltpu.CompilerParams(vmem_limit_bytes=32 * MIB),
        name="finish",
    )(pair, *totals, *held)


def swap(block, bits):
    count = lax.axis_size(AXES)
    return lax.ppermute(block, AXES, [(d, d ^ bits) for d in range(count)])


def phase(*blocks):
    return lax.optimization_barrier(blocks)


def cut_of(width):
    return (width // LANES + 1) // 2 * LANES


def gather_near(keep, give, core):
    theirs = swap(give, 1)
    ours = [jnp.where(core == 0, keep, theirs), jnp.where(core == 0, theirs, keep)]
    return jnp.concatenate(ours, 0)


def gather_far(mine):
    return jnp.stack([mine] + [swap(mine, 8 * step) for step in (1, 2, 3)])


def gather_cross(far):
    cut = cut_of(far.shape[-1])
    left, right = far[:, :, :cut], far[:, :, cut:]
    return jnp.stack([left, swap(left, 2)], 1), jnp.stack([right, swap(right, 4)], 1)


def gather_last(pair):
    left, right = pair
    left = jnp.stack([left, swap(left, 4)], 1)
    right = jnp.stack([right, swap(right, 2)], 2)
    own = jnp.concatenate([left, right], -1)
    return own.reshape(PIECES, *own.shape[3:])


def gather_plain(keep, give):
    whole = [lax.all_gather(half, AXES, axis=0, tiled=True) for half in (keep, give)]
    return [half.reshape(PIECES, -1, half.shape[1]) for half in whole]


def added(mine, theirs):
    return (mine.astype(F32) + theirs.astype(F32)).astype(BF)


def scatter_near(own, other):
    _, rows, width = own.shape
    return added(own, swap(other, 1)).reshape(4, 2, 2, rows, width)


def scatter_cross(near):
    cut = cut_of(near.shape[-1])
    left, right = near[..., :cut], near[..., cut:]
    return added(left[:, :, 0], swap(left[:, :, 1], 2)), added(right[:, 0], swap(right[:, 1], 4))


def scatter_last(pair):
    left, right = pair
    left = added(left[:, 0], swap(left[:, 1], 4))
    right = added(right[:, 0], swap(right[:, 1], 2))
    return jnp.concatenate([left, right], -1)


def scatter_far(far):
    total = far[0].astype(F32)
    for step in (1, 2, 3):
        total = total + swap(far[step], 8 * step).astype(F32)
    return total


def scatter_plain(pair):
    pieces, rows, width = pair[0].shape
    whole = jnp.stack(pair, 1).reshape(2 * pieces * rows, width)
    return lax.psum_scatter(whole, AXES, scatter_dimension=0, tiled=True).astype(F32)


def keep_pair(own, other):
    return own, other


def same(blocks):
    return blocks


def sum_everywhere(values):
    count = lax.axis_size(AXES)
    bit = 1
    while bit < count:
        values = values + swap(values, bit)
        bit *= 2
    return values


def gather_peers(block):
    held = [block[None]]
    bit = 1
    sizes = []
    while bit < lax.axis_size("psg"):
        sizes.append(bit)
        bit *= 2
    for bit in reversed(sizes):
        now = jnp.concatenate(held, 0) if len(held) > 1 else held[0]
        held = [now, swap(now, bit)]
        if bit > 1:
            held = [jnp.concatenate(held, 0)]
    return held


def peer_order(count):
    order, bit = [0], count // 2
    while bit > 0:
        order = order + [peer ^ bit for peer in order]
        bit //= 2
    return order


def local(hidden, lengths_in, positive, *shards):
    masters, firsts, seconds = shards[:6], shards[6:12], shards[12:]
    psg_count = lax.axis_size("psg")
    count = lax.axis_size(AXES)
    split = count == 2 * PIECES
    mine = lax.axis_index("psg")
    rows, width = hidden.shape
    wide = masters[2].shape[1]
    pairs = width // LANES
    queries = positive.shape[0]
    query_rows = queries * QLEN
    query_total = queries * count
    slots = lengths_in.shape[1]
    pack_rows = rows - query_rows
    index = lax.axis_index(AXES)
    if split:
        where = jnp.stack([index // 2, index % 2]).astype(jnp.int32)
    else:
        where = jnp.zeros((2,), jnp.int32)
    core = where[1]

    front_keep, front_give, rest_keep, rest_give, down_low = pack(
        where, masters[0], masters[1], masters[2], masters[4], masters[5], masters[3]
    )
    w_down = lax.all_gather(down_low, AXES, axis=0, tiled=True)
    facts = jnp.concatenate([lengths_in[0], positive])[None]
    if split:
        beside = gather_near(front_keep, front_give, core)
        column = gather_far(beside)
        column, rest_keep, rest_give = phase(column, rest_keep, rest_give)
        crossed = gather_cross(column)
        near_rest = gather_near(rest_keep, rest_give, core)
        shifted = swap(near_rest, 8)
        crossed, near_rest, shifted, facts = phase(crossed, near_rest, shifted, facts)
        own = gather_last(crossed)
        shifted = [near_rest, shifted] + [swap(near_rest, 8 * step) for step in (2, 3)]
        own, shifted[:3] = phase(own, shifted[:3])
        front = (own, swap(own, 1))
        front, shifted = phase(front, shifted)
        far_rest = jnp.stack(shifted)
    else:
        front = gather_plain(front_keep, front_give)
        rest = gather_plain(rest_keep, rest_give)

    facts = jnp.concatenate(gather_peers(facts), 0).reshape(psg_count, -1)
    lengths, chosen = facts[:, :slots], facts[:, slots:]
    ends = jnp.cumsum(lengths, 1)
    lane_slot = jnp.eye(psg_count, dtype=jnp.int32)[:, :, None]
    unused = LANES - psg_count * slots

    def by_lane(values):
        spread = (lane_slot * values[:, None, :]).reshape(psg_count, psg_count * slots)
        return jnp.pad(spread, ((0, 0), (0, unused)))

    end_lanes = by_lane(ends)
    begin_lanes = by_lane(ends - lengths)
    log_lanes = jnp.pad(jnp.log(lengths.astype(F32)).reshape(1, -1), ((0, 0), (0, unused)))
    place_of = [peer_order(psg_count).index(peer) for peer in range(psg_count)]
    theirs = jnp.bitwise_xor(chosen // slots, mine)
    places = sum(jnp.where(theirs == peer, place, 0) for peer, place in enumerate(place_of))
    chosen = (places * slots + chosen % slots)[:, :, None]
    places = jnp.arange(pack_rows, dtype=jnp.int32)
    segment = jnp.sum((places[:, None] >= ends[0][None, :]).astype(jnp.int32), -1)
    seg_col, seg_row = segment[:, None], segment[None, :]

    merged, turned, w_in, w_embed, vectors = project(where, hidden, *front)
    if split:
        crossed_rest = gather_cross(far_rest)
        merged, turned, crossed_rest = phase(merged, turned, crossed_rest)
    contexts = [attend(merged, seg_col, seg_row, query_rows, 0, pairs // 2)]
    if split:
        own = gather_last(crossed_rest)
        merged, own, contexts = phase(merged, own, contexts)
    contexts.append(attend(merged, seg_col, seg_row, query_rows, pairs // 2, pairs - pairs // 2))
    if split:
        rest = (own, swap(own, 1))
    unit_one, scale_one, low_one, active, slope, unit_two, scale_two, low_two, *held = encode(
        where, contexts, hidden, vectors, w_embed, w_down, *rest
    )
    projected, embedded, w_up, w_out = held
    loss_block, d_unit = score(
        gather_peers(embedded), begin_lanes, end_lanes, log_lanes, chosen, query_rows, query_total, slots
    )
    d_mid, d_down, *grad_embed, sums_top = back_top(
        where, d_unit, projected, unit_two, scale_two, low_two, w_embed, vectors
    )
    d_up, *grad_down, sums_up = back_down(where, d_down, w_down, slope, active)
    steps = (scatter_near, scatter_cross, scatter_last, scatter_far)
    closest, cross, last, final = steps if split else (keep_pair, same, same, scatter_plain)

    d_one, *grad_up = back_up(where, d_mid, low_one, d_up, w_up)
    downs = closest(*grad_down)
    here, d_one, grad_up, downs = phase(where, d_one, grad_up, downs)
    d_resid, d_context, *grad_out, sums_out = back_out(
        here, d_one, unit_one, scale_one, contexts, w_out, vectors
    )

    def back(held, *rest):
        *d_part, own, other, sums = attend_back(
            held, merged, d_context, turned, seg_col, seg_row, query_rows, *rest
        )
        return d_part, (own, other), sums

    third = pairs // 3
    downs, ups = cross(downs), closest(*grad_up)
    here, d_context, grad_out, downs, ups = phase(where, d_context, grad_out, downs, ups)
    part_one, ones, sums_one = back(here, 0, third, "copied", grad_out)
    downs, ups = last(downs), cross(ups)
    here, part_one, ones, downs, ups = phase(where, part_one, ones, downs, ups)
    part_two, twos, sums_two = back(here, third, third)
    total_down, ups, ones = final(downs), last(ups), closest(*ones)
    here, part_two, twos, total_down, ups, ones = phase(where, part_two, twos, total_down, ups, ones)
    part_three, threes, sums_three = back(
        here,
        2 * third,
        pairs - 2 * third,
        "vectors",
        (*grad_embed, sums_out, sums_top, sums_up, sums_one, sums_two),
    )
    total_up, ones, twos = final(ups), cross(ones), closest(*twos)
    part_three, threes, total_up, ones, twos = phase(part_three, threes, total_up, ones, twos)
    ones, threes = last(ones), closest(*threes)
    ones, threes = phase(ones, threes)
    parts = (part_one, part_two, part_three)
    ordered = [part[which] for which in (0, 1, 2) for part in parts]
    if split:
        twos = cross(jnp.concatenate([twos, threes], -1))
        input_grad = back_in(d_resid, ordered, w_in)
        input_grad, twos = phase(input_grad, twos)
        total_two = final(last(twos))
    else:
        input_grad = back_in(d_resid, ordered, w_in)
        total_two = final([jnp.concatenate([two, three], -1) for two, three in zip(twos, threes)])
    total_one = final(ones)

    totals = [total_down, total_up, total_one, total_two]
    squares = sum(jnp.sum(total * total) for total in totals)
    pair = jnp.stack([loss_block[0, 0], squares])
    pair = sum_everywhere(jnp.broadcast_to(pair[:, None], (2, LANES)))
    loss = pair[0, 0] / query_total
    grad_norm = jnp.sqrt(pair[1, 0])

    block = 3 * LANES
    inward_pieces = []
    for head_pair in range(pairs):
        source = 2 if head_pair < third else 3
        begin = (head_pair if head_pair < third else head_pair - third) * block
        for part in (0, 1, 2):
            target = part * width + head_pair * LANES
            inward_pieces.append((source, begin + part * LANES, LANES, target))
    first_end = third * block
    last_end = (pairs - third) * block
    vector_count = masters[5].shape[1]
    plans = (
        (RATE_MATRIX, DECAY, tuple(inward_pieces)),
        (RATE_MATRIX, DECAY, ((2, first_end, width, 0),)),
        (RATE_MATRIX, DECAY, ((1, 0, wide, 0),)),
        (RATE_MATRIX, DECAY, ((0, 0, width, 0),)),
        (RATE_MATRIX, DECAY, ((3, last_end + LANES, LANES, 0),)),
        (RATE_VECTOR, 0.0, ((3, last_end, vector_count, 0),)),
    )
    stepped = finish(plans, pair, totals, masters, firsts, seconds)
    return (loss, input_grad, grad_norm) + tuple(stepped)


def solution(mesh):
    by_rows = P(AXES, None)
    placed = (by_rows, by_rows, P(AXES)) + (by_rows,) * 18
    return jax.shard_map(
        local,
        mesh=mesh,
        in_specs=placed,
        out_specs=(P(), by_rows, P()) + (by_rows,) * 18,
        check_vma=False,
    )
```

```python
import functools

import jax
import jax.numpy as jnp
from jax import lax
from jax.experimental import pallas as pl
from jax.experimental.pallas import tpu as pltpu
from jax.sharding import PartitionSpec as P

HEADS = 12
HEAD = 64
QLEN = 32
STEP = 10

TAU_INV = 10.0
SCORE_SCALE = 10.0
CLIP_NORM = 0.02
BETA_ONE = 0.9
BETA_TWO = 0.999
ADAM_EPS = 1e-08
RATE_MATRIX = 0.05
RATE_VECTOR = 0.5
DECAY = 0.01
NORM_EPS = 1e-12
UNIT_EPS = 1e-06

AXES = ("group", "psg")
LANES = 128
PIECES = 16
TILE = 256
MIB = 2**20
BF = jnp.bfloat16
F32 = jnp.float32


def mm(left, right):
    return lax.dot_general(left, right, (((1,), (0,)), ((), ())), preferred_element_type=F32)


def mm_nt(left, right):
    return lax.dot_general(left, right, (((1,), (1,)), ((), ())), preferred_element_type=F32)


def mm_tn(left, right):
    return lax.dot_general(left, right, (((0,), (0,)), ((), ())), preferred_element_type=F32)


def full(shape):
    return pl.BlockSpec(shape, lambda *_: (0,) * len(shape))


def params(mib=56):
    return pltpu.CompilerParams(
        vmem_limit_bytes=mib * MIB, dimension_semantics=("arbitrary",)
    )


def cost(flops, moved, special=0):
    return pl.CostEstimate(flops=int(flops), bytes_accessed=int(moved), transcendentals=int(special))


def shape_of(shape, dtype):
    return jax.ShapeDtypeStruct(shape, dtype)


def far_shape(shape, dtype):
    return pltpu.HBM(shape, dtype)


def far(*blocks):
    held = [pltpu.with_memory_space_constraint(block, pltpu.HBM) for block in blocks]
    return held if len(held) > 1 else held[0]


def near_shape(shape, dtype):
    return pltpu.VMEM(shape, dtype)


def near(*blocks):
    held = [pltpu.with_memory_space_constraint(block, pltpu.VMEM) for block in blocks]
    return held if len(held) > 1 else held[0]


def any_space():
    return pl.BlockSpec(memory_space=pl.ANY)


def fetch_pieces(where_ref, own_ref, other_ref, moves, sems):
    chip, core = where_ref[0], where_ref[1]
    rows = own_ref.shape[1]

    def start(halves):
        for piece in range(own_ref.shape[0]):
            source = lax.bitwise_xor(chip, piece)
            for number, (half, first, width, target, column) in enumerate(moves):
                pltpu.make_async_copy(
                    halves[half].at[source, :, pl.ds(first, width)],
                    target.at[pl.ds(rows * piece, rows), pl.ds(column, width)],
                    sems.at[number],
                ).start()

    pl.when(core == 0)(lambda: start((own_ref, other_ref)))
    pl.when(core == 1)(lambda: start((other_ref, own_ref)))
    for number, (_, _, width, target, column) in enumerate(moves):
        landed = target.at[:, pl.ds(column, width)]
        pltpu.make_async_copy(landed, landed, sems.at[number]).wait()


def pack_kernel(where_ref, in_ref, out_ref, up_ref, embed_ref, turned_ref, down_ref, *targets):
    front_keep, front_give, rest_keep, rest_give, down_low = targets
    half_in, half_out, half_up = (ref.shape[1] // 2 for ref in (in_ref, out_ref, up_ref))
    owned = in_ref.shape[0]
    down_low[...] = down_ref[...].astype(BF)

    def fill(front, rest, half):
        front[:, :half_in] = in_ref[:, half * half_in : (half + 1) * half_in].astype(BF)
        if half == 0:
            front[:, half_in:] = embed_ref[...].astype(BF)
        else:
            empty = jnp.zeros((LANES - turned_ref.shape[0], owned), F32)
            front[:, half_in:] = jnp.concatenate([turned_ref[...], empty], 0).T.astype(BF)
        rest[:, :half_up] = up_ref[:, half * half_up : (half + 1) * half_up].astype(BF)
        rest[:, half_up:] = out_ref[:, half * half_out : (half + 1) * half_out].astype(BF)

    @pl.when(where_ref[1] == 0)
    def _():
        fill(front_keep, rest_keep, 0)
        fill(front_give, rest_give, 1)

    @pl.when(where_ref[1] == 1)
    def _():
        fill(front_keep, rest_keep, 1)
        fill(front_give, rest_give, 0)


def pack(where, inward, outward, upward, embed, vectors, downward):
    owned, width = outward.shape
    front = 3 * width // 2 + LANES
    rest = upward.shape[1] // 2 + width // 2
    vmem = pl.BlockSpec(memory_space=pltpu.VMEM)
    return pl.pallas_call(
        pack_kernel,
        in_specs=[pl.BlockSpec(memory_space=pltpu.SMEM)] + [vmem] * 6,
        out_specs=[vmem] * 5,
        out_shape=[
            shape_of((owned, front), BF),
            shape_of((owned, front), BF),
            shape_of((owned, rest), BF),
            shape_of((owned, rest), BF),
            shape_of(downward.shape, BF),
        ],
        compiler_params=pltpu.CompilerParams(vmem_limit_bytes=16 * MIB),
        name="pack",
    )(where, *far(inward, outward, upward, embed, vectors, downward))


def project_kernel(
    where_ref, rows_ref, own_ref, other_ref, merged_ref, turned_ref, in_ref, embed_ref, vec_ref, raw, sems
):
    width = rows_ref.shape[1]
    half_in = 3 * width // 2

    @pl.when(pl.program_id(0) == 0)
    def _():
        moves = [(half, 0, half_in, in_ref, half * half_in) for half in (0, 1)]
        moves.append((0, half_in, LANES, embed_ref, 0))
        moves.append((1, half_in, LANES, raw, 0))
        fetch_pieces(where_ref, own_ref, other_ref, moves, sems)
        vec_ref[...] = raw[...].astype(F32).T[: vec_ref.shape[0]]

    rows = rows_ref[...]
    turned_ref[...] = rows.T
    for part, bias in ((0, 4), (1, None), (2, 5)):
        block = mm(rows, in_ref[:, part * width : (part + 1) * width])
        if bias is not None:
            block = block + vec_ref[bias : bias + 1, :]
        merged_ref[:, part * width : (part + 1) * width] = block.astype(BF)


def project(where, hidden, own, other):
    rows, width = hidden.shape
    return pl.pallas_call(
        project_kernel,
        grid_spec=pltpu.PrefetchScalarGridSpec(
            num_scalar_prefetch=1,
            grid=(rows // TILE,),
            in_specs=[pl.BlockSpec((TILE, width), lambda i, w: (i, 0)), any_space(), any_space()],
            out_specs=[
                pl.BlockSpec((TILE, 3 * width), lambda i, w: (i, 0)),
                pl.BlockSpec((width, TILE), lambda i, w: (0, i)),
                full((width, 3 * width)),
                full((width, LANES)),
                full((16, width)),
            ],
            scratch_shapes=[pltpu.VMEM((width, LANES), BF), pltpu.SemaphoreType.DMA((4,))],
        ),
        out_shape=[
            far_shape((rows, 3 * width), BF),
            far_shape((width, rows), BF),
            far_shape((width, 3 * width), BF),
            shape_of((width, LANES), BF),
            shape_of((16, width), F32),
        ],
        compiler_params=params(20),
        cost_estimate=cost(6 * rows * width * width, 8 * rows * width + 16 * width * width),
        name="project",
    )(where, far(hidden), own, other)


def head_masks():
    lane = lax.broadcasted_iota(jnp.int32, (1, LANES), 1)
    return [(lane < HEAD).astype(BF), (lane >= HEAD).astype(BF)]


def softmax_rows(scores):
    peak = jnp.max(scores, -1, keepdims=True)
    expo = jnp.exp(scores - peak)
    return expo * (1.0 / jnp.sum(expo, -1, keepdims=True))


QUERY_TILE = 256
PACK_TILE = 384


def blocks_of(rows, query_rows):
    size = QUERY_TILE
    listed = [(first, size, first, size, True) for first in range(0, query_rows, size)]
    for first in range(query_rows, rows, PACK_TILE):
        listed.append((first, PACK_TILE, query_rows, rows - query_rows, False))
    return listed


def allowed_pairs(block, seg_col, seg_row, query_rows):
    first, count, _, keys, is_query = block
    if is_query:
        mine = lax.broadcasted_iota(jnp.int32, (count, keys), 0) // QLEN
        theirs = lax.broadcasted_iota(jnp.int32, (count, keys), 1) // QLEN
        return mine == theirs
    begin = first - query_rows
    return seg_col[begin : begin + count, :] == seg_row[0:1, :]


def attend_kernel(query_rows, seg_col, seg_row, q_ref, k_ref, v_ref, out_ref):
    masks = head_masks()
    blocks = blocks_of(q_ref.shape[0], query_rows)

    def products(block):
        first, count, begin, keys, _ = block
        query = q_ref[first : first + count, :]
        key = k_ref[begin : begin + keys, :]
        return [mm_nt(query * (mask * HEAD**-0.5), key) for mask in masks]

    ahead = products(blocks[0])
    for place, block in enumerate(blocks):
        first, count, begin, keys, _ = block
        scores = ahead
        if place + 1 < len(blocks):
            ahead = products(blocks[place + 1])
        allowed = allowed_pairs(block, seg_col, seg_row, query_rows)
        value = v_ref[begin : begin + keys, :]
        total = None
        for mask, score in zip(masks, scores):
            weights = softmax_rows(jnp.where(allowed, score, -1e9)).astype(BF)
            part = mm(weights, value * mask)
            total = part if total is None else total + part
        out_ref[first : first + count, :] = total.astype(BF)


def attend(merged, seg_col, seg_row, query_rows, first_pair, count):
    rows, wide = merged.shape
    pairs = wide // 3 // LANES
    pack = rows - query_rows

    def column(part):
        return pl.BlockSpec((rows, LANES), lambda h: (0, part * pairs + first_pair + h))

    return pl.pallas_call(
        functools.partial(attend_kernel, query_rows),
        grid=(count,),
        in_specs=[full((pack, 1)), full((1, pack)), column(0), column(1), column(2)],
        out_specs=pl.BlockSpec((rows, LANES), lambda h: (0, h)),
        out_shape=shape_of((rows, count * LANES), BF),
        compiler_params=params(16),
        cost_estimate=cost(
            16 * count * pack * pack * LANES, 8 * rows * count * LANES, 2 * count * pack * pack
        ),
        name="attend",
    )(seg_col, seg_row, *far(merged, merged, merged))


def put_rows(where_ref, own_ref, other_ref, values):
    pieces, rows = own_ref.shape[0], own_ref.shape[1]
    chip = lax.bitwise_and(where_ref[0], pieces - 1)

    def store(targets):
        for piece in range(pieces):
            for half in (0, 1):
                begin = (2 * piece + half) * rows
                targets[half][lax.bitwise_xor(chip, piece)] = values[begin : begin + rows, :].astype(BF)

    pl.when(where_ref[1] == 0)(lambda: store((own_ref, other_ref)))
    pl.when(where_ref[1] == 1)(lambda: store((other_ref, own_ref)))


def attend_back_pair(query_rows, seg_col, seg_row, q_ref, k_ref, v_ref, d_ref, dq_ref, dk_ref, dv_ref, acc_k, acc_v):
    masks = head_masks()
    rows = q_ref.shape[0]
    blocks = blocks_of(rows, query_rows)

    def products(block):
        first, count, begin, keys, _ = block
        query = q_ref[first : first + count, :]
        given = d_ref[first : first + count, :]
        key = k_ref[begin : begin + keys, :]
        value = v_ref[begin : begin + keys, :]
        made = []
        for mask in masks:
            scaled = query * (mask * HEAD**-0.5)
            own = given * mask
            made.append((scaled, own, mm_nt(scaled, key), mm_nt(own, value)))
        return made

    ahead = products(blocks[0])
    started = False
    for place, block in enumerate(blocks):
        first, count, begin, keys, is_query = block
        held = ahead
        if place + 1 < len(blocks):
            ahead = products(blocks[place + 1])
        allowed = allowed_pairs(block, seg_col, seg_row, query_rows)
        key = k_ref[begin : begin + keys, :]
        dq = dk = dv = 0.0
        for mask, (scaled, own, scores, d_weights) in zip(masks, held):
            weights = softmax_rows(jnp.where(allowed, scores, -1e9))
            inner = jnp.sum(d_weights * weights, -1, keepdims=True)
            d_scores = (weights * (d_weights - inner)).astype(BF)
            dq = dq + mm(d_scores, key * (mask * HEAD**-0.5))
            dk = dk + mm_tn(d_scores, scaled)
            dv = dv + mm_tn(weights.astype(BF), own)
        dq_ref[first : first + count, :] = dq.astype(BF)
        if is_query:
            dk_ref[begin : begin + keys, :] = dk.astype(BF)
            dv_ref[begin : begin + keys, :] = dv.astype(BF)
        elif started:
            acc_k[...] += dk
            acc_v[...] += dv
        else:
            acc_k[...] = dk
            acc_v[...] = dv
            started = True
    dk_ref[query_rows:, :] = acc_k[...].astype(BF)
    dv_ref[query_rows:, :] = acc_v[...].astype(BF)


def column_sums(block):
    return jnp.sum(block.astype(F32), 0, keepdims=True)


def attend_back_kernel(query_rows, count, extra, where_ref, *refs):
    seg_col, seg_row, q_ref, k_ref, v_ref, d_ref, turned_ref, *refs = refs
    passed, refs = refs[: len(refs) - 8], refs[len(refs) - 8 :]
    dq_ref, dk_ref, dv_ref, own_ref, other_ref, sum_ref, acc_k, acc_v = refs
    step = pl.program_id(0)

    @pl.when(step < count)
    def _():
        attend_back_pair(
            query_rows, seg_col, seg_row, q_ref, k_ref, v_ref, d_ref, dq_ref, dk_ref, dv_ref, acc_k, acc_v
        )
        turned = turned_ref[...]
        grads = [mm(turned, ref[...]) for ref in (dq_ref, dk_ref, dv_ref)]
        put_rows(where_ref, own_ref, other_ref, jnp.concatenate(grads, 1))
        empty = jnp.zeros((6, LANES), F32)
        sums = [column_sums(dq_ref[...]), column_sums(dv_ref[...]), empty]
        sum_ref[step] = jnp.concatenate(sums, 0)

    @pl.when(step >= count)
    def _():
        if extra == "copied":
            own_ref[...] = passed[0][...]
            other_ref[...] = passed[1][...]
        elif extra == "vectors":
            own_embed, other_embed, out_sums, top_sums, up_sums, *in_sums = passed
            width = out_sums.shape[1]
            blocks = [ref[place] for ref in in_sums for place in range(ref.shape[0])]
            both = jnp.concatenate(blocks + [sum_ref[place] for place in range(count)], 1)
            stacked = [out_sums[0:2, :], top_sums[0:2, :], both[0:2]]
            stacked += [out_sums[2:3, :], top_sums[2:3, :]]
            for part in range(up_sums.shape[1] // width):
                stacked.append(up_sums[0:1, part * width : (part + 1) * width])
            used = sum(block.shape[0] for block in stacked)
            stacked.append(jnp.zeros((LANES - used, width), F32))
            turned_sums = jnp.concatenate(stacked, 0).T
            empty = jnp.zeros((width, 2 * LANES), F32)
            put_rows(where_ref, own_ref, other_ref, jnp.concatenate([turned_sums, empty], 1))
            own_ref[:, :, LANES : 2 * LANES] = own_embed[...]
            other_ref[:, :, LANES : 2 * LANES] = other_embed[...]


def attend_back(
    where, merged, d_context, turned, seg_col, seg_row, query_rows, first_pair, count, extra=None, passed=()
):
    rows, wide = merged.shape
    width = wide // 3
    pairs = width // LANES
    pack = rows - query_rows
    owned = width // PIECES // 2
    block = 3 * LANES
    steps = count
    passed_specs = []
    if extra == "copied":
        steps = count + passed[0].shape[2] // block
        own = pl.BlockSpec((PIECES, owned, block), lambda h, w: (0, 0, jnp.maximum(h - count, 0)))
        passed_specs = [own, own]
    elif extra == "vectors":
        steps = count + 1
        passed_specs = [full(block_in.shape) for block_in in passed]

    def pair_of(step):
        return jnp.minimum(step, count - 1)

    def column(part):
        return pl.BlockSpec((rows, LANES), lambda h, w: (0, part * pairs + first_pair + pair_of(h)))

    own_column = pl.BlockSpec((rows, LANES), lambda h, w: (0, pair_of(h)))
    grad_block = pl.BlockSpec((PIECES, owned, block), lambda h, w: (0, 0, h))
    return pl.pallas_call(
        functools.partial(attend_back_kernel, query_rows, count, extra),
        grid_spec=pltpu.PrefetchScalarGridSpec(
            num_scalar_prefetch=1,
            grid=(steps,),
            in_specs=[
                full((pack, 1)),
                full((1, pack)),
                column(0),
                column(1),
                column(2),
                pl.BlockSpec((rows, LANES), lambda h, w: (0, first_pair + pair_of(h))),
                full((width, rows)),
                *passed_specs,
            ],
            out_specs=[
                own_column,
                own_column,
                own_column,
                grad_block,
                grad_block,
                full((count, 8, LANES)),
            ],
            scratch_shapes=[pltpu.VMEM((pack, LANES), F32), pltpu.VMEM((pack, LANES), F32)],
        ),
        out_shape=[
            shape_of((rows, count * LANES), BF),
            shape_of((rows, count * LANES), BF),
            shape_of((rows, count * LANES), BF),
            shape_of((PIECES, owned, steps * block), BF),
            shape_of((PIECES, owned, steps * block), BF),
            shape_of((count, 8, LANES), F32),
        ],
        compiler_params=params(24),
        cost_estimate=cost(
            count * (20 * pack * pack * LANES + 6 * rows * width * LANES),
            count * rows * LANES * 14,
            2 * count * pack * pack,
        ),
        name="attend_back",
    )(where, seg_col, seg_row, *far(merged, merged, merged), d_context, far(turned), *passed)


def normalize(residual):
    center = jnp.mean(residual, -1, keepdims=True)
    shifted = residual - center
    spread = jnp.mean(shifted * shifted, -1, keepdims=True)
    scale = lax.rsqrt(spread + NORM_EPS)
    return shifted * scale, scale


def normalize_back(d_out, gain, unit, scale):
    d_unit = d_out * gain
    return scale * (
        d_unit
        - jnp.mean(d_unit, -1, keepdims=True)
        - unit * jnp.mean(d_unit * unit, -1, keepdims=True)
    )


def gelu_parts(given):
    below = 0.5 + 0.5 * lax.erf(given * 0.5**0.5)
    bell = jnp.exp(-0.5 * given * given)
    return given * below, below + given * bell * 0.3989422804014327


def encode_kernel(
    where_ref,
    first_ref,
    second_ref,
    hidden_ref,
    vec_ref,
    embed_ref,
    down_ref,
    own_ref,
    other_ref,
    unit_ref,
    scale_ref,
    low_ref,
    active_ref,
    slope_ref,
    unit_two_ref,
    scale_two_ref,
    low_two_ref,
    proj_ref,
    row_ref,
    up_far,
    out_far,
    up_ref,
    out_ref,
    sems,
    sent,
):
    width = hidden_ref.shape[1]
    half, half_out = up_ref.shape[1] // 2, width // 2
    copies = [
        pltpu.make_async_copy(up_ref, up_far, sent.at[0]),
        pltpu.make_async_copy(out_ref, out_far, sent.at[1]),
    ]

    @pl.when(pl.program_id(0) == 0)
    def _():
        moves = []
        for side in (0, 1):
            moves.append((side, half, half_out, out_ref, side * half_out))
            moves.append((side, 0, half, up_ref, side * half))
        fetch_pieces(where_ref, own_ref, other_ref, moves, sems)
        for copy in copies:
            copy.start()

    cut = first_ref.shape[1]
    branch = mm(first_ref[...], out_ref[:cut, :]) + mm(second_ref[...], out_ref[cut:, :])
    unit, scale = normalize(hidden_ref[...].astype(F32) + (branch + vec_ref[6:7, :]))
    unit_ref[...] = unit
    scale_ref[...] = scale
    first = unit * vec_ref[0:1, :] + vec_ref[1:2, :]
    low = first.astype(BF)
    low_ref[...] = low
    parts = up_ref.shape[1] // width

    def raised_part(part):
        raised = mm(low, up_ref[:, part * width : (part + 1) * width])
        return raised + vec_ref[8 + part : 9 + part, :]

    ahead = raised_part(0)
    total = first + vec_ref[7:8, :]
    for part in range(parts):
        raised = ahead
        if part + 1 < parts:
            ahead = raised_part(part + 1)
        columns = slice(part * width, (part + 1) * width)
        value, slope = gelu_parts(raised)
        value = value.astype(BF)
        active_ref[:, columns] = value
        slope_ref[:, columns] = slope.astype(BF)
        total = total + mm(value, down_ref[columns, :])
    unit, scale = normalize(total)
    unit_two_ref[...] = unit
    scale_two_ref[...] = scale
    low = (unit * vec_ref[2:3, :] + vec_ref[3:4, :]).astype(BF)
    low_two_ref[...] = low
    projected = mm(low, embed_ref[...])
    proj_ref[...] = projected
    size = jnp.sum(projected * projected, -1, keepdims=True)
    row_ref[...] = (projected * lax.rsqrt(size + UNIT_EPS)).astype(BF)

    @pl.when(pl.program_id(0) == pl.num_programs(0) - 1)
    def _():
        for copy in copies:
            copy.wait()


def encode(where, contexts, hidden, vectors, w_embed, w_down, own, other):
    rows, width = hidden.shape
    wide = w_down.shape[0]

    def tile(columns):
        return pl.BlockSpec((TILE, columns), lambda i, w: (i, 0))

    return pl.pallas_call(
        encode_kernel,
        grid_spec=pltpu.PrefetchScalarGridSpec(
            num_scalar_prefetch=1,
            grid=(rows // TILE,),
            in_specs=[
                *[tile(part.shape[1]) for part in contexts],
                tile(width),
                full((16, width)),
                full((width, LANES)),
                full((wide, width)),
                any_space(),
                any_space(),
            ],
            out_specs=[
                tile(width),
                tile(1),
                tile(width),
                tile(wide),
                tile(wide),
                tile(width),
                tile(1),
                tile(width),
                tile(LANES),
                tile(LANES),
                any_space(),
                any_space(),
            ],
            scratch_shapes=[
                pltpu.VMEM((width, wide), BF),
                pltpu.VMEM((width, width), BF),
                pltpu.SemaphoreType.DMA((4,)),
                pltpu.SemaphoreType.DMA((2,)),
            ],
        ),
        out_shape=[
            far_shape((rows, width), F32),
            far_shape((rows, 1), F32),
            far_shape((rows, width), BF),
            far_shape((rows, wide), BF),
            far_shape((rows, wide), BF),
            far_shape((rows, width), F32),
            far_shape((rows, 1), F32),
            far_shape((rows, width), BF),
            far_shape((rows, LANES), F32),
            shape_of((rows, LANES), BF),
            far_shape((width, wide), BF),
            far_shape((width, width), BF),
        ],
        compiler_params=params(44),
        cost_estimate=cost(
            2 * rows * width * (width + 2 * wide), rows * (20 * width + 4 * wide), rows * wide
        ),
        name="encode",
    )(where, *contexts, far(hidden), vectors, w_embed, *far(w_down, own, other))


def split_two(values):
    high = values.astype(BF)
    return high, (values - high.astype(F32)).astype(BF)


def score_kernel(
    query_rows,
    query_total,
    slots,
    begin_ref,
    end_ref,
    log_ref,
    positive_ref,
    *refs,
):
    *block_refs, loss_ref, d_ref, rows_ref, expo, member, scaled = refs
    peers, rows, _ = rows_ref.shape
    place = 0
    for ref in block_refs:
        rows_ref[place : place + ref.shape[0]] = ref[...]
        place += ref.shape[0]
    pack = rows - query_rows
    half = query_rows // 2
    queries = half // QLEN
    place = lax.broadcasted_iota(jnp.int32, (pack, LANES), 0)
    lane = lax.broadcasted_iota(jnp.int32, (1, LANES), 1)
    for peer in range(peers):
        inside = (place >= begin_ref[peer : peer + 1, :]) & (place < end_ref[peer : peer + 1, :])
        member[peer] = inside.astype(F32).astype(BF)
    loss_ref[...] = jnp.zeros_like(loss_ref)

    def forward(step, carry):
        asker, part = step // 2, step % 2
        own_rows = pl.ds(pl.multiple_of(part * half, half), half)
        query = rows_ref[asker, own_rows, :]
        total = jnp.zeros((half, LANES), F32)
        peaks = jnp.zeros((half, LANES), F32)
        ahead = mm_nt(query, rows_ref[0, query_rows:, :])
        for peer in range(peers):
            similar = ahead
            if peer + 1 < peers:
                ahead = mm_nt(query, rows_ref[peer + 1, query_rows:, :])
            peak = jnp.max(similar, -1, keepdims=True)
            value = jnp.exp((similar - peak) * TAU_INV)
            if peer == 0:
                expo[asker, own_rows, :] = value
            else:

                @pl.when(asker == 0)
                def _():
                    expo[peers + peer, own_rows, :] = value

            high, low = split_two(value)
            total = total + (mm(high, member[peer]) + mm(low, member[peer]))
            peaks = jnp.where(lane // slots == peer, peak, peaks)
        used = lane < peers * slots
        total = jnp.where(used, total, 1.0)
        smooth = jnp.log(total) / TAU_INV + peaks - log_ref[...] / TAU_INV
        logits = SCORE_SCALE * jnp.sum(smooth.reshape(queries, QLEN, LANES), 1)
        logits = jnp.where(used, logits, -1e30)
        own_queries = pl.ds(pl.multiple_of(part * queries, queries), queries)
        picked = (positive_ref[asker, own_queries, :] == lane).astype(F32)
        high = jnp.max(logits, -1, keepdims=True)
        powers = jnp.where(used, jnp.exp(logits - high), 0.0)
        norm = jnp.sum(powers, -1, keepdims=True)
        each = high + jnp.log(norm) - jnp.sum(picked * logits, -1, keepdims=True)
        d_logits = (powers / norm - picked) / query_total
        spread = jnp.broadcast_to(
            (SCORE_SCALE * d_logits)[:, None, :], (queries, QLEN, LANES)
        ).reshape(half, LANES)
        exact = jnp.where(used, spread / total, 0.0)
        rounded = exact.astype(BF).astype(F32)
        rest = pltpu.roll(exact - rounded, LANES // 2, 1)
        scaled[asker, own_rows, :] = (rounded + rest).astype(BF)

        @pl.when(asker == 0)
        def _():
            loss_ref[...] += jnp.broadcast_to(jnp.sum(each), loss_ref.shape)

        return carry

    lax.fori_loop(0, 2 * peers, forward, 0)

    def factor(asker, peer):
        return mm_nt(scaled[asker], member[peer])

    plan = [(0, peer) for peer in range(peers)] + [(asker, 0) for asker in range(1, peers)]
    d_query = d_passage = None
    ahead = factor(*plan[0])
    for step, (asker, peer) in enumerate(plan):
        now = ahead
        if step + 1 < len(plan):
            ahead = factor(*plan[step + 1])
        d_similar = (expo[asker if peer == 0 else peers + peer] * now).astype(BF)
        if asker == 0:
            part = mm(d_similar, rows_ref[peer, query_rows:, :])
            d_query = part if d_query is None else d_query + part
        if peer == 0:
            part = mm_tn(d_similar, rows_ref[asker, :query_rows, :])
            d_passage = part if d_passage is None else d_passage + part
    d_ref[:query_rows, :] = d_query
    d_ref[query_rows:, :] = d_passage


def score(blocks, begins, ends, logs, positive, query_rows, query_total, slots):
    peers, rows = sum(block.shape[0] for block in blocks), blocks[0].shape[1]
    pack = rows - query_rows
    pairs = peers * peers * query_rows * pack
    vmem = pl.BlockSpec(memory_space=pltpu.VMEM)
    return pl.pallas_call(
        functools.partial(score_kernel, query_rows, float(query_total), slots),
        in_specs=[vmem] * (4 + len(blocks)),
        out_specs=[vmem, vmem],
        out_shape=[shape_of((8, LANES), F32), shape_of((rows, LANES), F32)],
        scratch_shapes=[
            pltpu.VMEM((peers, rows, LANES), BF),
            pltpu.VMEM((2 * peers, query_rows, pack), F32),
            pltpu.VMEM((peers, pack, LANES), BF),
            pltpu.VMEM((peers, query_rows, LANES), BF),
        ],
        compiler_params=pltpu.CompilerParams(vmem_limit_bytes=26 * MIB),
        cost_estimate=cost(8 * pairs * LANES, 4 * peers * rows * LANES, pairs),
        name="score",
    )(begins, ends, logs, positive, *blocks)


def back_top_kernel(
    where_ref,
    d_ref,
    proj_ref,
    unit_ref,
    scale_ref,
    low_ref,
    embed_ref,
    vec_ref,
    mid_ref,
    down_ref,
    own_ref,
    other_ref,
    sum_ref,
    acc,
):
    step = pl.program_id(0)

    @pl.when(step == 0)
    def _():
        acc[...] = jnp.zeros_like(acc)
        sum_ref[...] = jnp.zeros_like(sum_ref)

    projected = proj_ref[...]
    given = d_ref[...]
    size = lax.rsqrt(jnp.sum(projected * projected, -1, keepdims=True) + UNIT_EPS)
    along = jnp.sum(given * projected, -1, keepdims=True)
    d_proj = (size * given - projected * (size * size * size * along)).astype(BF)
    acc[...] += mm_tn(low_ref[...], d_proj)
    d_out = mm_nt(d_proj, embed_ref[...])
    unit = unit_ref[...]
    d_mid = normalize_back(d_out, vec_ref[2:3, :], unit, scale_ref[...])
    mid_ref[...] = d_mid
    low = d_mid.astype(BF)
    down_ref[...] = low
    sum_ref[0:1, :] += jnp.sum(d_out * unit, 0, keepdims=True)
    sum_ref[1:2, :] += jnp.sum(d_out, 0, keepdims=True)
    sum_ref[2:3, :] += jnp.sum(low.astype(F32), 0, keepdims=True)

    @pl.when(step == pl.num_programs(0) - 1)
    def _():
        put_rows(where_ref, own_ref, other_ref, acc[...])


def back_top(where, d_unit, projected, unit_two, scale_two, low_two, w_embed, vectors):
    rows, width = unit_two.shape
    owned = width // PIECES // 2

    def tile(columns):
        return pl.BlockSpec((TILE, columns), lambda i, w: (i, 0))

    return pl.pallas_call(
        back_top_kernel,
        grid_spec=pltpu.PrefetchScalarGridSpec(
            num_scalar_prefetch=1,
            grid=(rows // TILE,),
            in_specs=[
                tile(LANES),
                tile(LANES),
                tile(width),
                tile(1),
                tile(width),
                full((width, LANES)),
                full((16, width)),
            ],
            out_specs=[
                tile(width),
                tile(width),
                full((PIECES, owned, LANES)),
                full((PIECES, owned, LANES)),
                full((8, width)),
            ],
            scratch_shapes=[pltpu.VMEM((width, LANES), F32)],
        ),
        out_shape=[
            shape_of((rows, width), F32),
            shape_of((rows, width), BF),
            shape_of((PIECES, owned, LANES), BF),
            shape_of((PIECES, owned, LANES), BF),
            shape_of((8, width), F32),
        ],
        compiler_params=params(16),
        cost_estimate=cost(4 * rows * width * LANES, rows * width * 12),
        name="back_top",
    )(where, d_unit, projected, unit_two, scale_two, low_two, w_embed, vectors)


def back_down_kernel(
    where_ref, d_ref, down_ref, slope_ref, active_ref, up_ref, own_ref, other_ref, sum_ref
):
    given = d_ref[...]
    low = (mm_nt(given, down_ref[...]) * slope_ref[...].astype(F32)).astype(BF)
    up_ref[...] = low
    sum_ref[0:1, :] = jnp.sum(low.astype(F32), 0, keepdims=True)
    put_rows(where_ref, own_ref, other_ref, mm_tn(active_ref[...], given))


def back_down(where, d_down, w_down, slope, active):
    rows, width = d_down.shape
    wide = w_down.shape[0]
    steps = wide // width
    parts = PIECES // steps
    owned = wide // PIECES // 2
    column = pl.BlockSpec((rows, width), lambda t, w: (0, t))
    grad_block = pl.BlockSpec(
        (parts, owned, width), lambda t, w: (lax.bitwise_xor(t, w[0] // parts), 0, 0)
    )
    return pl.pallas_call(
        back_down_kernel,
        grid_spec=pltpu.PrefetchScalarGridSpec(
            num_scalar_prefetch=1,
            grid=(steps,),
            in_specs=[
                full((rows, width)),
                pl.BlockSpec((width, width), lambda t, w: (t, 0)),
                column,
                column,
            ],
            out_specs=[
                column,
                grad_block,
                grad_block,
                pl.BlockSpec((8, width), lambda t, w: (0, t)),
            ],
        ),
        out_shape=[
            near_shape((rows, wide), BF),
            shape_of((PIECES, owned, width), BF),
            shape_of((PIECES, owned, width), BF),
            shape_of((8, wide), F32),
        ],
        compiler_params=params(24),
        cost_estimate=cost(4 * rows * width * wide, 6 * rows * wide + 4 * wide * width),
        name="back_down",
    )(where, d_down, far(w_down), far(slope), far(active))


def back_up_kernel(where_ref, mid_ref, low_ref, d_ref, up_ref, out_ref, own_ref, other_ref, turned):
    @pl.when(pl.program_id(0) == 0)
    def _():
        out_ref[...] = mid_ref[...]
        turned[...] = low_ref[...].T

    given = d_ref[...]
    out_ref[...] += mm_nt(given, up_ref[...])
    put_rows(where_ref, own_ref, other_ref, mm(turned[...], given))


def back_up(where, d_mid, low_one, d_up, w_up):
    rows, width = d_mid.shape
    wide = w_up.shape[1]
    owned = width // PIECES // 2
    return pl.pallas_call(
        back_up_kernel,
        grid_spec=pltpu.PrefetchScalarGridSpec(
            num_scalar_prefetch=1,
            grid=(wide // width,),
            in_specs=[
                full((rows, width)),
                full((rows, width)),
                pl.BlockSpec((rows, width), lambda t, w: (0, t)),
                pl.BlockSpec((width, width), lambda t, w: (0, t)),
            ],
            out_specs=[
                full((rows, width)),
                pl.BlockSpec((PIECES, owned, width), lambda t, w: (0, 0, t)),
                pl.BlockSpec((PIECES, owned, width), lambda t, w: (0, 0, t)),
            ],
            scratch_shapes=[pltpu.VMEM((width, rows), BF)],
        ),
        out_shape=[
            shape_of((rows, width), F32),
            shape_of((PIECES, owned, wide), BF),
            shape_of((PIECES, owned, wide), BF),
        ],
        compiler_params=params(28),
        cost_estimate=cost(4 * rows * width * wide, 2 * rows * wide + 4 * wide * width),
        name="back_up",
    )(where, d_mid, far(low_one), near(d_up), far(w_up))


def back_out_kernel(
    where_ref,
    d_ref,
    unit_ref,
    scale_ref,
    first_ref,
    second_ref,
    out_ref,
    vec_ref,
    resid_ref,
    d_context_ref,
    own_ref,
    other_ref,
    sum_ref,
    acc,
):
    step = pl.program_id(0)

    @pl.when(step == 0)
    def _():
        acc[...] = jnp.zeros_like(acc)
        sum_ref[...] = jnp.zeros_like(sum_ref)

    d_out = d_ref[...]
    unit = unit_ref[...]
    d_resid = normalize_back(d_out, vec_ref[0:1, :], unit, scale_ref[...])
    resid_ref[...] = d_resid
    low = d_resid.astype(BF)
    d_context_ref[...] = mm_nt(low, out_ref[...]).astype(BF)
    cut = first_ref.shape[1]
    acc[:cut, :] += mm_tn(first_ref[...], low)
    acc[cut:, :] += mm_tn(second_ref[...], low)
    sum_ref[0:1, :] += jnp.sum(d_out * unit, 0, keepdims=True)
    sum_ref[1:2, :] += jnp.sum(d_out, 0, keepdims=True)
    sum_ref[2:3, :] += jnp.sum(low.astype(F32), 0, keepdims=True)

    @pl.when(step == pl.num_programs(0) - 1)
    def _():
        put_rows(where_ref, own_ref, other_ref, acc[...])


def back_out(where, d_one, unit_one, scale_one, contexts, w_out, vectors):
    rows, width = d_one.shape
    owned = width // PIECES // 2

    def tile(columns):
        return pl.BlockSpec((TILE, columns), lambda i, w: (i, 0))

    return pl.pallas_call(
        back_out_kernel,
        grid_spec=pltpu.PrefetchScalarGridSpec(
            num_scalar_prefetch=1,
            grid=(rows // TILE,),
            in_specs=[
                tile(width),
                tile(width),
                tile(1),
                *[tile(part.shape[1]) for part in contexts],
                full((width, width)),
                full((16, width)),
            ],
            out_specs=[
                tile(width),
                tile(width),
                full((PIECES, owned, width)),
                full((PIECES, owned, width)),
                full((8, width)),
            ],
            scratch_shapes=[pltpu.VMEM((width, width), F32)],
        ),
        out_shape=[
            shape_of((rows, width), F32),
            shape_of((rows, width), BF),
            shape_of((PIECES, owned, width), BF),
            shape_of((PIECES, owned, width), BF),
            shape_of((8, width), F32),
        ],
        compiler_params=params(20),
        cost_estimate=cost(4 * rows * width * width, rows * width * 16),
        name="back_out",
    )(where, d_one, unit_one, scale_one, *contexts, far(w_out), vectors)


def back_in_kernel(resid_ref, *refs):
    *parts, in_ref, out_ref = refs
    total = resid_ref[...]
    column = 0
    for part in parts:
        count = part.shape[1]
        total = total + mm_nt(part[...], in_ref[:, column : column + count])
        column += count
    out_ref[...] = total


def back_in(d_resid, parts, w_in):
    rows, width = d_resid.shape

    def tile(columns):
        return pl.BlockSpec((TILE, columns), lambda i: (i, 0))

    return pl.pallas_call(
        back_in_kernel,
        grid=(rows // TILE,),
        in_specs=[tile(width)] + [tile(p.shape[1]) for p in parts] + [full(w_in.shape)],
        out_specs=tile(width),
        out_shape=shape_of((rows, width), F32),
        compiler_params=params(24),
        cost_estimate=cost(6 * rows * width * width, rows * width * 14),
        name="back_in",
    )(d_resid, *parts, far(w_in))


def finish_kernel(steps, *refs):
    places = len(steps)
    pair_ref, *refs = refs
    totals, refs = refs[: len(refs) - 6 * places], refs[len(refs) - 6 * places :]
    weights, firsts, seconds = refs[:places], refs[places : 2 * places], refs[2 * places : 3 * places]
    outs = refs[3 * places :]
    norm = jnp.sqrt(pair_ref[1:2, 0:1])
    factor = CLIP_NORM / jnp.maximum(norm, CLIP_NORM)
    fix_one = 1.0 / (1.0 - BETA_ONE**STEP)
    fix_two = 1.0 / (1.0 - BETA_TWO**STEP)
    for item, (rate, decay, pieces) in enumerate(steps):
        for source, begin, width, target in pieces:
            if target is None:
                rows, columns = weights[item].shape
                grad = totals[source][:, begin : begin + width].T[:rows] * factor
                target, width = 0, columns
            else:
                grad = totals[source][:, begin : begin + width] * factor
            columns = slice(target, target + width)
            weight = weights[item][:, columns]
            first = BETA_ONE * firsts[item][:, columns] + (1.0 - BETA_ONE) * grad
            second = BETA_TWO * seconds[item][:, columns] + (1.0 - BETA_TWO) * grad * grad
            update = first * fix_one / (jnp.sqrt(second * fix_two) + ADAM_EPS)
            outs[item][:, columns] = first
            outs[places + item][:, columns] = second
            outs[2 * places + item][:, columns] = weight - rate * (update + decay * weight)


def finish(steps, pair, totals, masters, firsts, seconds):
    vmem = pl.BlockSpec(memory_space=pltpu.VMEM)
    held = [*masters, *firsts, *seconds]
    return pl.pallas_call(
        functools.partial(finish_kernel, steps),
        in_specs=[vmem] * (1 + len(totals) + len(held)),
        out_specs=[vmem] * len(held),
        out_shape=[shape_of(block.shape, F32) for block in held],
        compiler_params=pltpu.CompilerParams(vmem_limit_bytes=32 * MIB),
        name="finish",
    )(pair, *totals, *far(*held))


def swap(block, bits):
    count = lax.axis_size(AXES)
    return lax.ppermute(block, AXES, [(d, d ^ bits) for d in range(count)])


def phase(*blocks):
    return lax.optimization_barrier(blocks)


def cut_of(width):
    return (width // LANES + 1) // 2 * LANES


def gather_near(keep, give, core):
    theirs = swap(give, 1)
    ours = [jnp.where(core == 0, keep, theirs), jnp.where(core == 0, theirs, keep)]
    return jnp.concatenate(ours, 0)


def gather_far(mine):
    return jnp.stack([mine] + [swap(mine, 8 * step) for step in (1, 2, 3)])


def gather_cross(far):
    cut = cut_of(far.shape[-1])
    left, right = far[:, :, :cut], far[:, :, cut:]
    return jnp.stack([left, swap(left, 2)], 1), jnp.stack([right, swap(right, 4)], 1)


def gather_last(pair):
    left, right = pair
    left = jnp.stack([left, swap(left, 4)], 1)
    right = jnp.stack([right, swap(right, 2)], 2)
    own = jnp.concatenate([left, right], -1)
    return own.reshape(PIECES, *own.shape[3:])


def gather_plain(keep, give):
    whole = [lax.all_gather(half, AXES, axis=0, tiled=True) for half in (keep, give)]
    return [half.reshape(PIECES, -1, half.shape[1]) for half in whole]


def added(mine, theirs):
    return (mine.astype(F32) + theirs.astype(F32)).astype(BF)


def scatter_near(own, other):
    _, rows, width = own.shape
    return added(own, swap(other, 1)).reshape(4, 2, 2, rows, width)


def scatter_cross(near):
    cut = cut_of(near.shape[-1])
    left, right = near[..., :cut], near[..., cut:]
    return added(left[:, :, 0], swap(left[:, :, 1], 2)), added(right[:, 0], swap(right[:, 1], 4))


def scatter_last(pair):
    left, right = pair
    left = added(left[:, 0], swap(left[:, 1], 4))
    right = added(right[:, 0], swap(right[:, 1], 2))
    return jnp.concatenate([left, right], -1)


def scatter_far(far):
    total = far[0].astype(F32)
    for step in (1, 2, 3):
        total = total + swap(far[step], 8 * step).astype(F32)
    return total


def scatter_half(far):
    return added(far[:2], swap(far[2:], 16))


def scatter_end(half):
    return half[0].astype(F32) + swap(half[1], 8).astype(F32)


def scatter_plain(pair):
    pieces, rows, width = pair[0].shape
    whole = jnp.stack(pair, 1).reshape(2 * pieces * rows, width)
    return lax.psum_scatter(whole, AXES, scatter_dimension=0, tiled=True).astype(F32)


def keep_pair(own, other):
    return own, other


def same(blocks):
    return blocks


def sum_everywhere(values):
    count = lax.axis_size(AXES)
    bit = 1
    while bit < count:
        values = values + swap(values, bit)
        bit *= 2
    return values


def gather_peers(block):
    held = [block[None]]
    bit = 1
    sizes = []
    while bit < lax.axis_size("psg"):
        sizes.append(bit)
        bit *= 2
    for bit in reversed(sizes):
        now = jnp.concatenate(held, 0) if len(held) > 1 else held[0]
        held = [now, swap(now, bit)]
        if bit > 1:
            held = [jnp.concatenate(held, 0)]
    return held


def peer_order(count):
    order, bit = [0], count // 2
    while bit > 0:
        order = order + [peer ^ bit for peer in order]
        bit //= 2
    return order


def local(hidden, lengths_in, positive, *shards):
    masters, firsts, seconds = shards[:6], shards[6:12], shards[12:]
    psg_count = lax.axis_size("psg")
    count = lax.axis_size(AXES)
    split = count == 2 * PIECES
    mine = lax.axis_index("psg")
    rows, width = hidden.shape
    wide = masters[2].shape[1]
    pairs = width // LANES
    queries = positive.shape[0]
    query_rows = queries * QLEN
    query_total = queries * count
    slots = lengths_in.shape[1]
    pack_rows = rows - query_rows
    index = lax.axis_index(AXES)
    if split:
        where = jnp.stack([index // 2, index % 2]).astype(jnp.int32)
    else:
        where = jnp.zeros((2,), jnp.int32)
    core = where[1]

    front_keep, front_give, rest_keep, rest_give, down_low = pack(
        where, masters[0], masters[1], masters[2], masters[4], masters[5].T, masters[3]
    )
    w_down = lax.all_gather(down_low, AXES, axis=0, tiled=True)
    facts = jnp.concatenate([lengths_in[0], positive])[None]
    if split:
        beside = gather_near(front_keep, front_give, core)
        column = gather_far(beside)
        beside_rest = gather_near(rest_keep, rest_give, core)
        facts = gather_peers(facts)
        column, beside_rest, facts = phase(column, beside_rest, facts)
    else:
        facts = gather_peers(facts)
        front = gather_plain(front_keep, front_give)
        rest = gather_plain(rest_keep, rest_give)
    facts = jnp.concatenate(facts, 0).reshape(psg_count, -1)
    lengths, chosen = facts[:, :slots], facts[:, slots:]
    ends = jnp.cumsum(lengths, 1)
    lane_slot = jnp.eye(psg_count, dtype=jnp.int32)[:, :, None]
    unused = LANES // 2 - psg_count * slots

    def twice(values):
        return jnp.tile(jnp.pad(values, ((0, 0), (0, unused))), (1, 2))

    def by_lane(values):
        return twice((lane_slot * values[:, None, :]).reshape(psg_count, psg_count * slots))

    end_lanes = by_lane(ends)
    begin_lanes = by_lane(ends - lengths)
    log_lanes = twice(jnp.log(lengths.astype(F32)).reshape(1, -1))
    place_of = [peer_order(psg_count).index(peer) for peer in range(psg_count)]
    theirs = jnp.bitwise_xor(chosen // slots, mine)
    places = sum(jnp.where(theirs == peer, place, 0) for peer, place in enumerate(place_of))
    chosen = (places * slots + chosen % slots)[:, :, None]
    places = jnp.arange(pack_rows, dtype=jnp.int32)
    segment = jnp.sum((places[:, None] >= ends[0][None, :]).astype(jnp.int32), -1)
    seg_col, seg_row = segment[:, None], segment[None, :]

    notes = (begin_lanes, end_lanes, log_lanes, chosen, seg_col, seg_row)
    if split:
        crossed = gather_cross(column)
        moved = [beside_rest] + [swap(beside_rest, 8 * step) for step in (1, 2)]
        crossed, moved = phase(crossed, moved)
        own = gather_last(crossed)
        moved = moved + [swap(moved[0], 24)]
        own, moved, notes = phase(own, moved, notes)
        front, moved = phase((own, swap(own, 1)), moved)
        crossed_rest = gather_cross(jnp.stack(moved))
    begin_lanes, end_lanes, log_lanes, chosen, seg_col, seg_row = notes
    merged, turned, w_in, w_embed, vectors = project(where, hidden, *front)
    if split:
        merged, turned, crossed_rest = phase(merged, turned, crossed_rest)
    cut = 2 * pairs // 3
    contexts = [attend(merged, seg_col, seg_row, query_rows, 0, cut)]
    if split:
        own = gather_last(crossed_rest)
        merged, own, contexts = phase(merged, own, contexts)
    contexts.append(attend(merged, seg_col, seg_row, query_rows, cut, pairs - cut))
    if split:
        rest = (own, swap(own, 1))
    unit_one, scale_one, low_one, active, slope, unit_two, scale_two, low_two, *held = encode(
        where, contexts, hidden, vectors, w_embed, w_down, *rest
    )
    projected, embedded, w_up, w_out = held
    loss_block, d_unit = score(
        gather_peers(embedded), begin_lanes, end_lanes, log_lanes, chosen, query_rows, query_total, slots
    )
    d_mid, d_down, *grad_embed, sums_top = back_top(
        where, d_unit, projected, unit_two, scale_two, low_two, w_embed, vectors
    )
    d_up, *grad_down, sums_up = back_down(where, d_down, w_down, slope, active)
    steps = (scatter_near, scatter_cross, scatter_last, scatter_half, scatter_end, scatter_far)
    plain = (keep_pair, same, same, same, scatter_plain, scatter_plain)
    closest, cross, last, middle, end, final = steps if split else plain

    d_one, *grad_up = back_up(where, d_mid, low_one, d_up, w_up)
    downs = closest(*grad_down)
    here, d_one, grad_up, downs = phase(where, d_one, grad_up, downs)
    d_resid, d_context, *grad_out, sums_out = back_out(
        here, d_one, unit_one, scale_one, contexts, w_out, vectors
    )

    def back(held, *rest):
        *d_part, own, other, sums = attend_back(
            held, merged, d_context, turned, seg_col, seg_row, query_rows, *rest
        )
        return d_part, (own, other), sums

    third = pairs // 3
    downs, ups = cross(downs), closest(*grad_up)
    here, d_context, grad_out, downs, ups = phase(where, d_context, grad_out, downs, ups)
    part_one, ones, sums_one = back(here, 0, third, "copied", grad_out)
    downs, ups = last(downs), cross(ups)
    here, part_one, ones, downs, ups = phase(where, part_one, ones, downs, ups)
    part_two, twos, sums_two = back(here, third, third)
    downs, ups, ones = middle(downs), last(ups), closest(*ones)
    here, part_two, twos, downs, ups, ones = phase(where, part_two, twos, downs, ups, ones)
    part_three, threes, sums_three = back(
        here,
        2 * third,
        pairs - 2 * third,
        "vectors",
        (*grad_embed, sums_out, sums_top, sums_up, sums_one, sums_two),
    )
    total_down, ups, ones, twos = end(downs), middle(ups), cross(ones), closest(*twos)
    part_three, threes, total_down, ups, ones, twos = phase(
        part_three, threes, total_down, ups, ones, twos
    )
    total_up, ones, threes = end(ups), last(ones), closest(*threes)
    total_up, ones, threes, d_resid = phase(total_up, ones, threes, d_resid)
    parts = (part_one, part_two, part_three)
    ordered = [part[which] for which in (0, 1, 2) for part in parts]
    if split:
        ones, twos = middle(ones), cross(jnp.concatenate([twos, threes], -1))
        input_grad = back_in(d_resid, ordered, w_in)
        input_grad, ones, twos = phase(input_grad, ones, twos)
        total_one, twos = phase(end(ones), last(twos))
        total_two = final(twos)
    else:
        input_grad = back_in(d_resid, ordered, w_in)
        total_one = final(ones)
        total_two = final([jnp.concatenate([two, three], -1) for two, three in zip(twos, threes)])

    totals = [total_down, total_up, total_one, total_two]
    squares = sum(jnp.sum(total * total) for total in totals)
    pair = jnp.stack([loss_block[0, 0], squares])
    pair = sum_everywhere(jnp.broadcast_to(pair[:, None], (2, LANES)))
    loss = pair[0, 0] / query_total
    grad_norm = jnp.sqrt(pair[1, 0])

    block = 3 * LANES
    inward_pieces = []
    for head_pair in range(pairs):
        source = 2 if head_pair < third else 3
        begin = (head_pair if head_pair < third else head_pair - third) * block
        for part in (0, 1, 2):
            target = part * width + head_pair * LANES
            inward_pieces.append((source, begin + part * LANES, LANES, target))
    first_end = third * block
    last_end = (pairs - third) * block
    plans = (
        (RATE_MATRIX, DECAY, tuple(inward_pieces)),
        (RATE_MATRIX, DECAY, ((2, first_end, width, 0),)),
        (RATE_MATRIX, DECAY, ((1, 0, wide, 0),)),
        (RATE_MATRIX, DECAY, ((0, 0, width, 0),)),
        (RATE_MATRIX, DECAY, ((3, last_end + LANES, LANES, 0),)),
        (RATE_VECTOR, 0.0, ((3, last_end, LANES, None),)),
    )
    held = [list(group[:5]) + [group[5].T] for group in (masters, firsts, seconds)]
    stepped = finish(plans, pair, totals, *held)
    stepped = [block.T if place % 6 == 5 else block for place, block in enumerate(stepped)]
    return (loss, input_grad, grad_norm) + tuple(stepped)


def solution(mesh):
    by_rows = P(AXES, None)
    placed = (by_rows, by_rows, P(AXES)) + (by_rows,) * 18
    return jax.shard_map(
        local,
        mesh=mesh,
        in_specs=placed,
        out_specs=(P(), by_rows, P()) + (by_rows,) * 18,
        check_vma=False,
    )
```

```python
import functools

import jax
import jax.numpy as jnp
from jax import lax
from jax.experimental import pallas as pl
from jax.experimental.pallas import tpu as pltpu
from jax.sharding import PartitionSpec as P

HEADS = 12
HEAD = 64
QLEN = 32
STEP = 10

TAU_INV = 10.0
SCORE_SCALE = 10.0
CLIP_NORM = 0.02
BETA_ONE = 0.9
BETA_TWO = 0.999
ADAM_EPS = 1e-08
RATE_MATRIX = 0.05
RATE_VECTOR = 0.5
DECAY = 0.01
NORM_EPS = 1e-12
UNIT_EPS = 1e-06

AXES = ("group", "psg")
LANES = 128
PIECES = 16
TILE = 256
MIB = 2**20
BF = jnp.bfloat16
F32 = jnp.float32


def mm(left, right):
    return lax.dot_general(left, right, (((1,), (0,)), ((), ())), preferred_element_type=F32)


def mm_nt(left, right):
    return lax.dot_general(left, right, (((1,), (1,)), ((), ())), preferred_element_type=F32)


def mm_tn(left, right):
    return lax.dot_general(left, right, (((0,), (0,)), ((), ())), preferred_element_type=F32)


def full(shape):
    return pl.BlockSpec(shape, lambda *_: (0,) * len(shape))


def params(mib=56):
    return pltpu.CompilerParams(
        vmem_limit_bytes=mib * MIB, dimension_semantics=("arbitrary",)
    )


def cost(flops, moved, special=0):
    return pl.CostEstimate(flops=int(flops), bytes_accessed=int(moved), transcendentals=int(special))


def shape_of(shape, dtype):
    return jax.ShapeDtypeStruct(shape, dtype)


def far_shape(shape, dtype):
    return pltpu.HBM(shape, dtype)


def far(*blocks):
    held = [pltpu.with_memory_space_constraint(block, pltpu.HBM) for block in blocks]
    return held if len(held) > 1 else held[0]


def near_shape(shape, dtype):
    return pltpu.VMEM(shape, dtype)


def near(*blocks):
    held = [pltpu.with_memory_space_constraint(block, pltpu.VMEM) for block in blocks]
    return held if len(held) > 1 else held[0]


def any_space():
    return pl.BlockSpec(memory_space=pl.ANY)


def fetch_pieces(where_ref, own_ref, other_ref, moves, sems):
    chip, core = where_ref[0], where_ref[1]
    rows = own_ref.shape[1]

    def start(halves):
        for piece in range(own_ref.shape[0]):
            source = lax.bitwise_xor(chip, piece)
            for number, (half, first, width, target, column) in enumerate(moves):
                pltpu.make_async_copy(
                    halves[half].at[source, :, pl.ds(first, width)],
                    target.at[pl.ds(rows * piece, rows), pl.ds(column, width)],
                    sems.at[number],
                ).start()

    pl.when(core == 0)(lambda: start((own_ref, other_ref)))
    pl.when(core == 1)(lambda: start((other_ref, own_ref)))
    for number, (_, _, width, target, column) in enumerate(moves):
        landed = target.at[:, pl.ds(column, width)]
        pltpu.make_async_copy(landed, landed, sems.at[number]).wait()


def pack_kernel(where_ref, in_ref, out_ref, up_ref, embed_ref, turned_ref, down_ref, *targets):
    front_keep, front_give, rest_keep, rest_give, down_low = targets
    half_in, half_out, half_up = (ref.shape[1] // 2 for ref in (in_ref, out_ref, up_ref))
    owned = in_ref.shape[0]
    down_low[...] = down_ref[...].astype(BF)

    def fill(front, rest, half):
        front[:, :half_in] = in_ref[:, half * half_in : (half + 1) * half_in].astype(BF)
        if half == 0:
            front[:, half_in:] = embed_ref[...].astype(BF)
        else:
            empty = jnp.zeros((LANES - turned_ref.shape[0], owned), F32)
            front[:, half_in:] = jnp.concatenate([turned_ref[...], empty], 0).T.astype(BF)
        rest[:, :half_up] = up_ref[:, half * half_up : (half + 1) * half_up].astype(BF)
        rest[:, half_up:] = out_ref[:, half * half_out : (half + 1) * half_out].astype(BF)

    @pl.when(where_ref[1] == 0)
    def _():
        fill(front_keep, rest_keep, 0)
        fill(front_give, rest_give, 1)

    @pl.when(where_ref[1] == 1)
    def _():
        fill(front_keep, rest_keep, 1)
        fill(front_give, rest_give, 0)


def pack(where, inward, outward, upward, embed, vectors, downward):
    owned, width = outward.shape
    front = 3 * width // 2 + LANES
    rest = upward.shape[1] // 2 + width // 2
    vmem = pl.BlockSpec(memory_space=pltpu.VMEM)
    return pl.pallas_call(
        pack_kernel,
        in_specs=[pl.BlockSpec(memory_space=pltpu.SMEM)] + [vmem] * 6,
        out_specs=[vmem] * 5,
        out_shape=[
            shape_of((owned, front), BF),
            shape_of((owned, front), BF),
            shape_of((owned, rest), BF),
            shape_of((owned, rest), BF),
            shape_of(downward.shape, BF),
        ],
        compiler_params=pltpu.CompilerParams(vmem_limit_bytes=16 * MIB),
        name="pack",
    )(where, *far(inward, outward, upward, embed, vectors, downward))


def project_kernel(
    where_ref, rows_ref, own_ref, other_ref, merged_ref, turned_ref, in_ref, embed_ref, vec_ref, raw, sems
):
    width = rows_ref.shape[1]
    half_in = 3 * width // 2

    @pl.when(pl.program_id(0) == 0)
    def _():
        moves = [(half, 0, half_in, in_ref, half * half_in) for half in (0, 1)]
        moves.append((0, half_in, LANES, embed_ref, 0))
        moves.append((1, half_in, LANES, raw, 0))
        fetch_pieces(where_ref, own_ref, other_ref, moves, sems)
        vec_ref[...] = raw[...].astype(F32).T[: vec_ref.shape[0]]

    rows = rows_ref[...]
    turned_ref[...] = rows.T
    for part, bias in ((0, 4), (1, None), (2, 5)):
        block = mm(rows, in_ref[:, part * width : (part + 1) * width])
        if bias is not None:
            block = block + vec_ref[bias : bias + 1, :]
        merged_ref[:, part * width : (part + 1) * width] = block.astype(BF)


def project(where, hidden, own, other):
    rows, width = hidden.shape
    return pl.pallas_call(
        project_kernel,
        grid_spec=pltpu.PrefetchScalarGridSpec(
            num_scalar_prefetch=1,
            grid=(rows // TILE,),
            in_specs=[pl.BlockSpec((TILE, width), lambda i, w: (i, 0)), any_space(), any_space()],
            out_specs=[
                pl.BlockSpec((TILE, 3 * width), lambda i, w: (i, 0)),
                pl.BlockSpec((width, TILE), lambda i, w: (0, i)),
                full((width, 3 * width)),
                full((width, LANES)),
                full((16, width)),
            ],
            scratch_shapes=[pltpu.VMEM((width, LANES), BF), pltpu.SemaphoreType.DMA((4,))],
        ),
        out_shape=[
            far_shape((rows, 3 * width), BF),
            far_shape((width, rows), BF),
            far_shape((width, 3 * width), BF),
            shape_of((width, LANES), BF),
            shape_of((16, width), F32),
        ],
        compiler_params=params(20),
        cost_estimate=cost(6 * rows * width * width, 8 * rows * width + 16 * width * width),
        name="project",
    )(where, far(hidden), own, other)


def head_masks():
    lane = lax.broadcasted_iota(jnp.int32, (1, LANES), 1)
    return [(lane < HEAD).astype(BF), (lane >= HEAD).astype(BF)]


def softmax_rows(scores):
    peak = jnp.max(scores, -1, keepdims=True)
    expo = jnp.exp(scores - peak)
    return expo * (1.0 / jnp.sum(expo, -1, keepdims=True))


QUERY_TILE = 256
PACK_TILE = 384


def blocks_of(rows, query_rows):
    size = QUERY_TILE
    listed = [(first, size, first, size, True) for first in range(0, query_rows, size)]
    for first in range(query_rows, rows, PACK_TILE):
        listed.append((first, PACK_TILE, query_rows, rows - query_rows, False))
    return listed


def allowed_pairs(block, seg_col, seg_row, query_rows):
    first, count, _, keys, is_query = block
    if is_query:
        mine = lax.broadcasted_iota(jnp.int32, (count, keys), 0) // QLEN
        theirs = lax.broadcasted_iota(jnp.int32, (count, keys), 1) // QLEN
        return mine == theirs
    begin = first - query_rows
    return seg_col[begin : begin + count, :] == seg_row[0:1, :]


def attend_kernel(query_rows, seg_col, seg_row, q_ref, k_ref, v_ref, out_ref):
    masks = head_masks()
    blocks = blocks_of(q_ref.shape[0], query_rows)

    def products(block):
        first, count, begin, keys, _ = block
        query = q_ref[first : first + count, :]
        key = k_ref[begin : begin + keys, :]
        return [mm_nt(query * (mask * HEAD**-0.5), key) for mask in masks]

    ahead = products(blocks[0])
    for place, block in enumerate(blocks):
        first, count, begin, keys, _ = block
        scores = ahead
        if place + 1 < len(blocks):
            ahead = products(blocks[place + 1])
        allowed = allowed_pairs(block, seg_col, seg_row, query_rows)
        value = v_ref[begin : begin + keys, :]
        total = None
        for mask, score in zip(masks, scores):
            weights = softmax_rows(jnp.where(allowed, score, -1e9)).astype(BF)
            part = mm(weights, value * mask)
            total = part if total is None else total + part
        out_ref[first : first + count, :] = total.astype(BF)


def attend(merged, seg_col, seg_row, query_rows, first_pair, count):
    rows, wide = merged.shape
    pairs = wide // 3 // LANES
    pack = rows - query_rows

    def column(part):
        return pl.BlockSpec((rows, LANES), lambda h: (0, part * pairs + first_pair + h))

    return pl.pallas_call(
        functools.partial(attend_kernel, query_rows),
        grid=(count,),
        in_specs=[full((pack, 1)), full((1, pack)), column(0), column(1), column(2)],
        out_specs=pl.BlockSpec((rows, LANES), lambda h: (0, h)),
        out_shape=shape_of((rows, count * LANES), BF),
        compiler_params=params(16),
        cost_estimate=cost(
            16 * count * pack * pack * LANES, 8 * rows * count * LANES, 2 * count * pack * pack
        ),
        name="attend",
    )(seg_col, seg_row, *far(merged, merged, merged))


def put_rows(where_ref, own_ref, other_ref, values):
    pieces, rows = own_ref.shape[0], own_ref.shape[1]
    chip = lax.bitwise_and(where_ref[0], pieces - 1)

    def store(targets):
        for piece in range(pieces):
            for half in (0, 1):
                begin = (2 * piece + half) * rows
                targets[half][lax.bitwise_xor(chip, piece)] = values[begin : begin + rows, :].astype(BF)

    pl.when(where_ref[1] == 0)(lambda: store((own_ref, other_ref)))
    pl.when(where_ref[1] == 1)(lambda: store((other_ref, own_ref)))


def attend_back_pair(query_rows, seg_col, seg_row, q_ref, k_ref, v_ref, d_ref, dq_ref, dk_ref, dv_ref, acc_k, acc_v):
    masks = head_masks()
    rows = q_ref.shape[0]
    blocks = blocks_of(rows, query_rows)

    def products(block):
        first, count, begin, keys, _ = block
        query = q_ref[first : first + count, :]
        given = d_ref[first : first + count, :]
        key = k_ref[begin : begin + keys, :]
        value = v_ref[begin : begin + keys, :]
        made = []
        for mask in masks:
            scaled = query * (mask * HEAD**-0.5)
            own = given * mask
            made.append((scaled, own, mm_nt(scaled, key), mm_nt(own, value)))
        return made

    ahead = products(blocks[0])
    started = False
    for place, block in enumerate(blocks):
        first, count, begin, keys, is_query = block
        held = ahead
        if place + 1 < len(blocks):
            ahead = products(blocks[place + 1])
        allowed = allowed_pairs(block, seg_col, seg_row, query_rows)
        key = k_ref[begin : begin + keys, :]
        dq = dk = dv = 0.0
        for mask, (scaled, own, scores, d_weights) in zip(masks, held):
            weights = softmax_rows(jnp.where(allowed, scores, -1e9))
            inner = jnp.sum(d_weights * weights, -1, keepdims=True)
            d_scores = (weights * (d_weights - inner)).astype(BF)
            dq = dq + mm(d_scores, key * (mask * HEAD**-0.5))
            dk = dk + mm_tn(d_scores, scaled)
            dv = dv + mm_tn(weights.astype(BF), own)
        dq_ref[first : first + count, :] = dq.astype(BF)
        if is_query:
            dk_ref[begin : begin + keys, :] = dk.astype(BF)
            dv_ref[begin : begin + keys, :] = dv.astype(BF)
        elif started:
            acc_k[...] += dk
            acc_v[...] += dv
        else:
            acc_k[...] = dk
            acc_v[...] = dv
            started = True
    dk_ref[query_rows:, :] = acc_k[...].astype(BF)
    dv_ref[query_rows:, :] = acc_v[...].astype(BF)


def column_sums(block):
    return jnp.sum(block.astype(F32), 0, keepdims=True)


def attend_back_kernel(query_rows, count, extra, where_ref, *refs):
    seg_col, seg_row, q_ref, k_ref, v_ref, d_ref, turned_ref, *refs = refs
    passed, refs = refs[: len(refs) - 8], refs[len(refs) - 8 :]
    dq_ref, dk_ref, dv_ref, own_ref, other_ref, sum_ref, acc_k, acc_v = refs
    step = pl.program_id(0)

    @pl.when(step < count)
    def _():
        attend_back_pair(
            query_rows, seg_col, seg_row, q_ref, k_ref, v_ref, d_ref, dq_ref, dk_ref, dv_ref, acc_k, acc_v
        )
        turned = turned_ref[...]
        grads = [mm(turned, ref[...]) for ref in (dq_ref, dk_ref, dv_ref)]
        put_rows(where_ref, own_ref, other_ref, jnp.concatenate(grads, 1))
        empty = jnp.zeros((6, LANES), F32)
        sums = [column_sums(dq_ref[...]), column_sums(dv_ref[...]), empty]
        sum_ref[step] = jnp.concatenate(sums, 0)

    @pl.when(step >= count)
    def _():
        if extra == "copied":
            own_ref[...] = passed[0][...]
            other_ref[...] = passed[1][...]
        elif extra == "vectors":
            own_embed, other_embed, out_sums, top_sums, up_sums, *in_sums = passed
            width = out_sums.shape[1]
            blocks = [ref[place] for ref in in_sums for place in range(ref.shape[0])]
            both = jnp.concatenate(blocks + [sum_ref[place] for place in range(count)], 1)
            stacked = [out_sums[0:2, :], top_sums[0:2, :], both[0:2]]
            stacked += [out_sums[2:3, :], top_sums[2:3, :]]
            for part in range(up_sums.shape[1] // width):
                stacked.append(up_sums[0:1, part * width : (part + 1) * width])
            used = sum(block.shape[0] for block in stacked)
            stacked.append(jnp.zeros((LANES - used, width), F32))
            turned_sums = jnp.concatenate(stacked, 0).T
            empty = jnp.zeros((width, 2 * LANES), F32)
            put_rows(where_ref, own_ref, other_ref, jnp.concatenate([turned_sums, empty], 1))
            own_ref[:, :, LANES : 2 * LANES] = own_embed[...]
            other_ref[:, :, LANES : 2 * LANES] = other_embed[...]


def attend_back(
    where, merged, d_context, turned, seg_col, seg_row, query_rows, first_pair, count, extra=None, passed=()
):
    rows, wide = merged.shape
    width = wide // 3
    pairs = width // LANES
    pack = rows - query_rows
    owned = width // PIECES // 2
    block = 3 * LANES
    steps = count
    passed_specs = []
    if extra == "copied":
        steps = count + passed[0].shape[2] // block
        own = pl.BlockSpec((PIECES, owned, block), lambda h, w: (0, 0, jnp.maximum(h - count, 0)))
        passed_specs = [own, own]
    elif extra == "vectors":
        steps = count + 1
        passed_specs = [full(block_in.shape) for block_in in passed]

    def pair_of(step):
        return jnp.minimum(step, count - 1)

    def column(part):
        return pl.BlockSpec((rows, LANES), lambda h, w: (0, part * pairs + first_pair + pair_of(h)))

    own_column = pl.BlockSpec((rows, LANES), lambda h, w: (0, pair_of(h)))
    grad_block = pl.BlockSpec((PIECES, owned, block), lambda h, w: (0, 0, h))
    return pl.pallas_call(
        functools.partial(attend_back_kernel, query_rows, count, extra),
        grid_spec=pltpu.PrefetchScalarGridSpec(
            num_scalar_prefetch=1,
            grid=(steps,),
            in_specs=[
                full((pack, 1)),
                full((1, pack)),
                column(0),
                column(1),
                column(2),
                pl.BlockSpec((rows, LANES), lambda h, w: (0, first_pair + pair_of(h))),
                full((width, rows)),
                *passed_specs,
            ],
            out_specs=[
                own_column,
                own_column,
                own_column,
                grad_block,
                grad_block,
                full((count, 8, LANES)),
            ],
            scratch_shapes=[pltpu.VMEM((pack, LANES), F32), pltpu.VMEM((pack, LANES), F32)],
        ),
        out_shape=[
            shape_of((rows, count * LANES), BF),
            shape_of((rows, count * LANES), BF),
            shape_of((rows, count * LANES), BF),
            shape_of((PIECES, owned, steps * block), BF),
            shape_of((PIECES, owned, steps * block), BF),
            shape_of((count, 8, LANES), F32),
        ],
        compiler_params=params(24),
        cost_estimate=cost(
            count * (20 * pack * pack * LANES + 6 * rows * width * LANES),
            count * rows * LANES * 14,
            2 * count * pack * pack,
        ),
        name="attend_back",
    )(where, seg_col, seg_row, *far(merged, merged, merged), d_context, far(turned), *passed)


def normalize(residual):
    center = jnp.mean(residual, -1, keepdims=True)
    shifted = residual - center
    spread = jnp.mean(shifted * shifted, -1, keepdims=True)
    scale = lax.rsqrt(spread + NORM_EPS)
    return shifted * scale, scale


def normalize_back(d_out, gain, unit, scale):
    d_unit = d_out * gain
    return scale * (
        d_unit
        - jnp.mean(d_unit, -1, keepdims=True)
        - unit * jnp.mean(d_unit * unit, -1, keepdims=True)
    )


def gelu_parts(given):
    below = 0.5 + 0.5 * lax.erf(given * 0.5**0.5)
    bell = jnp.exp(-0.5 * given * given)
    return given * below, below + given * bell * 0.3989422804014327


def encode_kernel(
    where_ref,
    first_ref,
    second_ref,
    hidden_ref,
    vec_ref,
    embed_ref,
    down_ref,
    own_ref,
    other_ref,
    unit_ref,
    scale_ref,
    low_ref,
    active_ref,
    slope_ref,
    unit_two_ref,
    scale_two_ref,
    low_two_ref,
    proj_ref,
    row_ref,
    up_far,
    out_far,
    up_ref,
    out_ref,
    sems,
    sent,
):
    width = hidden_ref.shape[1]
    half, half_out = up_ref.shape[1] // 2, width // 2
    copies = [
        pltpu.make_async_copy(up_ref, up_far, sent.at[0]),
        pltpu.make_async_copy(out_ref, out_far, sent.at[1]),
    ]

    @pl.when(pl.program_id(0) == 0)
    def _():
        moves = []
        for side in (0, 1):
            moves.append((side, half, half_out, out_ref, side * half_out))
            moves.append((side, 0, half, up_ref, side * half))
        fetch_pieces(where_ref, own_ref, other_ref, moves, sems)
        for copy in copies:
            copy.start()

    cut = first_ref.shape[1]
    branch = mm(first_ref[...], out_ref[:cut, :]) + mm(second_ref[...], out_ref[cut:, :])
    unit, scale = normalize(hidden_ref[...].astype(F32) + (branch + vec_ref[6:7, :]))
    unit_ref[...] = unit
    scale_ref[...] = scale
    first = unit * vec_ref[0:1, :] + vec_ref[1:2, :]
    low = first.astype(BF)
    low_ref[...] = low
    parts = up_ref.shape[1] // width

    def raised_part(part):
        raised = mm(low, up_ref[:, part * width : (part + 1) * width])
        return raised + vec_ref[8 + part : 9 + part, :]

    ahead = raised_part(0)
    total = first + vec_ref[7:8, :]
    for part in range(parts):
        raised = ahead
        if part + 1 < parts:
            ahead = raised_part(part + 1)
        columns = slice(part * width, (part + 1) * width)
        value, slope = gelu_parts(raised)
        value = value.astype(BF)
        active_ref[:, columns] = value
        slope_ref[:, columns] = slope.astype(BF)
        total = total + mm(value, down_ref[columns, :])
    unit, scale = normalize(total)
    unit_two_ref[...] = unit
    scale_two_ref[...] = scale
    low = (unit * vec_ref[2:3, :] + vec_ref[3:4, :]).astype(BF)
    low_two_ref[...] = low
    projected = mm(low, embed_ref[...])
    proj_ref[...] = projected
    size = jnp.sum(projected * projected, -1, keepdims=True)
    row_ref[...] = (projected * lax.rsqrt(size + UNIT_EPS)).astype(BF)

    @pl.when(pl.program_id(0) == pl.num_programs(0) - 1)
    def _():
        for copy in copies:
            copy.wait()


def encode(where, contexts, hidden, vectors, w_embed, w_down, own, other):
    rows, width = hidden.shape
    wide = w_down.shape[0]

    def tile(columns):
        return pl.BlockSpec((TILE, columns), lambda i, w: (i, 0))

    return pl.pallas_call(
        encode_kernel,
        grid_spec=pltpu.PrefetchScalarGridSpec(
            num_scalar_prefetch=1,
            grid=(rows // TILE,),
            in_specs=[
                *[tile(part.shape[1]) for part in contexts],
                tile(width),
                full((16, width)),
                full((width, LANES)),
                full((wide, width)),
                any_space(),
                any_space(),
            ],
            out_specs=[
                tile(width),
                tile(1),
                tile(width),
                tile(wide),
                tile(wide),
                tile(width),
                tile(1),
                tile(width),
                tile(LANES),
                tile(LANES),
                any_space(),
                any_space(),
            ],
            scratch_shapes=[
                pltpu.VMEM((width, wide), BF),
                pltpu.VMEM((width, width), BF),
                pltpu.SemaphoreType.DMA((4,)),
                pltpu.SemaphoreType.DMA((2,)),
            ],
        ),
        out_shape=[
            far_shape((rows, width), F32),
            far_shape((rows, 1), F32),
            far_shape((rows, width), BF),
            far_shape((rows, wide), BF),
            far_shape((rows, wide), BF),
            far_shape((rows, width), F32),
            far_shape((rows, 1), F32),
            far_shape((rows, width), BF),
            far_shape((rows, LANES), F32),
            shape_of((rows, LANES), BF),
            far_shape((width, wide), BF),
            far_shape((width, width), BF),
        ],
        compiler_params=params(44),
        cost_estimate=cost(
            2 * rows * width * (width + 2 * wide), rows * (20 * width + 4 * wide), rows * wide
        ),
        name="encode",
    )(where, *contexts, far(hidden), vectors, w_embed, *far(w_down, own, other))


def split_two(values):
    high = values.astype(BF)
    return high, (values - high.astype(F32)).astype(BF)


def score_kernel(
    query_rows,
    query_total,
    slots,
    begin_ref,
    end_ref,
    log_ref,
    positive_ref,
    *refs,
):
    *block_refs, loss_ref, d_ref, rows_ref, expo, member, scaled = refs
    peers, rows, _ = rows_ref.shape
    place = 0
    for ref in block_refs:
        rows_ref[place : place + ref.shape[0]] = ref[...]
        place += ref.shape[0]
    pack = rows - query_rows
    half = query_rows // 2
    queries = half // QLEN
    place = lax.broadcasted_iota(jnp.int32, (pack, LANES), 0)
    lane = lax.broadcasted_iota(jnp.int32, (1, LANES), 1)
    for peer in range(peers):
        inside = (place >= begin_ref[peer : peer + 1, :]) & (place < end_ref[peer : peer + 1, :])
        member[peer] = inside.astype(F32).astype(BF)
    loss_ref[...] = jnp.zeros_like(loss_ref)

    def forward(step, carry):
        asker, part = step // 2, step % 2
        own_rows = pl.ds(pl.multiple_of(part * half, half), half)
        query = rows_ref[asker, own_rows, :]
        total = jnp.zeros((half, LANES), F32)
        peaks = jnp.zeros((half, LANES), F32)
        ahead = mm_nt(query, rows_ref[0, query_rows:, :])
        for peer in range(peers):
            similar = ahead
            if peer + 1 < peers:
                ahead = mm_nt(query, rows_ref[peer + 1, query_rows:, :])
            peak = jnp.max(similar, -1, keepdims=True)
            value = jnp.exp((similar - peak) * TAU_INV)
            if peer == 0:
                expo[asker, own_rows, :] = value
            else:

                @pl.when(asker == 0)
                def _():
                    expo[peers + peer, own_rows, :] = value

            high, low = split_two(value)
            total = total + (mm(high, member[peer]) + mm(low, member[peer]))
            peaks = jnp.where(lane // slots == peer, peak, peaks)
        used = lane < peers * slots
        total = jnp.where(used, total, 1.0)
        smooth = jnp.log(total) / TAU_INV + peaks - log_ref[...] / TAU_INV
        logits = SCORE_SCALE * jnp.sum(smooth.reshape(queries, QLEN, LANES), 1)
        logits = jnp.where(used, logits, -1e30)
        own_queries = pl.ds(pl.multiple_of(part * queries, queries), queries)
        picked = (positive_ref[asker, own_queries, :] == lane).astype(F32)
        high = jnp.max(logits, -1, keepdims=True)
        powers = jnp.where(used, jnp.exp(logits - high), 0.0)
        norm = jnp.sum(powers, -1, keepdims=True)
        each = high + jnp.log(norm) - jnp.sum(picked * logits, -1, keepdims=True)
        d_logits = (powers / norm - picked) / query_total
        spread = jnp.broadcast_to(
            (SCORE_SCALE * d_logits)[:, None, :], (queries, QLEN, LANES)
        ).reshape(half, LANES)
        exact = jnp.where(used, spread / total, 0.0)
        rounded = exact.astype(BF).astype(F32)
        rest = pltpu.roll(exact - rounded, LANES // 2, 1)
        scaled[asker, own_rows, :] = (rounded + rest).astype(BF)

        @pl.when(asker == 0)
        def _():
            loss_ref[...] += jnp.broadcast_to(jnp.sum(each), loss_ref.shape)

        return carry

    lax.fori_loop(0, 2 * peers, forward, 0)

    def factor(asker, peer):
        return mm_nt(scaled[asker], member[peer])

    plan = [(0, peer) for peer in range(peers)] + [(asker, 0) for asker in range(1, peers)]
    d_query = d_passage = None
    ahead = factor(*plan[0])
    for step, (asker, peer) in enumerate(plan):
        now = ahead
        if step + 1 < len(plan):
            ahead = factor(*plan[step + 1])
        d_similar = (expo[asker if peer == 0 else peers + peer] * now).astype(BF)
        if asker == 0:
            part = mm(d_similar, rows_ref[peer, query_rows:, :])
            d_query = part if d_query is None else d_query + part
        if peer == 0:
            part = mm_tn(d_similar, rows_ref[asker, :query_rows, :])
            d_passage = part if d_passage is None else d_passage + part
    d_ref[:query_rows, :] = d_query
    d_ref[query_rows:, :] = d_passage


def score(blocks, begins, ends, logs, positive, query_rows, query_total, slots):
    peers, rows = sum(block.shape[0] for block in blocks), blocks[0].shape[1]
    pack = rows - query_rows
    pairs = peers * peers * query_rows * pack
    vmem = pl.BlockSpec(memory_space=pltpu.VMEM)
    return pl.pallas_call(
        functools.partial(score_kernel, query_rows, float(query_total), slots),
        in_specs=[vmem] * (4 + len(blocks)),
        out_specs=[vmem, vmem],
        out_shape=[shape_of((8, LANES), F32), shape_of((rows, LANES), F32)],
        scratch_shapes=[
            pltpu.VMEM((peers, rows, LANES), BF),
            pltpu.VMEM((2 * peers, query_rows, pack), F32),
            pltpu.VMEM((peers, pack, LANES), BF),
            pltpu.VMEM((peers, query_rows, LANES), BF),
        ],
        compiler_params=pltpu.CompilerParams(vmem_limit_bytes=26 * MIB),
        cost_estimate=cost(8 * pairs * LANES, 4 * peers * rows * LANES, pairs),
        name="score",
    )(begins, ends, logs, positive, *blocks)


def back_top_kernel(
    where_ref,
    d_ref,
    proj_ref,
    unit_ref,
    scale_ref,
    low_ref,
    embed_ref,
    vec_ref,
    mid_ref,
    down_ref,
    own_ref,
    other_ref,
    sum_ref,
    acc,
):
    step = pl.program_id(0)

    @pl.when(step == 0)
    def _():
        acc[...] = jnp.zeros_like(acc)
        sum_ref[...] = jnp.zeros_like(sum_ref)

    projected = proj_ref[...]
    given = d_ref[...]
    size = lax.rsqrt(jnp.sum(projected * projected, -1, keepdims=True) + UNIT_EPS)
    along = jnp.sum(given * projected, -1, keepdims=True)
    d_proj = (size * given - projected * (size * size * size * along)).astype(BF)
    acc[...] += mm_tn(low_ref[...], d_proj)
    d_out = mm_nt(d_proj, embed_ref[...])
    unit = unit_ref[...]
    d_mid = normalize_back(d_out, vec_ref[2:3, :], unit, scale_ref[...])
    mid_ref[...] = d_mid
    low = d_mid.astype(BF)
    down_ref[...] = low
    sum_ref[0:1, :] += jnp.sum(d_out * unit, 0, keepdims=True)
    sum_ref[1:2, :] += jnp.sum(d_out, 0, keepdims=True)
    sum_ref[2:3, :] += jnp.sum(low.astype(F32), 0, keepdims=True)

    @pl.when(step == pl.num_programs(0) - 1)
    def _():
        put_rows(where_ref, own_ref, other_ref, acc[...])


def back_top(where, d_unit, projected, unit_two, scale_two, low_two, w_embed, vectors):
    rows, width = unit_two.shape
    owned = width // PIECES // 2

    def tile(columns):
        return pl.BlockSpec((TILE, columns), lambda i, w: (i, 0))

    return pl.pallas_call(
        back_top_kernel,
        grid_spec=pltpu.PrefetchScalarGridSpec(
            num_scalar_prefetch=1,
            grid=(rows // TILE,),
            in_specs=[
                tile(LANES),
                tile(LANES),
                tile(width),
                tile(1),
                tile(width),
                full((width, LANES)),
                full((16, width)),
            ],
            out_specs=[
                tile(width),
                tile(width),
                full((PIECES, owned, LANES)),
                full((PIECES, owned, LANES)),
                full((8, width)),
            ],
            scratch_shapes=[pltpu.VMEM((width, LANES), F32)],
        ),
        out_shape=[
            shape_of((rows, width), F32),
            shape_of((rows, width), BF),
            shape_of((PIECES, owned, LANES), BF),
            shape_of((PIECES, owned, LANES), BF),
            shape_of((8, width), F32),
        ],
        compiler_params=params(16),
        cost_estimate=cost(4 * rows * width * LANES, rows * width * 12),
        name="back_top",
    )(where, d_unit, projected, unit_two, scale_two, low_two, w_embed, vectors)


def back_down_kernel(
    where_ref, d_ref, down_ref, slope_ref, active_ref, up_ref, own_ref, other_ref, sum_ref
):
    given = d_ref[...]
    low = (mm_nt(given, down_ref[...]) * slope_ref[...].astype(F32)).astype(BF)
    up_ref[...] = low
    sum_ref[0:1, :] = jnp.sum(low.astype(F32), 0, keepdims=True)
    put_rows(where_ref, own_ref, other_ref, mm_tn(active_ref[...], given))


def back_down(where, d_down, w_down, slope, active):
    rows, width = d_down.shape
    wide = w_down.shape[0]
    steps = wide // width
    parts = PIECES // steps
    owned = wide // PIECES // 2
    column = pl.BlockSpec((rows, width), lambda t, w: (0, t))
    grad_block = pl.BlockSpec(
        (parts, owned, width), lambda t, w: (lax.bitwise_xor(t, w[0] // parts), 0, 0)
    )
    return pl.pallas_call(
        back_down_kernel,
        grid_spec=pltpu.PrefetchScalarGridSpec(
            num_scalar_prefetch=1,
            grid=(steps,),
            in_specs=[
                full((rows, width)),
                pl.BlockSpec((width, width), lambda t, w: (t, 0)),
                column,
                column,
            ],
            out_specs=[
                column,
                grad_block,
                grad_block,
                pl.BlockSpec((8, width), lambda t, w: (0, t)),
            ],
        ),
        out_shape=[
            near_shape((rows, wide), BF),
            shape_of((PIECES, owned, width), BF),
            shape_of((PIECES, owned, width), BF),
            shape_of((8, wide), F32),
        ],
        compiler_params=params(24),
        cost_estimate=cost(4 * rows * width * wide, 6 * rows * wide + 4 * wide * width),
        name="back_down",
    )(where, d_down, far(w_down), far(slope), far(active))


def back_up_kernel(where_ref, mid_ref, low_ref, d_ref, up_ref, out_ref, own_ref, other_ref, turned):
    @pl.when(pl.program_id(0) == 0)
    def _():
        out_ref[...] = mid_ref[...]
        turned[...] = low_ref[...].T

    given = d_ref[...]
    out_ref[...] += mm_nt(given, up_ref[...])
    put_rows(where_ref, own_ref, other_ref, mm(turned[...], given))


def back_up(where, d_mid, low_one, d_up, w_up):
    rows, width = d_mid.shape
    wide = w_up.shape[1]
    owned = width // PIECES // 2
    return pl.pallas_call(
        back_up_kernel,
        grid_spec=pltpu.PrefetchScalarGridSpec(
            num_scalar_prefetch=1,
            grid=(wide // width,),
            in_specs=[
                full((rows, width)),
                full((rows, width)),
                pl.BlockSpec((rows, width), lambda t, w: (0, t)),
                pl.BlockSpec((width, width), lambda t, w: (0, t)),
            ],
            out_specs=[
                full((rows, width)),
                pl.BlockSpec((PIECES, owned, width), lambda t, w: (0, 0, t)),
                pl.BlockSpec((PIECES, owned, width), lambda t, w: (0, 0, t)),
            ],
            scratch_shapes=[pltpu.VMEM((width, rows), BF)],
        ),
        out_shape=[
            shape_of((rows, width), F32),
            shape_of((PIECES, owned, wide), BF),
            shape_of((PIECES, owned, wide), BF),
        ],
        compiler_params=params(28),
        cost_estimate=cost(4 * rows * width * wide, 2 * rows * wide + 4 * wide * width),
        name="back_up",
    )(where, d_mid, far(low_one), near(d_up), far(w_up))


def back_out_kernel(
    where_ref,
    d_ref,
    unit_ref,
    scale_ref,
    first_ref,
    second_ref,
    out_ref,
    vec_ref,
    resid_ref,
    d_context_ref,
    own_ref,
    other_ref,
    sum_ref,
    acc,
):
    step = pl.program_id(0)

    @pl.when(step == 0)
    def _():
        acc[...] = jnp.zeros_like(acc)
        sum_ref[...] = jnp.zeros_like(sum_ref)

    d_out = d_ref[...]
    unit = unit_ref[...]
    d_resid = normalize_back(d_out, vec_ref[0:1, :], unit, scale_ref[...])
    resid_ref[...] = d_resid
    low = d_resid.astype(BF)
    d_context_ref[...] = mm_nt(low, out_ref[...]).astype(BF)
    cut = first_ref.shape[1]
    acc[:cut, :] += mm_tn(first_ref[...], low)
    acc[cut:, :] += mm_tn(second_ref[...], low)
    sum_ref[0:1, :] += jnp.sum(d_out * unit, 0, keepdims=True)
    sum_ref[1:2, :] += jnp.sum(d_out, 0, keepdims=True)
    sum_ref[2:3, :] += jnp.sum(low.astype(F32), 0, keepdims=True)

    @pl.when(step == pl.num_programs(0) - 1)
    def _():
        put_rows(where_ref, own_ref, other_ref, acc[...])


def back_out(where, d_one, unit_one, scale_one, contexts, w_out, vectors):
    rows, width = d_one.shape
    owned = width // PIECES // 2

    def tile(columns):
        return pl.BlockSpec((TILE, columns), lambda i, w: (i, 0))

    return pl.pallas_call(
        back_out_kernel,
        grid_spec=pltpu.PrefetchScalarGridSpec(
            num_scalar_prefetch=1,
            grid=(rows // TILE,),
            in_specs=[
                tile(width),
                tile(width),
                tile(1),
                *[tile(part.shape[1]) for part in contexts],
                full((width, width)),
                full((16, width)),
            ],
            out_specs=[
                tile(width),
                tile(width),
                full((PIECES, owned, width)),
                full((PIECES, owned, width)),
                full((8, width)),
            ],
            scratch_shapes=[pltpu.VMEM((width, width), F32)],
        ),
        out_shape=[
            shape_of((rows, width), F32),
            shape_of((rows, width), BF),
            shape_of((PIECES, owned, width), BF),
            shape_of((PIECES, owned, width), BF),
            shape_of((8, width), F32),
        ],
        compiler_params=params(20),
        cost_estimate=cost(4 * rows * width * width, rows * width * 16),
        name="back_out",
    )(where, d_one, unit_one, scale_one, *contexts, far(w_out), vectors)


def back_in_kernel(resid_ref, *refs):
    *parts, in_ref, out_ref = refs
    total = resid_ref[...]
    column = 0
    for part in parts:
        count = part.shape[1]
        total = total + mm_nt(part[...], in_ref[:, column : column + count])
        column += count
    out_ref[...] = total


def back_in(d_resid, parts, w_in):
    rows, width = d_resid.shape

    def tile(columns):
        return pl.BlockSpec((TILE, columns), lambda i: (i, 0))

    return pl.pallas_call(
        back_in_kernel,
        grid=(rows // TILE,),
        in_specs=[tile(width)] + [tile(p.shape[1]) for p in parts] + [full(w_in.shape)],
        out_specs=tile(width),
        out_shape=shape_of((rows, width), F32),
        compiler_params=params(24),
        cost_estimate=cost(6 * rows * width * width, rows * width * 14),
        name="back_in",
    )(d_resid, *parts, far(w_in))


def finish_kernel(steps, *refs):
    places = len(steps)
    pair_ref, *refs = refs
    totals, refs = refs[: len(refs) - 6 * places], refs[len(refs) - 6 * places :]
    weights, firsts, seconds = refs[:places], refs[places : 2 * places], refs[2 * places : 3 * places]
    outs = refs[3 * places :]
    norm = jnp.sqrt(pair_ref[1:2, 0:1])
    factor = CLIP_NORM / jnp.maximum(norm, CLIP_NORM)
    fix_one = 1.0 / (1.0 - BETA_ONE**STEP)
    fix_two = 1.0 / (1.0 - BETA_TWO**STEP)
    for item, (rate, decay, pieces) in enumerate(steps):
        for source, begin, width, target in pieces:
            if target is None:
                rows, columns = weights[item].shape
                grad = totals[source][:, begin : begin + width].T[:rows] * factor
                target, width = 0, columns
            else:
                grad = totals[source][:, begin : begin + width] * factor
            columns = slice(target, target + width)
            weight = weights[item][:, columns]
            first = BETA_ONE * firsts[item][:, columns] + (1.0 - BETA_ONE) * grad
            second = BETA_TWO * seconds[item][:, columns] + (1.0 - BETA_TWO) * grad * grad
            update = first * fix_one / (jnp.sqrt(second * fix_two) + ADAM_EPS)
            outs[item][:, columns] = first
            outs[places + item][:, columns] = second
            outs[2 * places + item][:, columns] = weight - rate * (update + decay * weight)


def finish(steps, pair, totals, masters, firsts, seconds):
    vmem = pl.BlockSpec(memory_space=pltpu.VMEM)
    held = [*masters, *firsts, *seconds]
    return pl.pallas_call(
        functools.partial(finish_kernel, steps),
        in_specs=[vmem] * (1 + len(totals) + len(held)),
        out_specs=[vmem] * len(held),
        out_shape=[shape_of(block.shape, F32) for block in held],
        compiler_params=pltpu.CompilerParams(vmem_limit_bytes=32 * MIB),
        name="finish",
    )(pair, *totals, *far(*held))


def swap(block, bits):
    count = lax.axis_size(AXES)
    return lax.ppermute(block, AXES, [(d, d ^ bits) for d in range(count)])


def phase(*blocks):
    return lax.optimization_barrier(blocks)


def cut_of(width):
    return (width // LANES + 1) // 2 * LANES


def gather_near(keep, give, core):
    theirs = swap(give, 1)
    ours = [jnp.where(core == 0, keep, theirs), jnp.where(core == 0, theirs, keep)]
    return jnp.concatenate(ours, 0)


def gather_far(mine):
    return jnp.stack([mine] + [swap(mine, 8 * step) for step in (1, 2, 3)])


def gather_cross(far):
    cut = cut_of(far.shape[-1])
    left, right = far[:, :, :cut], far[:, :, cut:]
    return jnp.stack([left, swap(left, 2)], 1), jnp.stack([right, swap(right, 4)], 1)


def gather_last(pair):
    left, right = pair
    left = jnp.stack([left, swap(left, 4)], 1)
    right = jnp.stack([right, swap(right, 2)], 2)
    own = jnp.concatenate([left, right], -1)
    return own.reshape(PIECES, *own.shape[3:])


def gather_plain(keep, give):
    whole = [lax.all_gather(half, AXES, axis=0, tiled=True) for half in (keep, give)]
    return [half.reshape(PIECES, -1, half.shape[1]) for half in whole]


def added(mine, theirs):
    return (mine.astype(F32) + theirs.astype(F32)).astype(BF)


def scatter_near(own, other):
    _, rows, width = own.shape
    return added(own, swap(other, 1)).reshape(4, 2, 2, rows, width)


def scatter_cross(near):
    cut = cut_of(near.shape[-1])
    left, right = near[..., :cut], near[..., cut:]
    return added(left[:, :, 0], swap(left[:, :, 1], 2)), added(right[:, 0], swap(right[:, 1], 4))


def scatter_last(pair):
    left, right = pair
    left = added(left[:, 0], swap(left[:, 1], 4))
    right = added(right[:, 0], swap(right[:, 1], 2))
    return jnp.concatenate([left, right], -1)


def scatter_far(far):
    total = far[0].astype(F32)
    for step in (1, 2, 3):
        total = total + swap(far[step], 8 * step).astype(F32)
    return total


def scatter_half(far):
    return added(far[:2], swap(far[2:], 16))


def scatter_end(half):
    return half[0].astype(F32) + swap(half[1], 8).astype(F32)


def scatter_plain(pair):
    pieces, rows, width = pair[0].shape
    whole = jnp.stack(pair, 1).reshape(2 * pieces * rows, width)
    return lax.psum_scatter(whole, AXES, scatter_dimension=0, tiled=True).astype(F32)


def keep_pair(own, other):
    return own, other


def same(blocks):
    return blocks


def sum_everywhere(values):
    count = lax.axis_size(AXES)
    values = values + swap(values, 1)
    bit = 2
    while bit < count:
        if 2 * bit < count:
            near, far_one, far_two = [swap(values, bit * step) for step in (1, 2, 3)]
            values = (values + near) + (far_one + far_two)
        else:
            values = values + swap(values, bit)
        bit *= 4
    return values


def gather_peers(block):
    held = [block[None]]
    bit = 1
    sizes = []
    while bit < lax.axis_size("psg"):
        sizes.append(bit)
        bit *= 2
    for bit in reversed(sizes):
        now = jnp.concatenate(held, 0) if len(held) > 1 else held[0]
        held = [now, swap(now, bit)]
        if bit > 1:
            held = [jnp.concatenate(held, 0)]
    return held


def peer_order(count):
    order, bit = [0], count // 2
    while bit > 0:
        order = order + [peer ^ bit for peer in order]
        bit //= 2
    return order


def local(hidden, lengths_in, positive, *shards):
    masters, firsts, seconds = shards[:6], shards[6:12], shards[12:]
    psg_count = lax.axis_size("psg")
    count = lax.axis_size(AXES)
    split = count == 2 * PIECES
    mine = lax.axis_index("psg")
    rows, width = hidden.shape
    wide = masters[2].shape[1]
    pairs = width // LANES
    queries = positive.shape[0]
    query_rows = queries * QLEN
    query_total = queries * count
    slots = lengths_in.shape[1]
    pack_rows = rows - query_rows
    index = lax.axis_index(AXES)
    if split:
        where = jnp.stack([index // 2, index % 2]).astype(jnp.int32)
    else:
        where = jnp.zeros((2,), jnp.int32)
    core = where[1]

    front_keep, front_give, rest_keep, rest_give, down_low = pack(
        where, masters[0], masters[1], masters[2], masters[4], masters[5].T, masters[3]
    )
    w_down = lax.all_gather(down_low, AXES, axis=0, tiled=True)
    facts = jnp.concatenate([lengths_in[0], positive])[None]
    if split:
        beside = gather_near(front_keep, front_give, core)
        column = gather_far(beside)
        beside_rest = gather_near(rest_keep, rest_give, core)
        facts = gather_peers(facts)
        column, beside_rest, facts = phase(column, beside_rest, facts)
    else:
        facts = gather_peers(facts)
        front = gather_plain(front_keep, front_give)
        rest = gather_plain(rest_keep, rest_give)
    facts = jnp.concatenate(facts, 0).reshape(psg_count, -1)
    lengths, chosen = facts[:, :slots], facts[:, slots:]
    ends = jnp.cumsum(lengths, 1)
    lane_slot = jnp.eye(psg_count, dtype=jnp.int32)[:, :, None]
    unused = LANES // 2 - psg_count * slots

    def twice(values):
        return jnp.tile(jnp.pad(values, ((0, 0), (0, unused))), (1, 2))

    def by_lane(values):
        return twice((lane_slot * values[:, None, :]).reshape(psg_count, psg_count * slots))

    end_lanes = by_lane(ends)
    begin_lanes = by_lane(ends - lengths)
    log_lanes = twice(jnp.log(lengths.astype(F32)).reshape(1, -1))
    place_of = [peer_order(psg_count).index(peer) for peer in range(psg_count)]
    theirs = jnp.bitwise_xor(chosen // slots, mine)
    places = sum(jnp.where(theirs == peer, place, 0) for peer, place in enumerate(place_of))
    chosen = (places * slots + chosen % slots)[:, :, None]
    places = jnp.arange(pack_rows, dtype=jnp.int32)
    segment = jnp.sum((places[:, None] >= ends[0][None, :]).astype(jnp.int32), -1)
    seg_col, seg_row = segment[:, None], segment[None, :]

    notes = (begin_lanes, end_lanes, log_lanes, chosen, seg_col, seg_row)
    if split:
        crossed = gather_cross(column)
        moved = [beside_rest] + [swap(beside_rest, 8 * step) for step in (1, 2)]
        crossed, moved = phase(crossed, moved)
        own = gather_last(crossed)
        moved = moved + [swap(moved[0], 24)]
        own, moved, notes = phase(own, moved, notes)
        front, moved = phase((own, swap(own, 1)), moved)
        crossed_rest = gather_cross(jnp.stack(moved))
    begin_lanes, end_lanes, log_lanes, chosen, seg_col, seg_row = notes
    merged, turned, w_in, w_embed, vectors = project(where, hidden, *front)
    if split:
        merged, turned, crossed_rest = phase(merged, turned, crossed_rest)
    cut = 2 * pairs // 3
    contexts = [attend(merged, seg_col, seg_row, query_rows, 0, cut)]
    if split:
        own = gather_last(crossed_rest)
        merged, own, contexts = phase(merged, own, contexts)
    contexts.append(attend(merged, seg_col, seg_row, query_rows, cut, pairs - cut))
    if split:
        rest = (own, swap(own, 1))
    unit_one, scale_one, low_one, active, slope, unit_two, scale_two, low_two, *held = encode(
        where, contexts, hidden, vectors, w_embed, w_down, *rest
    )
    projected, embedded, w_up, w_out = held
    loss_block, d_unit = score(
        gather_peers(embedded), begin_lanes, end_lanes, log_lanes, chosen, query_rows, query_total, slots
    )
    d_mid, d_down, *grad_embed, sums_top = back_top(
        where, d_unit, projected, unit_two, scale_two, low_two, w_embed, vectors
    )
    d_up, *grad_down, sums_up = back_down(where, d_down, w_down, slope, active)
    steps = (scatter_near, scatter_cross, scatter_last, scatter_half, scatter_end, scatter_far)
    plain = (keep_pair, same, same, same, scatter_plain, scatter_plain)
    closest, cross, last, middle, end, final = steps if split else plain

    d_one, *grad_up = back_up(where, d_mid, low_one, d_up, w_up)
    downs = closest(*grad_down)
    here, d_one, grad_up, downs = phase(where, d_one, grad_up, downs)
    d_resid, d_context, *grad_out, sums_out = back_out(
        here, d_one, unit_one, scale_one, contexts, w_out, vectors
    )

    def back(held, *rest):
        *d_part, own, other, sums = attend_back(
            held, merged, d_context, turned, seg_col, seg_row, query_rows, *rest
        )
        return d_part, (own, other), sums

    third = pairs // 3
    downs, ups = cross(downs), closest(*grad_up)
    here, d_context, grad_out, downs, ups = phase(where, d_context, grad_out, downs, ups)
    part_one, ones, sums_one = back(here, 0, third, "copied", grad_out)
    downs, ups = last(downs), cross(ups)
    here, part_one, ones, downs, ups = phase(where, part_one, ones, downs, ups)
    part_two, twos, sums_two = back(here, third, third)
    downs, ups, ones = middle(downs), last(ups), closest(*ones)
    here, part_two, twos, downs, ups, ones = phase(where, part_two, twos, downs, ups, ones)
    part_three, threes, sums_three = back(
        here,
        2 * third,
        pairs - 2 * third,
        "vectors",
        (*grad_embed, sums_out, sums_top, sums_up, sums_one, sums_two),
    )
    total_down, ups, ones, twos = end(downs), middle(ups), cross(ones), closest(*twos)
    part_three, threes, total_down, ups, ones, twos = phase(
        part_three, threes, total_down, ups, ones, twos
    )
    total_up, ones, threes = end(ups), last(ones), closest(*threes)
    total_up, ones, threes, d_resid = phase(total_up, ones, threes, d_resid)
    parts = (part_one, part_two, part_three)
    ordered = [part[which] for which in (0, 1, 2) for part in parts]
    if split:
        ones, twos = middle(ones), cross(jnp.concatenate([twos, threes], -1))
        input_grad = back_in(d_resid, ordered, w_in)
        input_grad, ones, twos = phase(input_grad, ones, twos)
        total_one, twos = phase(end(ones), last(twos))
        total_two = final(twos)
    else:
        input_grad = back_in(d_resid, ordered, w_in)
        total_one = final(ones)
        total_two = final([jnp.concatenate([two, three], -1) for two, three in zip(twos, threes)])

    totals = [total_down, total_up, total_one, total_two]
    squares = sum(jnp.sum(total * total) for total in totals)
    pair = jnp.stack([loss_block[0, 0], squares])
    pair = sum_everywhere(jnp.broadcast_to(pair[:, None], (2, LANES)))
    loss = pair[0, 0] / query_total
    grad_norm = jnp.sqrt(pair[1, 0])

    block = 3 * LANES
    inward_pieces = []
    for head_pair in range(pairs):
        source = 2 if head_pair < third else 3
        begin = (head_pair if head_pair < third else head_pair - third) * block
        for part in (0, 1, 2):
            target = part * width + head_pair * LANES
            inward_pieces.append((source, begin + part * LANES, LANES, target))
    first_end = third * block
    last_end = (pairs - third) * block
    plans = (
        (RATE_MATRIX, DECAY, tuple(inward_pieces)),
        (RATE_MATRIX, DECAY, ((2, first_end, width, 0),)),
        (RATE_MATRIX, DECAY, ((1, 0, wide, 0),)),
        (RATE_MATRIX, DECAY, ((0, 0, width, 0),)),
        (RATE_MATRIX, DECAY, ((3, last_end + LANES, LANES, 0),)),
        (RATE_VECTOR, 0.0, ((3, last_end, LANES, None),)),
    )
    held = [list(group[:5]) + [group[5].T] for group in (masters, firsts, seconds)]
    stepped = finish(plans, pair, totals, *held)
    stepped = [block.T if place % 6 == 5 else block for place, block in enumerate(stepped)]
    return (loss, input_grad, grad_norm) + tuple(stepped)


def solution(mesh):
    by_rows = P(AXES, None)
    placed = (by_rows, by_rows, P(AXES)) + (by_rows,) * 18
    return jax.shard_map(
        local,
        mesh=mesh,
        in_specs=placed,
        out_specs=(P(), by_rows, P()) + (by_rows,) * 18,
        check_vma=False,
    )
```
